512 devices in a mesh: lon: 32 (over y, x), lat: 16 (over z, core).
Axes of the slice: x: 4, y: 8, z: 8, core: 2. Of those that a mesh axis runs over, the one named last changes fastest.
Arguments:
- tendency: float32 [3, 16, 16, 32, 2304], P(None, None, 'lat', 'lon'), may hold values from -8 to 8
- state: float32 [16, 3, 2, 512, 512], P('lat', None, None, 'lon'), may hold values from -6 to 6
- stiffness: float32 [16], replicated, may hold values from 0.2 to 20
- damping: float32 [16], replicated, may hold values from 0.05 to 2
Outputs:
- new_state: float32 [16, 3, 2, 512, 512], P('lat', None, None, 'lon')
- new_fields: float32 [3, 16, 16, 32, 2304], P(None, None, 'lat', 'lon')
The draws below stay inside these ranges and needn't reach their ends.
All inputs are finite; a program needn't handle non-finite values.
Results may differ from the reference program's by a relative error of at most 0.0044.
Values sent between devices are 32-bit elements; how exact they have to be, the bound alone decides.
A program may use at most 128 MiB of HBM per device.

```python
import math
import jax
import jax.numpy as jnp
from jax import lax

NLAT = 768
NLON = 1536
M = 512
MODES = 16
LAT_DEV = 48
LON_DEV = 48


def levels(key, shape, split, smallest, top_value):
    gain, own = 1.0, jax.random.fold_in(key, 6)
    for position, blocks in split:
        steps = jnp.exp(jax.random.uniform(jax.random.fold_in(own, position), (blocks,), jnp.float32, smallest / len(split), top_value / len(split)))
        gain = gain * jnp.repeat(steps, shape[position] // blocks).reshape([-1 if axis == position else 1 for axis in range(len(shape))])
    return gain


def centred(stream_key, extent, scale, reach, cuts=(), kind=jnp.bfloat16):
    result = scale * jax.random.normal(stream_key, extent, jnp.float32)
    if cuts:
        result = result * levels(stream_key, extent, cuts, -0.22, 0.18)
    return jnp.clip(result, -reach, reach).astype(kind)


def setup_inputs(seed: int = 0) -> dict:
    keys = jax.random.split(jax.random.key(seed), 5)
    return {
        "tendency": centred(keys[0], (3, MODES, NLAT // LAT_DEV, NLON // LON_DEV, LAT_DEV * LON_DEV), 2.0, 8.0, ((2, 16), (3, 32)), jnp.float32),
        "state": centred(keys[1], (MODES, 3, 2, M, M), 1.0, 6.0, ((0, 16), (3, 32)), jnp.float32),
        "stiffness": jnp.clip(jnp.exp(jax.random.uniform(keys[2], (MODES,), jnp.float32, math.log(0.2), math.log(20.0))), 0.2, 20.0),
        "damping": jnp.clip(jnp.exp(jax.random.uniform(keys[3], (MODES,), jnp.float32, math.log(0.05), math.log(2.0))), 0.05, 2.0),
    }


def colatitude(colat_index, nlat):
    return math.pi * (colat_index.astype(jnp.float32) + 0.5) / nlat

def combine_blocks(early, later):
    e00, e01, e10, e11, e_log = early
    l00, l01, l10, l11, l_log = later
    p00 = l00 * e00 + l01 * e10
    p01 = l00 * e01 + l01 * e11
    p10 = l10 * e00 + l11 * e10
    p11 = l10 * e01 + l11 * e11
    largest = jnp.maximum(jnp.maximum(jnp.abs(p00), jnp.abs(p01)), jnp.maximum(jnp.abs(p10), jnp.abs(p11)))
    return (p00 / largest, p01 / largest, p10 / largest, p11 / largest, e_log + l_log + jnp.log(largest))

def legendre_values(wave_index, colat_index, nlat, kmax):
    theta = colatitude(colat_index, nlat)
    cosine = jnp.cos(theta)[None, None, :]
    log_sine = jnp.log(jnp.sin(theta))[None, :]
    orders = wave_index.astype(jnp.float32)[:, None]
    offsets = jnp.arange(kmax, dtype=jnp.float32)[None, :]
    degree = orders + offsets
    spacing = jnp.maximum(offsets * (2.0 * orders + offsets), 1.0)
    slope_term = jnp.sqrt(jnp.maximum(4.0 * degree * degree - 1.0, 0.0) / spacing)
    lag_num = (2.0 * degree + 1.0) * (offsets - 1.0) * (degree - 1.0 + orders)
    lag_term = jnp.sqrt(jnp.maximum(lag_num, 0.0) / (jnp.maximum(2.0 * degree - 3.0, 1.0) * spacing))
    nblocks = kmax // 8
    width = wave_index.shape[0]
    lat_count = colat_index.shape[0]
    slope_term = slope_term.reshape(width, nblocks, 8)
    lag_term = lag_term.reshape(width, nblocks, 8)
    initial = (jnp.arange(kmax) == 0).reshape(nblocks, 8)

    def advance(state_pair, offset):
        upper, lower = state_pair
        moved = slope_term[:, :, offset, None] * cosine * upper - lag_term[:, :, offset, None] * lower
        hold = initial[None, :, offset, None]
        return (jnp.where(hold, upper, moved), jnp.where(hold, lower, upper))
    ones = jnp.ones((width, nblocks, lat_count), jnp.float32)
    zeros = jnp.zeros((width, nblocks, lat_count), jnp.float32)
    left = (ones, zeros)
    right = (zeros, ones)
    for offset in range(8):
        left = advance(left, offset)
        right = advance(right, offset)
    largest = jnp.maximum(jnp.maximum(jnp.abs(left[0]), jnp.abs(right[0])), jnp.maximum(jnp.abs(left[1]), jnp.abs(right[1])))
    elements = (left[0] / largest, right[0] / largest, left[1] / largest, right[1] / largest, jnp.log(largest))
    prefix = lax.associative_scan(combine_blocks, elements, axis=1)
    upper = jnp.concatenate([ones[:, :1], prefix[0][:, :-1]], axis=1)
    lower = jnp.concatenate([zeros[:, :1], prefix[2][:, :-1]], axis=1)
    shifted = jnp.concatenate([zeros[:, :1], prefix[4][:, :-1]], axis=1)
    largest = jnp.maximum(jnp.abs(upper), jnp.abs(lower))
    upper = upper / largest
    lower = lower / largest
    half_orders = orders + 0.5
    log_start = 0.5 * jnp.log(half_orders) + 0.5 * lax.lgamma(half_orders) - 0.5 * lax.lgamma(orders + 1.0) - 0.25 * math.log(math.pi) + orders * log_sine
    growth = jnp.exp(shifted + jnp.log(largest) + log_start[:, None, :])
    state_pair = (upper, lower)
    columns = []
    for offset in range(8):
        state_pair = advance(state_pair, offset)
        columns.append(state_pair[0] * growth)
    values = jnp.stack(columns, axis=2).reshape(width, kmax, lat_count)
    inside = (degree <= kmax - 1.0)[:, :, None]
    return jnp.where(inside, values, 0.0)

def semi_implicit(vorticity, divergence, height, stiff_modes, damp_modes, eigen_ratio, inside):
    denominator = 1.0 + stiff_modes * eigen_ratio
    damped = jnp.where(inside, 1.0 / (1.0 + damp_modes * eigen_ratio * eigen_ratio), 0.0)
    new_divergence = (divergence + eigen_ratio * height) / denominator
    new_height = (height - stiff_modes * divergence) / denominator
    return (vorticity * damped, new_divergence * damped, new_height * damped)

def reference(tendency, state, stiffness, damping):
    lat_blocks = NLAT // LAT_DEV
    lon_blocks = NLON // LON_DEV
    grid = tendency.reshape(3, MODES, lat_blocks, lon_blocks, LAT_DEV, LON_DEV)
    grid = jnp.transpose(grid, (0, 1, 2, 4, 3, 5)).reshape(3, MODES, NLAT, NLON)
    spectra = jnp.fft.rfft(grid, axis=-1)[..., :M] / NLON
    fourier = jnp.stack([jnp.real(spectra), jnp.imag(spectra)], axis=-1).astype(jnp.float32)
    fourier = jnp.moveaxis(fourier, 3, 0).reshape(M // 8, 8, 3, MODES, NLAT, 2)
    moved_state = jnp.moveaxis(state, 3, 0).reshape(M // 8, 8, MODES, 3, 2, M)
    colat_index = jnp.arange(NLAT, dtype=jnp.int32)
    weights = math.pi / NLAT * jnp.sin(colatitude(colat_index, NLAT))
    stiff_modes = stiffness[None, :, None, None]
    damp_modes = damping[None, :, None, None]

    def one_block(inputs):
        block_index, fourier_block, state_block = inputs
        wave_index = block_index * 8 + jnp.arange(8, dtype=jnp.int32)
        legendre = legendre_values(wave_index, colat_index, NLAT, M)
        weighted = legendre * (M * weights)[None, None, :]
        sums = state_block + jnp.einsum('mkj,mfcjr->mcfrk', weighted, fourier_block, precision=lax.Precision.HIGHEST)
        degree = wave_index.astype(jnp.float32)[:, None] + jnp.arange(M, dtype=jnp.float32)[None, :]
        eigen_ratio = (degree * (degree + 1.0) / (M * (M - 1.0)))[:, None, None, :]
        inside = (degree <= M - 1.0)[:, None, None, :]
        fields_new = semi_implicit(sums[:, :, 0], sums[:, :, 1], sums[:, :, 2], stiff_modes, damp_modes, eigen_ratio, inside)
        updated = jnp.stack(fields_new, axis=2)
        synthesis = jnp.einsum('mkj,mcfrk->mfcjr', legendre, updated, precision=lax.Precision.HIGHEST)
        return (updated, synthesis)
    updated, synthesis = lax.map(one_block, (jnp.arange(M // 8, dtype=jnp.int32), fourier, moved_state))
    new_state = jnp.moveaxis(updated.reshape(M, MODES, 3, 2, M), 0, 3)
    synthesis = synthesis.reshape(M, 3, MODES, NLAT, 2)
    real_part = jnp.moveaxis(synthesis[..., 0], 0, -1)
    imag_part = jnp.moveaxis(synthesis[..., 1], 0, -1)
    padding = ((0, 0), (0, 0), (0, 0), (0, NLON // 2 + 1 - M))
    spectrum = lax.complex(jnp.pad(real_part, padding), jnp.pad(imag_part, padding))
    plain = (jnp.fft.irfft(spectrum, n=NLON, axis=-1) * (NLON / M)).astype(jnp.float32)
    blocked = plain.reshape(3, MODES, lat_blocks, LAT_DEV, lon_blocks, LON_DEV)
    new_fields = jnp.transpose(blocked, (0, 1, 2, 4, 3, 5)).reshape(3, MODES, lat_blocks, lon_blocks, LAT_DEV * LON_DEV)
    return (new_state, new_fields)
```

```python
import functools
import math

import jax
import jax.numpy as jnp
import ml_dtypes
import numpy as np
from jax import lax
from jax.experimental import pallas as pl
from jax.experimental.pallas import tpu as pltpu
from jax.sharding import PartitionSpec as P

NLAT = 768
NLON = 1536
WAVES = 512
MODES = 16
LON = 32
LAT = 16
BLK = 48
MDEV = 16
GROUPS = 8
MSG_G = 27
MSG_C = 18
FR = 6
ROWS = 48
MESH = pl.DeviceIdType.MESH
F32 = jnp.float32
BF16 = jnp.bfloat16


def split_constant(table):
    high = table.astype(np.float32).astype(ml_dtypes.bfloat16)
    low = (table - high.astype(np.float64)).astype(np.float32).astype(ml_dtypes.bfloat16)
    return high, low


@functools.lru_cache(maxsize=None)
def fourier_constants():
    slot = np.arange(LON * 64)
    block, inner = slot // 64, slot % 64
    lon = block * BLK + inner
    valid = (inner < BLK)[:, None]
    wave = np.arange(WAVES)
    angle = 2.0 * np.pi / NLON * ((lon[:, None] * wave[None, :]) % NLON)
    cosine = np.where(valid, np.cos(angle), 0.0).reshape(-1, LON, MDEV)
    sine = np.where(valid, np.sin(angle), 0.0).reshape(-1, LON, MDEV)
    basis = np.stack([cosine, -sine], axis=2).reshape(LON * 64, 2 * WAVES)
    factor = np.where(wave == 0, 1.0, 2.0).reshape(LON, 1, MDEV) / WAVES
    factor = np.broadcast_to(factor, (LON, 2, MDEV)).reshape(2 * WAVES, 1)
    return split_constant(basis / NLON) + split_constant(factor * basis.T)


@functools.lru_cache(maxsize=None)
def start_constants():
    start = [
        (0.5 * math.log(m + 0.5) + 0.5 * math.lgamma(m + 0.5) - 0.5 * math.lgamma(m + 1.0) - 0.25 * math.log(math.pi))
        / math.log(2.0)
        for m in range(WAVES)
    ]
    return np.tile(np.array(start, np.float32).reshape(LON, MDEV), (1, GROUPS))


def lanes(shape):
    return lax.broadcasted_iota(jnp.int32, shape, len(shape) - 1)


def swap_groups(items):
    group = lanes(items[0].shape) // 16
    items = list(items)
    for step in (4, 2, 1):
        keep = (group & step) == 0
        for low in range(GROUPS):
            if low & step:
                continue
            high = low + step
            x, y = items[low], items[high]
            items[low] = jnp.where(keep, x, pltpu.roll(y, 16 * step, 1))
            items[high] = jnp.where(keep, pltpu.roll(x, 128 - 16 * step, 1), y)
    return items


def fold_rows(parts):
    row = lax.broadcasted_iota(jnp.int32, (8, 128), 0)
    upper = row < 4
    four = []
    for index in range(4):
        x, y = parts[index], parts[index + 4]
        four.append(jnp.where(upper, x, y) + pltpu.roll(jnp.where(upper, y, x), 4, 0))
    for step in (2, 1):
        keep = (row & step) == 0
        four = [
            jnp.where(
                keep,
                four[index] + pltpu.roll(four[index], 8 - step, 0),
                four[index + step] + pltpu.roll(four[index + step], step, 0),
            )
            for index in range(step)
        ]
    return four[0]


def split(x):
    high = x.astype(BF16)
    return high, (x - high.astype(F32)).astype(BF16)


def mirrored(south, a):
    return jnp.where(south, GROUPS - 1 - a, a)


def block_rows(index, size):
    return pl.ds(pl.multiple_of(index * size, size), size)


def gather_rows(t_ref, sb_ref):
    def body(d, _):
        c, h = d // 2, d % 2
        for f in range(3):
            sb_ref[pl.ds(d * MSG_G + f * 9, 9), :] = t_ref[pl.ds((f * MODES + c) * 18 + h * 9, 9), :]
        return 0

    lax.fori_loop(0, LON, body, 0)


def legendre_tables(q, start_ref, slope_ref, lag_ref, trig_ref, p_ref):
    wave = (lanes((1, 128)) % MDEV + q * MDEV).astype(F32)

    def coefficients(block, _):
        offsets = (lax.broadcasted_iota(jnp.int32, (64, 128), 0) + block * 64).astype(F32)
        degree = wave + offsets
        spacing = jnp.maximum(offsets * (2.0 * wave + offsets), 1.0)
        slope = jnp.sqrt(jnp.maximum(4.0 * degree * degree - 1.0, 0.0) / spacing)
        numerator = (2.0 * degree + 1.0) * (offsets - 1.0) * (degree - 1.0 + wave)
        lag = jnp.sqrt(jnp.maximum(numerator, 0.0) / (jnp.maximum(2.0 * degree - 3.0, 1.0) * spacing))
        first = offsets < 0.5
        slope_ref[block_rows(block, 64), :] = jnp.where(first, 0.0, slope)
        lag_ref[block_rows(block, 64), :] = jnp.where(first, 1.0, lag)
        return 0

    lax.fori_loop(0, WAVES // 64, coefficients, 0)
    row = lax.broadcasted_iota(jnp.int32, (ROWS, 128), 0)
    colat = (row % 16) * 24 + (row // 16) * 8 + lanes((ROWS, 128)) // MDEV
    theta = math.pi * (colat.astype(F32) + 0.5) / NLAT
    mu = jnp.cos(theta)
    sine = jnp.sin(theta)
    trig_ref[...] = sine * (WAVES * math.pi / NLAT)
    log_sine = jnp.log(sine) * (1.0 / math.log(2.0))
    coarse = jnp.floor(log_sine * 1024.0) * (1.0 / 1024.0)
    whole = wave * coarse
    exponent = jnp.floor(whole)
    fraction = (whole - exponent) + wave * (log_sine - coarse) + start_ref[pl.ds(q, 1), :]
    lower = -jnp.exp2(fraction)
    upper = jnp.zeros_like(lower)

    def body(block, carry):
        upper, lower, exponent = carry
        growth = jnp.exp2(jnp.maximum(exponent, -140.0))
        for offset in range(8):
            k = block * 8 + offset
            moved = (slope_ref[pl.ds(k, 1), :] * mu) * upper - lag_ref[pl.ds(k, 1), :] * lower
            upper, lower = moved, upper
            inside = wave + k.astype(F32) <= WAVES - 1.0
            p_ref[block_rows(k, ROWS), :] = jnp.where(inside, upper * growth, 0.0)
        big = jnp.maximum(jnp.abs(upper), jnp.abs(lower)) > 2.0**32
        scale = jnp.where(big, 2.0**-32, 1.0)
        return upper * scale, lower * scale, exponent + jnp.where(big, 32.0, 0.0)

    lax.fori_loop(0, WAVES // 8, body, (upper, lower, exponent))


def forward_operand(r_ref, x_ref):
    lane = lanes((16, 128))

    def body(pair, _):
        columns = [
            [r_ref[pl.ds((2 * pair + par) * MSG_G + c, 16, stride=3), :] for c in range(3)] for par in range(2)
        ]
        for a in range(GROUPS):
            first, offset = divmod(BLK * a, 128)
            pieces = []
            for par in range(2):
                source = columns[par][first]
                if offset + BLK > 128:
                    source = jnp.where(lane >= offset, source, columns[par][first + 1])
                shift = (64 * par - offset) % 128
                pieces.append(pltpu.roll(source, shift, 1) if shift else source)
            high, low = split(jnp.where(lane < 64, pieces[0], pieces[1]))
            x_ref[a * 16 : (a + 1) * 16, block_rows(pair, 128)] = high
            x_ref[128 + a * 16 : 128 + (a + 1) * 16, block_rows(pair, 128)] = low
        return 0

    lax.fori_loop(0, LON // 2, body, 0)


def product(x_ref, high_ref, low_ref, block):
    columns = block_rows(block, 256)
    both = jnp.dot(x_ref[...], high_ref[:, columns], preferred_element_type=F32)
    rest = jnp.dot(x_ref[0:128, :], low_ref[:, columns], preferred_element_type=F32)
    return both[0:128] + both[128:256] + rest


def forward_transform(q, south, x_ref, high_ref, low_ref, block_ref, m_ref, send):
    def body(step, _):
        block = (step + q // 8) % 4
        block_ref[...] = product(x_ref, high_ref, low_ref, block)
        for half in range(2):
            items = swap_groups(
                [block_ref[block_rows(mirrored(south, a), 16), half * 128 : (half + 1) * 128] for a in range(GROUPS)]
            )
            for group in range(GROUPS):
                owner = block * 8 + half * 4 + group // 2
                m_ref[pl.ds(owner * MSG_C + (group % 2) * 9, 9), :] = items[group][0:9]
            for index in range(4):
                send(block * 8 + half * 4 + index)
        return 0

    lax.fori_loop(0, 4, body, 0)


def analysis(g_ref, trig_ref, even_ref, odd_ref, p_ref, a_ref):
    for f in range(3):
        for r in range(2):
            for s in range(3):
                north = g_ref[pl.ds(r * 9 + f * 3 + s, 16, stride=MSG_C), :]
                south = g_ref[pl.ds(16 * MSG_C + r * 9 + f * 3 + 2 - s, 16, stride=MSG_C), :]
                weight = trig_ref[s * 16 : (s + 1) * 16, :]
                rows = slice((f * 2 + r) * ROWS + s * 16, (f * 2 + r) * ROWS + (s + 1) * 16)
                even_ref[rows, :] = (north + south) * weight
                odd_ref[rows, :] = (north - south) * weight

    def body(block, _):
        totals = [[None] * 8 for _ in range(FR)]
        for parity, source in ((0, even_ref), (1, odd_ref)):
            planes = [p_ref[block_rows(block * 8 + k, ROWS), :] for k in range(parity, 8, 2)]
            for fr in range(FR):
                field = source[fr * ROWS : (fr + 1) * ROWS, :]
                for index, plane in enumerate(planes):
                    terms = plane * field
                    pieces = [terms[8 * n : 8 * n + 8] for n in range(6)]
                    total = (pieces[0] + pieces[1]) + (pieces[2] + pieces[3]) + (pieces[4] + pieces[5])
                    totals[fr][parity + 2 * index] = total
        for fr in range(FR):
            a_ref[pl.ds(pl.multiple_of(fr * WAVES + block * 8, 8), 8), :] = fold_rows(totals[fr])
        return 0

    lax.fori_loop(0, WAVES // 8, body, 0)


def update(q, stiff, damp, state_ref, a_ref, ns_ref, st_ref):
    wave = (lax.broadcasted_iota(jnp.int32, (MDEV, WAVES), 0) + q * MDEV).astype(F32)
    degree = wave + lanes((MDEV, WAVES)).astype(F32)
    ratio = degree * (degree + 1.0) / (WAVES * (WAVES - 1.0))
    inside = degree <= WAVES - 1.0
    denominator = 1.0 + stiff * ratio
    damped = jnp.where(inside, 1.0 / (1.0 + damp * ratio * ratio), 0.0)

    def total(fr):
        turned = jnp.transpose(a_ref[fr * WAVES : (fr + 1) * WAVES, :])
        pieces = [turned[16 * n : 16 * n + 16] for n in range(GROUPS)]
        summed = ((pieces[0] + pieces[1]) + (pieces[2] + pieces[3])) + ((pieces[4] + pieces[5]) + (pieces[6] + pieces[7]))
        return state_ref[fr * MDEV : (fr + 1) * MDEV, :] + summed

    def put(fr, value):
        ns_ref[fr * MDEV : (fr + 1) * MDEV, :] = value
        st_ref[fr * WAVES : (fr + 1) * WAVES, :] = jnp.transpose(jnp.concatenate([value] * GROUPS, axis=0))

    for r in range(2):
        vorticity, divergence, height = total(r), total(2 + r), total(4 + r)
        put(r, vorticity * damped)
        put(2 + r, (divergence + ratio * height) / denominator * damped)
        put(4 + r, (height - stiff * divergence) / denominator * damped)


def synthesis(p_ref, st_ref, h_ref):
    for chunk in range(2):
        members = range(chunk * 3, chunk * 3 + 3)

        def body(block, carry):
            sums = list(carry)
            for k in range(8):
                plane = p_ref[block_rows(block * 8 + k, ROWS), :]
                for n, fr in enumerate(members):
                    value = st_ref[pl.ds(fr * WAVES + block * 8 + k, 1), :]
                    sums[2 * n + k % 2] = sums[2 * n + k % 2] + plane * value
            return tuple(sums)

        zero = jnp.zeros((ROWS, 128), F32)
        sums = lax.fori_loop(0, WAVES // 8, body, (zero,) * 6)
        for n, fr in enumerate(members):
            f, r = divmod(fr, 2)
            north = sums[2 * n] + sums[2 * n + 1]
            south = sums[2 * n] - sums[2 * n + 1]
            for s in range(3):
                rows = slice(s * 16, (s + 1) * 16)
                h_ref[pl.ds(r * 9 + f * 3 + s, 16, stride=MSG_C), :] = north[rows]
                h_ref[pl.ds(16 * MSG_C + r * 9 + f * 3 + 2 - s, 16, stride=MSG_C), :] = south[rows]


def inverse_operand(south, cp_ref, y_ref):
    def body(column, _):
        items = swap_groups(
            [cp_ref[pl.ds((column * 4 + g // 2) * MSG_C + (g % 2) * 9, 16), :] for g in range(GROUPS)]
        )
        for a in range(GROUPS):
            row = mirrored(south, a)
            high, low = split(items[a])
            y_ref[block_rows(row, 16), block_rows(column, 128)] = high
            y_ref[block_rows(row + GROUPS, 16), block_rows(column, 128)] = low
        return 0

    lax.fori_loop(0, 2 * WAVES // 128, body, 0)


def inverse_transform(q, y_ref, high_ref, low_ref, block_ref, w_ref, send):
    lane = lanes((16, 128))

    def body(step, _):
        block = (step + q // 4) % 8
        block_ref[...] = product(y_ref, high_ref, low_ref, block)
        for index in range(4):
            half, par = divmod(index, 2)
            owner = block * 4 + index
            columns = [None] * 3
            for a in range(GROUPS):
                first, offset = divmod(BLK * a, 128)
                piece = block_ref[a * 16 : (a + 1) * 16, half * 128 : (half + 1) * 128]
                shift = (offset - 64 * par) % 128
                piece = pltpu.roll(piece, shift, 1) if shift else piece
                if columns[first] is None:
                    columns[first] = piece
                else:
                    columns[first] = jnp.where(lane >= offset, piece, columns[first])
                if offset + BLK > 128:
                    columns[first + 1] = piece
            for c in range(3):
                w_ref[pl.ds(owner * MSG_G + c, 9, stride=3), :] = columns[c][0:9]
            send(owner)
        return 0

    lax.fori_loop(0, 8, body, 0)


def scatter_rows(o_ref, out_ref):
    def body(d, _):
        c, h = d // 2, d % 2
        for f in range(3):
            out_ref[pl.ds((f * MODES + c) * 18 + h * 9, 9), :] = o_ref[pl.ds(d * MSG_G + f * 9, 9), :]
        return 0

    lax.fori_loop(0, LON, body, 0)


def slot_of(source):
    return jnp.where(source < 16, source, 47 - source)


def kernel(
    t_ref,
    state_ref,
    start_ref,
    stiff_ref,
    damp_ref,
    fh_any,
    fl_any,
    ih_any,
    il_any,
    ns_ref,
    out_ref,
    fh_ref,
    fl_ref,
    ih_ref,
    il_ref,
    sb_ref,
    r_ref,
    x_ref,
    fblock_ref,
    m_ref,
    g_ref,
    even_ref,
    odd_ref,
    slope_ref,
    lag_ref,
    trig_ref,
    p_ref,
    a_ref,
    st_ref,
    h_ref,
    cp_ref,
    y_ref,
    iblock_ref,
    w_ref,
    o_ref,
    const_sem,
    send_sem,
    recv_sem,
):
    q = lax.axis_index("lon")
    p = lax.axis_index("lat")
    owned = q // 2
    half = q % 2
    south = p >= LAT // 2
    my_source = slot_of(p * 2 + half)

    loads = [
        pltpu.make_async_copy(source, target, const_sem.at[index])
        for index, (source, target) in enumerate(
            ((fh_any, fh_ref), (fl_any, fl_ref), (ih_any, ih_ref), (il_any, il_ref))
        )
    ]
    for load in loads:
        load.start()

    def grid_peer(n):
        return n, p

    def wave_peer(n):
        return n, owned

    def row_peer(n):
        source = slot_of(n)
        return p * 2 + source % 2, source // 2

    def message(stage, n):
        if stage == 0:
            return grid_peer(n), sb_ref.at[pl.ds(n * MSG_G, MSG_G)], r_ref, q, MSG_G
        if stage == 1:
            return wave_peer(n), m_ref.at[pl.ds(n * MSG_C, MSG_C)], g_ref, my_source, MSG_C
        if stage == 2:
            return row_peer(n), h_ref.at[pl.ds(n * MSG_C, MSG_C)], cp_ref, q, MSG_C
        return grid_peer(n), w_ref.at[pl.ds(n * MSG_G, MSG_G)], o_ref, q, MSG_G

    def remote(stage, n):
        (lon, lat), source, target, slot, size = message(stage, n)
        here = jnp.logical_and(lon == q, lat == p)
        copy = pltpu.make_async_remote_copy(
            src_ref=source,
            dst_ref=target.at[pl.ds(slot * size, size)],
            send_sem=send_sem.at[stage, n],
            recv_sem=recv_sem.at[stage, slot],
            device_id=(lon, lat),
            device_id_type=MESH,
        )
        return here, copy

    def send(stage, n):
        (lon, lat), source, target, slot, size = message(stage, n)
        here, copy = remote(stage, n)

        @pl.when(jnp.logical_not(here))
        def _():
            copy.start()

        @pl.when(here)
        def _():
            pltpu.make_async_copy(
                source, target.at[pl.ds(slot * size, size)], recv_sem.at[stage, slot]
            ).start()

    def finish(stage):
        def body(n, _):
            here, copy = remote(stage, n)

            @pl.when(jnp.logical_not(here))
            def _():
                copy.wait_send()

            return 0

        lax.fori_loop(0, 32, body, 0)

    def receive(stage):
        size = MSG_G if stage in (0, 3) else MSG_C
        target = (r_ref, g_ref, cp_ref, o_ref)[stage]

        def body(n, _):
            part = target.at[pl.ds(n * size, size)]
            pltpu.make_async_copy(part, part, recv_sem.at[stage, n]).wait()
            return 0

        lax.fori_loop(0, 32, body, 0)

    barrier = pltpu.get_barrier_semaphore()

    def greet(n, _):
        for peer in (grid_peer, wave_peer, row_peer):
            lon, lat = peer(n)

            @pl.when(jnp.logical_not(jnp.logical_and(lon == q, lat == p)))
            def _():
                pl.semaphore_signal(barrier, inc=1, device_id=(lon, lat), device_id_type=MESH)

        return 0

    lax.fori_loop(0, 32, greet, 0)
    gather_rows(t_ref, sb_ref)
    pl.semaphore_wait(barrier, jnp.where(owned == p, 93, 95))

    lax.fori_loop(0, LON, lambda n, _: (send(0, (n + q + 1) % LON), 0)[1], 0)
    legendre_tables(q, start_ref, slope_ref, lag_ref, trig_ref, p_ref)
    receive(0)
    forward_operand(r_ref, x_ref)
    loads[0].wait()
    loads[1].wait()
    forward_transform(q, south, x_ref, fh_ref, fl_ref, fblock_ref, m_ref, functools.partial(send, 1))
    receive(1)
    analysis(g_ref, trig_ref, even_ref, odd_ref, p_ref, a_ref)
    update(q, stiff_ref[p], damp_ref[p], state_ref, a_ref, ns_ref, st_ref)
    synthesis(p_ref, st_ref, h_ref)
    lax.fori_loop(0, 32, lambda n, _: (send(2, (n + q) % 32), 0)[1], 0)
    loads[2].wait()
    loads[3].wait()
    receive(2)
    inverse_operand(south, cp_ref, y_ref)
    inverse_transform(q, y_ref, ih_ref, il_ref, iblock_ref, w_ref, functools.partial(send, 3))
    receive(3)
    scatter_rows(o_ref, out_ref)
    for stage in range(4):
        finish(stage)


def body(tendency, state, stiffness, damping):
    fields, modes = tendency.shape[0], tendency.shape[1]
    rows = fields * modes * 18
    vmem = pl.BlockSpec(memory_space=pltpu.VMEM)
    smem = pl.BlockSpec(memory_space=pltpu.SMEM)
    anywhere = pl.BlockSpec(memory_space=pl.ANY)
    constants = fourier_constants()
    new_state, new_fields = pl.pallas_call(
        kernel,
        out_shape=(
            jax.ShapeDtypeStruct((FR * MDEV, WAVES), F32),
            jax.ShapeDtypeStruct((rows, 128), F32),
        ),
        in_specs=[vmem, vmem, vmem, smem, smem] + [anywhere] * 4,
        out_specs=(vmem, vmem),
        scratch_shapes=[
            pltpu.VMEM((64 * LON, 2 * WAVES), BF16),
            pltpu.VMEM((64 * LON, 2 * WAVES), BF16),
            pltpu.VMEM((2 * WAVES, 64 * LON), BF16),
            pltpu.VMEM((2 * WAVES, 64 * LON), BF16),
            pltpu.VMEM((LON * MSG_G, 128), F32),
            pltpu.VMEM((LON * MSG_G + 32, 128), F32),
            pltpu.VMEM((256, 64 * LON), BF16),
            pltpu.VMEM((128, 256), F32),
            pltpu.VMEM((32 * MSG_C, 128), F32),
            pltpu.VMEM((32 * MSG_C, 128), F32),
            pltpu.VMEM((FR * ROWS, 128), F32),
            pltpu.VMEM((FR * ROWS, 128), F32),
            pltpu.VMEM((WAVES, 128), F32),
            pltpu.VMEM((WAVES, 128), F32),
            pltpu.VMEM((ROWS, 128), F32),
            pltpu.VMEM((WAVES * ROWS, 128), F32),
            pltpu.VMEM((FR * WAVES, 128), F32),
            pltpu.VMEM((FR * WAVES, 128), F32),
            pltpu.VMEM((32 * MSG_C, 128), F32),
            pltpu.VMEM((32 * MSG_C + 16, 128), F32),
            pltpu.VMEM((256, 2 * WAVES), BF16),
            pltpu.VMEM((128, 256), F32),
            pltpu.VMEM((LON * MSG_G, 128), F32),
            pltpu.VMEM((LON * MSG_G, 128), F32),
            pltpu.SemaphoreType.DMA((4,)),
            pltpu.SemaphoreType.DMA((4, 32)),
            pltpu.SemaphoreType.DMA((4, 32)),
        ],
        compiler_params=pltpu.CompilerParams(
            collective_id=0, has_side_effects=True, vmem_limit_bytes=52 * 2**20
        ),
        name="spectral_step",
    )(
        tendency.reshape(rows, 128),
        state.reshape(FR * MDEV, WAVES),
        jnp.asarray(start_constants()),
        stiffness,
        damping,
        *[jnp.asarray(table) for table in constants],
    )
    return new_state.reshape(state.shape), new_fields.reshape(tendency.shape)


def solution(mesh):
    return jax.shard_map(
        body,
        mesh=mesh,
        in_specs=(P(None, None, "lat", "lon", None), P("lat", None, None, "lon", None), P(), P()),
        out_specs=(P("lat", None, None, "lon", None), P(None, None, "lat", "lon", None)),
        check_vma=False,
    )
```

```python
import functools
import math

import jax
import jax.numpy as jnp
import ml_dtypes
import numpy as np
from jax import lax
from jax.experimental import pallas as pl
from jax.experimental.pallas import tpu as pltpu
from jax.sharding import PartitionSpec as P

NLAT = 768
NLON = 1536
WAVES = 512
MODES = 16
LON = 32
LAT = 16
BLK = 48
MDEV = 16
GROUPS = 8
MSG_G = 27
SLOT_G = 48
SLOT_C = 32
MSG_C = 18
FR = 6
PLANE = 384
ROWS = 48
MESH = pl.DeviceIdType.MESH
F32 = jnp.float32
BF16 = jnp.bfloat16


def split_constant(table):
    high = table.astype(np.float32).astype(ml_dtypes.bfloat16)
    low = (table - high.astype(np.float64)).astype(np.float32).astype(ml_dtypes.bfloat16)
    return high, low


def lon_of(place):
    return (place % 8) * 4 + place // 8


def place_of(lon):
    return (lon % 4) * 8 + lon // 4


@functools.lru_cache(maxsize=None)
def fourier_constants():
    slot = np.arange(LON * 64)
    block, inner = lon_of(slot // 64), slot % 64
    lon = block * BLK + inner
    valid = (inner < BLK)[:, None]
    wave = np.arange(WAVES)
    angle = 2.0 * np.pi / NLON * ((lon[:, None] * wave[None, :]) % NLON)
    owners = lon_of(np.arange(LON))
    cosine = np.where(valid, np.cos(angle), 0.0).reshape(-1, LON, MDEV)[:, owners]
    sine = np.where(valid, np.sin(angle), 0.0).reshape(-1, LON, MDEV)[:, owners]
    basis = np.stack([cosine, -sine], axis=2).reshape(LON * 64, 2 * WAVES)
    factor = np.where(wave == 0, 1.0, 2.0).reshape(LON, 1, MDEV) / WAVES
    factor = np.broadcast_to(factor[owners], (LON, 2, MDEV)).reshape(2 * WAVES, 1)
    return split_constant(basis / NLON) + split_constant(factor * basis.T)


@functools.lru_cache(maxsize=None)
def start_constants():
    start = [
        (0.5 * math.log(m + 0.5) + 0.5 * math.lgamma(m + 0.5) - 0.5 * math.lgamma(m + 1.0) - 0.25 * math.log(math.pi))
        / math.log(2.0)
        for m in range(WAVES)
    ]
    return np.tile(np.array(start, np.float32).reshape(LON, MDEV), (1, GROUPS))


def lanes(shape):
    return lax.broadcasted_iota(jnp.int32, shape, len(shape) - 1)


def swap_groups(items):
    group = lanes(items[0].shape) // 16
    items = list(items)
    for step in (4, 2, 1):
        keep = (group & step) == 0
        for low in range(GROUPS):
            if low & step:
                continue
            high = low + step
            x, y = items[low], items[high]
            items[low] = jnp.where(keep, x, pltpu.roll(y, 16 * step, 1))
            items[high] = jnp.where(keep, pltpu.roll(x, 128 - 16 * step, 1), y)
    return items


def fold_rows(parts):
    row = lax.broadcasted_iota(jnp.int32, (8, 128), 0)
    upper = row < 4
    four = []
    for index in range(4):
        x, y = parts[index], parts[index + 4]
        four.append(jnp.where(upper, x, y) + pltpu.roll(jnp.where(upper, y, x), 4, 0))
    for step in (2, 1):
        keep = (row & step) == 0
        four = [
            jnp.where(
                keep,
                four[index] + pltpu.roll(four[index], 8 - step, 0),
                four[index + step] + pltpu.roll(four[index + step], step, 0),
            )
            for index in range(step)
        ]
    return four[0]


def split(x):
    high = x.astype(BF16)
    return high, (x - high.astype(F32)).astype(BF16)


def mirrored(south, a):
    return jnp.where(south, GROUPS - 1 - a, a)


def block_rows(index, size):
    return pl.ds(pl.multiple_of(index * size, size), size)


def gather_rows(t_ref, sb_ref):
    def body(d, _):
        c, h = d // 2, d % 2
        for f in range(3):
            sb_ref[pl.ds(d * MSG_G + f * 9, 9), :] = t_ref[pl.ds((f * MODES + c) * 18 + h * 9, 9), :]
        return 0

    lax.fori_loop(0, LON, body, 0)


def legendre_tables(q, start_ref, slope_ref, lag_ref, trig_ref, p_ref):
    wave = (lanes((1, 128)) % MDEV + q * MDEV).astype(F32)

    def coefficients(block, _):
        offsets = (lax.broadcasted_iota(jnp.int32, (64, 128), 0) + block * 64).astype(F32)
        degree = wave + offsets
        spacing = jnp.maximum(offsets * (2.0 * wave + offsets), 1.0)
        slope = jnp.sqrt(jnp.maximum(4.0 * degree * degree - 1.0, 0.0) / spacing)
        numerator = (2.0 * degree + 1.0) * (offsets - 1.0) * (degree - 1.0 + wave)
        lag = jnp.sqrt(jnp.maximum(numerator, 0.0) / (jnp.maximum(2.0 * degree - 3.0, 1.0) * spacing))
        first = offsets < 0.5
        slope_ref[block_rows(block, 64), :] = jnp.where(first, 0.0, slope)
        lag_ref[block_rows(block, 64), :] = jnp.where(first, 1.0, lag)
        return 0

    lax.fori_loop(0, WAVES // 64, coefficients, 0)
    row = lax.broadcasted_iota(jnp.int32, (ROWS, 128), 0)
    colat = ((row // 24) * 8 + row % 8) * 24 + (row // 8 % 3) * 8 + lanes((ROWS, 128)) // MDEV
    theta = math.pi * (colat.astype(F32) + 0.5) / NLAT
    mu = jnp.cos(theta)
    sine = jnp.sin(theta)
    trig_ref[...] = sine * (WAVES * math.pi / NLAT)
    log_sine = jnp.log(sine) * (1.0 / math.log(2.0))
    coarse = jnp.floor(log_sine * 1024.0) * (1.0 / 1024.0)
    whole = wave * coarse
    exponent = jnp.floor(whole)
    fraction = (whole - exponent) + wave * (log_sine - coarse) + start_ref[pl.ds(q, 1), :]
    lower = -jnp.exp2(fraction)
    upper = jnp.zeros_like(lower)

    def body(block, carry):
        upper, lower, exponent = carry
        growth = jnp.exp2(jnp.maximum(exponent, -140.0))
        for offset in range(8):
            k = block * 8 + offset
            moved = (slope_ref[pl.ds(k, 1), :] * mu) * upper - lag_ref[pl.ds(k, 1), :] * lower
            upper, lower = moved, upper
            inside = wave + k.astype(F32) <= WAVES - 1.0
            p_ref[pl.ds(block * PLANE + offset, ROWS, stride=8), :] = jnp.where(inside, upper * growth, 0.0)
        big = jnp.maximum(jnp.abs(upper), jnp.abs(lower)) > 2.0**32
        scale = jnp.where(big, 2.0**-32, 1.0)
        return upper * scale, lower * scale, exponent + jnp.where(big, 32.0, 0.0)

    lax.fori_loop(0, WAVES // 8, body, (upper, lower, exponent))


def forward_operand(group, r_ref, x_ref):
    lane = lanes((16, 128))

    def body(pair, _):
        first_row = (group * 8 + 2 * pair) * SLOT_G
        columns = [[r_ref[pl.ds(first_row + par * SLOT_G + c, 16, stride=3), :] for c in range(3)] for par in range(2)]
        for a in range(GROUPS):
            first, offset = divmod(BLK * a, 128)
            pieces = []
            for par in range(2):
                source = columns[par][first]
                if offset + BLK > 128:
                    source = jnp.where(lane >= offset, source, columns[par][first + 1])
                shift = (64 * par - offset) % 128
                pieces.append(pltpu.roll(source, shift, 1) if shift else source)
            high, low = split(jnp.where(lane < 64, pieces[0], pieces[1]))
            x_ref[a * 16 : (a + 1) * 16, block_rows(pair, 128)] = high
            x_ref[128 + a * 16 : 128 + (a + 1) * 16, block_rows(pair, 128)] = low
        return 0

    lax.fori_loop(0, 4, body, 0)


def product(x_ref, high_ref, low_ref, rows, columns):
    both = jnp.dot(x_ref[...], high_ref[rows, columns], preferred_element_type=F32)
    rest = jnp.dot(x_ref[0:128, :], low_ref[rows, columns], preferred_element_type=F32)
    return both[0:128] + both[128:256] + rest


def add_products(group, x_ref, high_ref, low_ref, sum_ref):
    rows = block_rows(group, x_ref.shape[1])

    def body(block, _):
        columns = block_rows(block, 256)
        sum_ref[:, columns] += product(x_ref, high_ref, low_ref, rows, columns)
        return 0

    lax.fori_loop(0, sum_ref.shape[1] // 256, body, 0)


def forward_blocks(q, south, group, x_ref, high_ref, low_ref, sum_ref, block_ref, m_ref, send):
    rows = block_rows(group, x_ref.shape[1])

    def body(step, _):
        block = (step + q % 4) % 4
        columns = block_rows(block, 256)
        block_ref[...] = sum_ref[:, columns] + product(x_ref, high_ref, low_ref, rows, columns)
        for half in range(2):
            items = swap_groups(
                [block_ref[block_rows(mirrored(south, a), 16), half * 128 : (half + 1) * 128] for a in range(GROUPS)]
            )
            for group in range(GROUPS):
                owner = block * 8 + half * 4 + group // 2
                m_ref[pl.ds(owner * MSG_C + (group % 2) * 9, 9), :] = items[group][0:9]
            for index in range(4):
                send(block * 8 + half * 4 + index)
        return 0

    lax.fori_loop(0, 4, body, 0)


def analysis(g_ref, trig_ref, eo_ref, p_ref, a_ref):
    for n in range(2):
        for s in range(3):
            weight = trig_ref[n * 24 + s * 8 : n * 24 + s * 8 + 8, :]
            for f in range(3):
                for r in range(2):
                    north = g_ref[pl.ds(n * 8 * MSG_C + r * 9 + f * 3 + s, 8, stride=MSG_C), :]
                    south = g_ref[pl.ds((16 + n * 8) * MSG_C + r * 9 + f * 3 + 2 - s, 8, stride=MSG_C), :]
                    first = (f * 2 + r) * PLANE + (n * 24 + s * 8) * 8
                    even, odd = (north + south) * weight, (north - south) * weight
                    for k in range(8):
                        eo_ref[pl.ds(first + k, 8, stride=8), :] = odd if k % 2 else even

    def body(quad, _):
        def rows(group, sums):
            sums = list(sums)
            for row in range(8):
                first = (group * 8 + row) * 8
                fields = [eo_ref[pl.ds(pl.multiple_of(fr * PLANE + first, 8), 8), :] for fr in range(FR)]
                for b in range(4):
                    plane = p_ref[pl.ds(pl.multiple_of((quad * 4 + b) * PLANE + first, 8), 8), :]
                    for fr in range(FR):
                        sums[b * FR + fr] = sums[b * FR + fr] + plane * fields[fr]
            return tuple(sums)

        sums = lax.fori_loop(0, ROWS // 8, rows, (jnp.zeros((8, 128), F32),) * (4 * FR))
        for b in range(4):
            for fr in range(FR):
                a_ref[pl.ds(pl.multiple_of(fr * WAVES + (quad * 4 + b) * 8, 8), 8), :] = sums[b * FR + fr]
        return 0

    lax.fori_loop(0, WAVES // 32, body, 0)


def update(q, stiff, damp, state_ref, a_ref, ns_ref, st_ref):
    wave = (lax.broadcasted_iota(jnp.int32, (MDEV, WAVES), 0) + q * MDEV).astype(F32)
    degree = wave + lanes((MDEV, WAVES)).astype(F32)
    ratio = degree * (degree + 1.0) / (WAVES * (WAVES - 1.0))
    inside = degree <= WAVES - 1.0
    denominator = 1.0 + stiff * ratio
    damped = jnp.where(inside, 1.0 / (1.0 + damp * ratio * ratio), 0.0)

    def total(fr):
        turned = jnp.transpose(a_ref[fr * WAVES : (fr + 1) * WAVES, :])
        pieces = [turned[16 * n : 16 * n + 16] for n in range(GROUPS)]
        summed = ((pieces[0] + pieces[1]) + (pieces[2] + pieces[3])) + ((pieces[4] + pieces[5]) + (pieces[6] + pieces[7]))
        return state_ref[fr * MDEV : (fr + 1) * MDEV, :] + summed

    def put(fr, value):
        ns_ref[fr * MDEV : (fr + 1) * MDEV, :] = value
        st_ref[fr * WAVES : (fr + 1) * WAVES, :] = jnp.transpose(jnp.concatenate([value] * GROUPS, axis=0))

    for r in range(2):
        vorticity, divergence, height = total(r), total(2 + r), total(4 + r)
        put(r, vorticity * damped)
        put(2 + r, (divergence + ratio * height) / denominator * damped)
        put(4 + r, (height - stiff * divergence) / denominator * damped)


def synthesis(p_ref, st_ref, h_ref):
    sign = jnp.where(lax.broadcasted_iota(jnp.int32, (8, 128), 0) % 2 == 0, 1.0, -1.0)

    def body(group, _):
        n, s = group // 3, group % 3
        for chunk in range(2):

            def degrees(block, sums):
                sums = list(sums)
                for b in range(2):
                    first = (block * 2 + b) * PLANE + group * 64
                    values = [
                        st_ref[pl.ds(pl.multiple_of((chunk * 3 + m) * WAVES + (block * 2 + b) * 8, 8), 8), :]
                        for m in range(3)
                    ]
                    for row in range(8):
                        plane = p_ref[pl.ds(pl.multiple_of(first + row * 8, 8), 8), :]
                        for m in range(3):
                            sums[m * 8 + row] = sums[m * 8 + row] + plane * values[m]
                return tuple(sums)

            sums = lax.fori_loop(0, WAVES // 16, degrees, (jnp.zeros((8, 128), F32),) * 24)
            for m in range(3):
                f, r = divmod(chunk * 3 + m, 2)
                parts = list(sums[m * 8 : m * 8 + 8])
                line = r * 9 + f * 3
                h_ref[pl.ds(n * 8 * MSG_C + line + s, 8, stride=MSG_C), :] = fold_rows(parts)
                parts = [part * sign for part in parts]
                h_ref[pl.ds((16 + n * 8) * MSG_C + line + 2 - s, 8, stride=MSG_C), :] = fold_rows(parts)
        return 0

    lax.fori_loop(0, ROWS // 8, body, 0)


def inverse_operand(group, south, cp_ref, y_ref):
    for column in range(2):
        first = (group * 8 + column * 4) * SLOT_C
        items = swap_groups([cp_ref[pl.ds(first + g // 2 * SLOT_C + g % 2 * 9, 16), :] for g in range(GROUPS)])
        for a in range(GROUPS):
            row = mirrored(south, a)
            high, low = split(items[a])
            y_ref[block_rows(row, 16), column * 128 : (column + 1) * 128] = high
            y_ref[block_rows(row + GROUPS, 16), column * 128 : (column + 1) * 128] = low


def inverse_blocks(q, group, y_ref, high_ref, low_ref, sum_ref, block_ref, w_ref, send):
    lane = lanes((16, 128))
    rows = block_rows(group, y_ref.shape[1])

    def body(step, _):
        block = (step + q % 4 * 2) % 8
        columns = block_rows(block, 256)
        block_ref[...] = sum_ref[:, columns] + product(y_ref, high_ref, low_ref, rows, columns)
        for index in range(4):
            half, par = divmod(index, 2)
            owner = block * 4 + index
            columns = [None] * 3
            for a in range(GROUPS):
                first, offset = divmod(BLK * a, 128)
                piece = block_ref[a * 16 : (a + 1) * 16, half * 128 : (half + 1) * 128]
                shift = (offset - 64 * par) % 128
                piece = pltpu.roll(piece, shift, 1) if shift else piece
                if columns[first] is None:
                    columns[first] = piece
                else:
                    columns[first] = jnp.where(lane >= offset, piece, columns[first])
                if offset + BLK > 128:
                    columns[first + 1] = piece
            for c in range(3):
                w_ref[pl.ds(owner * MSG_G + c, 9, stride=3), :] = columns[c][0:9]
            send(owner)
        return 0

    lax.fori_loop(0, 8, body, 0)


def slot_of(source):
    return jnp.where(source < 16, source, 47 - source)


def kernel(
    t_any,
    state_any,
    start_any,
    stiff_any,
    damp_any,
    fh_any,
    fl_any,
    ih_any,
    il_any,
    ns_ref,
    o_ref,
    t_ref,
    state_ref,
    start_ref,
    stiff_ref,
    damp_ref,
    fh_ref,
    fl_ref,
    ih_ref,
    il_ref,
    sb_ref,
    r_ref,
    x_ref,
    fsum_ref,
    block_ref,
    m_ref,
    g_ref,
    eo_ref,
    slope_ref,
    lag_ref,
    trig_ref,
    p_ref,
    a_ref,
    st_ref,
    h_ref,
    cp_ref,
    y_ref,
    isum_ref,
    w_ref,
    load_sem,
    send_sem,
    recv_sem,
    ready_sem,
):
    q = lax.axis_index("lon")
    p = lax.axis_index("lat")
    here = place_of(q)
    south = p >= LAT // 2
    owned, half = q // 2, q % 2
    my_source = slot_of(p * 2 + half)
    back_mode = (q // 4 + 16 - p // 2 - p % 2 * 4) % 8 * 2 + q % 4 // 2
    back_half = q % 2
    back_slot = slot_of(p * 2 + back_half)

    barrier = pltpu.get_barrier_semaphore()

    def greet_lon(n, _):
        pl.semaphore_signal(barrier, inc=1, device_id=((q + n) % LON, p), device_id_type=MESH)
        return 0

    def greet_lat(n, _):
        pl.semaphore_signal(barrier, inc=1, device_id=(q, (p + n) % LAT), device_id_type=MESH)
        return 0

    lax.fori_loop(1, LON, greet_lon, 0)
    lax.fori_loop(1, LAT, greet_lat, 0)

    loads = [
        pltpu.make_async_copy(source, target, load_sem.at[index])
        for index, (source, target) in enumerate(
            (
                (t_any, t_ref),
                (start_any, start_ref),
                (fh_any, fh_ref),
                (fl_any, fl_ref),
                (state_any, state_ref),
                (stiff_any, stiff_ref),
                (damp_any, damp_ref),
                (ih_any, ih_ref),
                (il_any, il_ref),
            )
        )
    ]
    for load in loads:
        load.start()

    def copy(source, target, stage, group, peer):
        return pltpu.make_async_remote_copy(
            src_ref=source,
            dst_ref=target,
            send_sem=send_sem.at[stage],
            recv_sem=recv_sem.at[stage, group],
            device_id=peer,
            device_id_type=MESH,
        )

    def copy_or_keep(source, target, stage, group, peer):
        lon, lat = peer
        own = jnp.logical_and(lon == q, lat == p)

        @pl.when(jnp.logical_not(own))
        def _():
            copy(source, target, stage, group, peer).start()

        @pl.when(own)
        def _():
            pltpu.make_async_copy(source, target, recv_sem.at[stage, group]).start()

    def wait(ref, first, rows, sem):
        part = ref.at[pl.ds(first, rows)]
        pltpu.make_async_copy(part, part, sem).wait()

    def send_grid(n, _):
        place = (here // 8 + n // 8) % 4 * 8 + (here + n) % 8
        lon = lon_of(place)
        copy(sb_ref.at[pl.ds(lon * MSG_G, MSG_G)], r_ref.at[pl.ds(here * SLOT_G, MSG_G)], 0, here // 8, (lon, p)).start()
        return 0

    def send_waves(place):
        copy_or_keep(
            m_ref.at[pl.ds(place * MSG_C, MSG_C)],
            g_ref.at[pl.ds(my_source * MSG_C, MSG_C)],
            1,
            0,
            (lon_of(place), owned),
        )

    def send_rows(n, _):
        slot = (here // 8 + n // 8) % 4 * 8 + (here + n) % 8
        source = slot_of(slot)
        lat = source // 2
        lon = (p // 2 + lat // 2 + lat % 2 * 4) % 8 * 4 + p % 2 * 2 + source % 2
        copy_or_keep(
            h_ref.at[pl.ds(slot * MSG_C, MSG_C)],
            cp_ref.at[pl.ds(here * SLOT_C, MSG_C)],
            2,
            here // 8,
            (lon, lat),
        )
        return 0

    back_rows = pl.ds((back_mode * 2 + back_half) * MSG_G, MSG_G)

    def send_back(place):
        lon = lon_of(place)
        copy_or_keep(w_ref.at[pl.ds(place * MSG_G, MSG_G)], o_ref.at[back_rows], 3, 0, (lon, p))

    loads[0].wait()
    gather_rows(t_ref, sb_ref)
    pl.semaphore_wait(barrier, LON - 1 + LAT - 1)
    lax.fori_loop(1, LON, send_grid, 0)
    pltpu.make_async_copy(
        sb_ref.at[pl.ds(q * MSG_G, MSG_G)], r_ref.at[pl.ds(here * SLOT_G, MSG_G)], recv_sem.at[0, here // 8]
    ).start()

    def tell(n, _):
        pl.semaphore_signal(ready_sem, inc=1, device_id=(q, (p + n) % LAT), device_id_type=MESH)
        return 0

    lax.fori_loop(1, LAT, tell, 0)

    loads[1].wait()
    legendre_tables(q, start_ref, slope_ref, lag_ref, trig_ref, p_ref)
    fsum_ref[...] = jnp.zeros_like(fsum_ref)
    isum_ref[...] = jnp.zeros_like(isum_ref)
    loads[2].wait()
    loads[3].wait()

    def grid_group(step):
        group = (here // 8 + 4 - step) % 4
        wait(r_ref, group * 8 * SLOT_G, 8 * MSG_G, recv_sem.at[0, group])
        forward_operand(group, r_ref, x_ref)
        return group

    def forward_step(step, _):
        add_products(grid_group(step), x_ref, fh_ref, fl_ref, fsum_ref)
        return 0

    lax.fori_loop(0, 3, forward_step, 0)
    group = grid_group(3)
    pl.semaphore_wait(ready_sem, LAT - 1)
    forward_blocks(q, south, group, x_ref, fh_ref, fl_ref, fsum_ref, block_ref, m_ref, send_waves)
    for load in loads[4:]:
        load.wait()
    wait(sb_ref, 0, (LON - 1) * MSG_G, send_sem.at[0])
    wait(g_ref, 0, 32 * MSG_C, recv_sem.at[1, 0])
    analysis(g_ref, trig_ref, eo_ref, p_ref, a_ref)
    update(q, stiff_ref[p], damp_ref[p], state_ref, a_ref, ns_ref, st_ref)
    synthesis(p_ref, st_ref, h_ref)
    lax.fori_loop(0, 32, send_rows, 0)

    def wait_sent(ref, own, stage):
        @pl.when(own)
        def _():
            wait(ref, 0, 31 * MSG_C, send_sem.at[stage])

        @pl.when(jnp.logical_not(own))
        def _():
            wait(ref, 0, 32 * MSG_C, send_sem.at[stage])

    wait_sent(m_ref, owned == p, 1)

    def waves_group(step):
        group = (back_slot // 8 + 4 - step) % 4
        wait(cp_ref, group * 8 * SLOT_C, 8 * MSG_C, recv_sem.at[2, group])
        inverse_operand(group, south, cp_ref, y_ref)
        return group

    def inverse_step(step, _):
        add_products(waves_group(step), y_ref, ih_ref, il_ref, isum_ref)
        return 0

    lax.fori_loop(0, 3, inverse_step, 0)
    inverse_blocks(q, waves_group(3), y_ref, ih_ref, il_ref, isum_ref, block_ref, w_ref, send_back)
    wait_sent(h_ref, back_mode == p, 2)
    wait(o_ref, 0, LON * MSG_G, recv_sem.at[3, 0])
    wait(w_ref, 0, (LON - 1) * MSG_G, send_sem.at[3])


def place_kernel(ns_ref, o_ref, ns_any, out_any, ns_sem, out_sem):
    state_copy = pltpu.make_async_copy(ns_ref, ns_any, ns_sem)
    state_copy.start()

    def body(d, _):
        for f in range(3):
            pltpu.make_async_copy(
                o_ref.at[pl.ds(d * MSG_G + f * 9, 9)],
                out_any.at[pl.ds((f * MODES + d // 2) * 18 + d % 2 * 9, 9)],
                out_sem,
            ).start()
        return 0

    lax.fori_loop(0, LON, body, 0)
    pltpu.make_async_copy(o_ref, out_any, out_sem).wait()
    state_copy.wait()


def body(tendency, state, stiffness, damping):
    rows = LON * MSG_G
    vmem = pl.BlockSpec(memory_space=pltpu.VMEM)
    anywhere = pl.BlockSpec(memory_space=pl.ANY)
    shapes = (jax.ShapeDtypeStruct((FR * MDEV, WAVES), F32), jax.ShapeDtypeStruct((rows, 128), F32))
    new_state, new_fields = pl.pallas_call(
        kernel,
        out_shape=shapes,
        in_specs=[anywhere] * 9,
        out_specs=(vmem, vmem),
        scratch_shapes=[
            pltpu.VMEM((rows, 128), F32),
            pltpu.VMEM((FR * MDEV, WAVES), F32),
            pltpu.VMEM((LON, 128), F32),
            pltpu.SMEM((MODES,), F32),
            pltpu.SMEM((MODES,), F32),
            pltpu.VMEM((64 * LON, 2 * WAVES), BF16),
            pltpu.VMEM((64 * LON, 2 * WAVES), BF16),
            pltpu.VMEM((2 * WAVES, 64 * LON), BF16),
            pltpu.VMEM((2 * WAVES, 64 * LON), BF16),
            pltpu.VMEM((rows, 128), F32),
            pltpu.VMEM((LON * SLOT_G, 128), F32),
            pltpu.VMEM((256, 512), BF16),
            pltpu.VMEM((128, 2 * WAVES), F32),
            pltpu.VMEM((128, 256), F32),
            pltpu.VMEM((32 * MSG_C, 128), F32),
            pltpu.VMEM((32 * MSG_C, 128), F32),
            pltpu.VMEM((FR * PLANE, 128), F32),
            pltpu.VMEM((WAVES, 128), F32),
            pltpu.VMEM((WAVES, 128), F32),
            pltpu.VMEM((ROWS, 128), F32),
            pltpu.VMEM((WAVES // 8 * PLANE, 128), F32),
            pltpu.VMEM((FR * WAVES, 128), F32),
            pltpu.VMEM((FR * WAVES, 128), F32),
            pltpu.VMEM((32 * MSG_C, 128), F32),
            pltpu.VMEM((32 * SLOT_C, 128), F32),
            pltpu.VMEM((256, 256), BF16),
            pltpu.VMEM((128, 64 * LON), F32),
            pltpu.VMEM((rows, 128), F32),
            pltpu.SemaphoreType.DMA((9,)),
            pltpu.SemaphoreType.DMA((4,)),
            pltpu.SemaphoreType.DMA((4, 4)),
            pltpu.SemaphoreType.REGULAR,
        ],
        compiler_params=pltpu.CompilerParams(
            collective_id=0, has_side_effects=True, vmem_limit_bytes=63 * 2**20
        ),
        name="spectral_step",
    )(
        tendency.reshape(rows, 128),
        state.reshape(FR * MDEV, WAVES),
        jnp.asarray(start_constants()),
        stiffness,
        damping,
        *[jnp.asarray(table) for table in fourier_constants()],
    )
    new_state, new_fields = pl.pallas_call(
        place_kernel,
        out_shape=shapes,
        in_specs=[vmem, vmem],
        out_specs=(anywhere, anywhere),
        scratch_shapes=[pltpu.SemaphoreType.DMA, pltpu.SemaphoreType.DMA],
        name="place_rows",
    )(new_state, new_fields)
    return new_state.reshape(state.shape), new_fields.reshape(tendency.shape)


def solution(mesh):
    return jax.shard_map(
        body,
        mesh=mesh,
        in_specs=(P(None, None, "lat", "lon", None), P("lat", None, None, "lon", None), P(), P()),
        out_specs=(P("lat", None, None, "lon", None), P(None, None, "lat", "lon", None)),
        check_vma=False,
    )
```

```python
import functools
import math

import jax
import jax.numpy as jnp
import ml_dtypes
import numpy as np
from jax import lax
from jax.experimental import pallas as pl
from jax.experimental.pallas import tpu as pltpu
from jax.sharding import PartitionSpec as P

NLAT = 768
NLON = 1536
WAVES = 512
MODES = 16
LON = 32
LAT = 16
BLK = 48
MDEV = 16
GROUPS = 8
MSG_G = 27
SLOT_G = 48
SLOT_C = 32
MSG_C = 18
FR = 6
HALF = 8
QUADS = 17
LINES = QUADS * 32
LINES_PAD = 768
PLANE = 384
ROWS = 48
MESH = pl.DeviceIdType.MESH
F32 = jnp.float32
BF16 = jnp.bfloat16


def split_constant(table):
    high = table.astype(np.float32).astype(ml_dtypes.bfloat16)
    low = (table - high.astype(np.float64)).astype(np.float32).astype(ml_dtypes.bfloat16)
    return high, low


def lon_of(place):
    return (place % 8) * 4 + place // 8


def place_of(lon):
    return (lon % 4) * 8 + lon // 4


@functools.lru_cache(maxsize=None)
def fourier_constants():
    slot = np.arange(LON * 64)
    block, inner = lon_of(slot // 64), slot % 64
    lon = block * BLK + inner
    valid = (inner < BLK)[:, None]
    wave = np.arange(WAVES)
    angle = 2.0 * np.pi / NLON * ((lon[:, None] * wave[None, :]) % NLON)
    owners = lon_of(np.arange(LON))
    sets = np.stack([owners, 63 - owners], axis=1)
    cosine = np.where(valid, np.cos(angle), 0.0).reshape(-1, 64, HALF)[:, sets]
    sine = np.where(valid, np.sin(angle), 0.0).reshape(-1, 64, HALF)[:, sets]
    basis = np.stack([cosine, -sine], axis=3).reshape(LON * 64, 2 * WAVES)
    factor = np.where(wave == 0, 1.0, 2.0).reshape(64, HALF)[sets] / WAVES
    factor = np.broadcast_to(factor[:, :, None, :], (LON, 2, 2, HALF)).reshape(2 * WAVES, 1)
    return split_constant(basis / NLON) + split_constant(factor * basis.T)


@functools.lru_cache(maxsize=None)
def start_constants():
    start = [
        (0.5 * math.log(m + 0.5) + 0.5 * math.lgamma(m + 0.5) - 0.5 * math.lgamma(m + 1.0) - 0.25 * math.log(math.pi))
        / math.log(2.0)
        for m in range(WAVES)
    ]
    return np.tile(np.array(start, np.float32).reshape(64, HALF), (1, 2 * GROUPS))


def lanes(shape):
    return lax.broadcasted_iota(jnp.int32, shape, len(shape) - 1)


def swap_groups(items):
    group = lanes(items[0].shape) // 16
    items = list(items)
    for step in (4, 2, 1):
        keep = (group & step) == 0
        for low in range(GROUPS):
            if low & step:
                continue
            high = low + step
            x, y = items[low], items[high]
            items[low] = jnp.where(keep, x, pltpu.roll(y, 16 * step, 1))
            items[high] = jnp.where(keep, pltpu.roll(x, 128 - 16 * step, 1), y)
    return items


def fold_rows(parts):
    row = lax.broadcasted_iota(jnp.int32, (8, 128), 0)
    upper = row < 4
    four = []
    for index in range(4):
        x, y = parts[index], parts[index + 4]
        four.append(jnp.where(upper, x, y) + pltpu.roll(jnp.where(upper, y, x), 4, 0))
    for step in (2, 1):
        keep = (row & step) == 0
        four = [
            jnp.where(
                keep,
                four[index] + pltpu.roll(four[index], 8 - step, 0),
                four[index + step] + pltpu.roll(four[index + step], step, 0),
            )
            for index in range(step)
        ]
    return four[0]


def split(x):
    high = x.astype(BF16)
    return high, (x - high.astype(F32)).astype(BF16)


def mirrored(south, a):
    return jnp.where(south, GROUPS - 1 - a, a)


def block_rows(index, size):
    return pl.ds(pl.multiple_of(index * size, size), size)


def gather_rows(t_ref, sb_ref):
    def body(d, _):
        c, h = d // 2, d % 2
        for f in range(3):
            sb_ref[pl.ds(d * MSG_G + f * 9, 9), :] = t_ref[pl.ds((f * MODES + c) * 18 + h * 9, 9), :]
        return 0

    lax.fori_loop(0, LON, body, 0)


def set_lines(q):
    return (64 - q + 3) // 4 * 32


def legendre_tables(q, start_ref, slope_ref, lag_ref, trig_ref, p_ref):
    member = lanes((1, 128)) % HALF
    waves = ((member + HALF * q).astype(F32), (member + HALF * (63 - q)).astype(F32))
    split_line = set_lines(q)

    def coefficients(block, _):
        line = lax.broadcasted_iota(jnp.int32, (32, 128), 0) + block * 32
        second = line >= split_line
        offsets = jnp.where(second, line - split_line, line).astype(F32)
        wave = jnp.where(second, waves[1], waves[0])
        degree = wave + offsets
        spacing = jnp.maximum(offsets * (2.0 * wave + offsets), 1.0)
        slope = jnp.sqrt(jnp.maximum(4.0 * degree * degree - 1.0, 0.0) / spacing)
        numerator = (2.0 * degree + 1.0) * (offsets - 1.0) * (degree - 1.0 + wave)
        lag = jnp.sqrt(jnp.maximum(numerator, 0.0) / (jnp.maximum(2.0 * degree - 3.0, 1.0) * spacing))
        first = offsets < 0.5
        slope_ref[block_rows(block, 32), :] = jnp.where(first, 0.0, slope)
        lag_ref[block_rows(block, 32), :] = jnp.where(first, 1.0, lag)
        return 0

    lax.fori_loop(0, QUADS, coefficients, 0)
    row = lax.broadcasted_iota(jnp.int32, (ROWS, 128), 0)
    colat = ((row // 24) * 8 + row % 8) * 24 + (row // 8 % 3) * 8 + lanes((ROWS, 128)) // MDEV
    theta = math.pi * (colat.astype(F32) + 0.5) / NLAT
    mu = jnp.cos(theta)
    sine = jnp.sin(theta)
    trig_ref[...] = sine * (WAVES * math.pi / NLAT)
    log_sine = jnp.log(sine) * (1.0 / math.log(2.0))
    coarse = jnp.floor(log_sine * 1024.0) * (1.0 / 1024.0)
    blocks = split_line // 8

    for which, (begin, end) in enumerate(((0, blocks), (blocks, LINES // 8))):
        wave = waves[which]
        whole = wave * coarse
        exponent = jnp.floor(whole)
        start = start_ref[pl.ds(63 - q if which else q, 1), :]
        lower = -jnp.exp2((whole - exponent) + wave * (log_sine - coarse) + start)

        def body(block, carry, begin=begin, wave=wave):
            upper, lower, exponent = carry
            growth = jnp.exp2(jnp.maximum(exponent, -140.0))
            for offset in range(8):
                line = block * 8 + offset
                moved = (slope_ref[pl.ds(line, 1), :] * mu) * upper - lag_ref[pl.ds(line, 1), :] * lower
                upper, lower = moved, upper
                k = line - begin * 8
                inside = wave + k.astype(F32) <= WAVES - 1.0
                p_ref[pl.ds(block * PLANE + offset, ROWS, stride=8), :] = jnp.where(inside, upper * growth, 0.0)
            big = jnp.maximum(jnp.abs(upper), jnp.abs(lower)) > 2.0**32
            scale = jnp.where(big, 2.0**-32, 1.0)
            return upper * scale, lower * scale, exponent + jnp.where(big, 32.0, 0.0)

        lax.fori_loop(begin, end, body, (jnp.zeros_like(lower), lower, exponent))


def forward_operand(group, r_ref, x_ref):
    lane = lanes((16, 128))

    def body(pair, _):
        first_row = (group * 8 + 2 * pair) * SLOT_G
        columns = [[r_ref[pl.ds(first_row + par * SLOT_G + c, 16, stride=3), :] for c in range(3)] for par in range(2)]
        for a in range(GROUPS):
            first, offset = divmod(BLK * a, 128)
            pieces = []
            for par in range(2):
                source = columns[par][first]
                if offset + BLK > 128:
                    source = jnp.where(lane >= offset, source, columns[par][first + 1])
                shift = (64 * par - offset) % 128
                pieces.append(pltpu.roll(source, shift, 1) if shift else source)
            high, low = split(jnp.where(lane < 64, pieces[0], pieces[1]))
            x_ref[a * 16 : (a + 1) * 16, block_rows(pair, 128)] = high
            x_ref[128 + a * 16 : 128 + (a + 1) * 16, block_rows(pair, 128)] = low
        return 0

    lax.fori_loop(0, 4, body, 0)


def product(x_ref, high_ref, low_ref, rows, columns):
    both = jnp.dot(x_ref[...], high_ref[rows, columns], preferred_element_type=F32)
    rest = jnp.dot(x_ref[0:128, :], low_ref[rows, columns], preferred_element_type=F32)
    return both[0:128] + both[128:256] + rest


def add_products(group, x_ref, high_ref, low_ref, sum_ref):
    rows = block_rows(group, x_ref.shape[1])

    def body(block, _):
        columns = block_rows(block, 256)
        sum_ref[:, columns] += product(x_ref, high_ref, low_ref, rows, columns)
        return 0

    lax.fori_loop(0, sum_ref.shape[1] // 256, body, 0)


def forward_blocks(q, south, group, x_ref, high_ref, low_ref, sum_ref, block_ref, m_ref, send):
    rows = block_rows(group, x_ref.shape[1])

    def body(step, _):
        block = (step + q % 4) % 4
        columns = block_rows(block, 256)
        block_ref[...] = sum_ref[:, columns] + product(x_ref, high_ref, low_ref, rows, columns)
        for half in range(2):
            items = swap_groups(
                [block_ref[block_rows(mirrored(south, a), 16), half * 128 : (half + 1) * 128] for a in range(GROUPS)]
            )
            for group in range(GROUPS):
                owner = block * 8 + half * 4 + group // 2
                m_ref[pl.ds(owner * MSG_C + (group % 2) * 9, 9), :] = items[group][0:9]
            for index in range(4):
                send(block * 8 + half * 4 + index)
        return 0

    lax.fori_loop(0, 4, body, 0)


def analysis(q, g_ref, trig_ref, eo_ref, p_ref, a_ref):
    for n in range(2):
        for s in range(3):
            weight = trig_ref[n * 24 + s * 8 : n * 24 + s * 8 + 8, :]
            for which in range(2):
                for f in range(3):
                    line = which * 9 + f * 3
                    north = g_ref[pl.ds(n * 8 * MSG_C + line + s, 8, stride=MSG_C), :]
                    south = g_ref[pl.ds((16 + n * 8) * MSG_C + line + 2 - s, 8, stride=MSG_C), :]
                    first = (which * 3 + f) * PLANE + (n * 24 + s * 8) * 8
                    even, odd = (north + south) * weight, (north - south) * weight
                    for k in range(8):
                        eo_ref[pl.ds(first + k, 8, stride=8), :] = odd if k % 2 else even

    quads = set_lines(q) // 32

    def body(quad, _):
        base = jnp.where(quad >= quads, 3 * PLANE, 0)

        def rows(group, sums):
            sums = list(sums)
            for row in range(16):
                first = (group * 16 + row) * 8
                fields = [eo_ref[pl.ds(pl.multiple_of(base + f * PLANE + first, 8), 8), :] for f in range(3)]
                for b in range(4):
                    plane = p_ref[pl.ds(pl.multiple_of((quad * 4 + b) * PLANE + first, 8), 8), :]
                    for f in range(3):
                        sums[b * 3 + f] = sums[b * 3 + f] + plane * fields[f]
            return tuple(sums)

        sums = lax.fori_loop(0, ROWS // 16, rows, (jnp.zeros((8, 128), F32),) * 12)
        for b in range(4):
            for f in range(3):
                a_ref[pl.ds(pl.multiple_of(f * LINES_PAD + (quad * 4 + b) * 8, 8), 8), :] = sums[b * 3 + f]
        return 0

    lax.fori_loop(0, QUADS, body, 0)


def update(q, stiff, damp, state_refs, a_ref, ns_refs, st_ref):
    for which in range(2):
        state_ref, ns_ref = state_refs[which], ns_refs[which]
        size = ns_ref.shape[2]
        start = pl.multiple_of(set_lines(q) if which else 0 * q, 32)
        member = lax.broadcasted_iota(jnp.int32, (MDEV, size), 0) % HALF
        wave = (member + HALF * (63 - q if which else q)).astype(F32)
        degree = wave + lanes((MDEV, size)).astype(F32)
        ratio = degree * (degree + 1.0) / (WAVES * (WAVES - 1.0))
        inside = degree <= WAVES - 1.0
        denominator = 1.0 + stiff * ratio
        damped = jnp.where(inside, 1.0 / (1.0 + damp * ratio * ratio), 0.0)

        def total(f):
            turned = jnp.transpose(a_ref[pl.ds(f * LINES_PAD + start, size), :])
            pieces = [turned[16 * n : 16 * n + 16] for n in range(GROUPS)]
            summed = ((pieces[0] + pieces[1]) + (pieces[2] + pieces[3])) + (
                (pieces[4] + pieces[5]) + (pieces[6] + pieces[7])
            )
            old = jnp.concatenate([state_ref[f * 2], state_ref[f * 2 + 1]], axis=0)
            return jnp.where(inside, old + summed, 0.0)

        def put(f, value):
            ns_ref[f * 2] = value[0:8]
            ns_ref[f * 2 + 1] = value[8:16]
            turned = jnp.transpose(jnp.concatenate([value] * GROUPS, axis=0))
            st_ref[pl.ds(f * LINES_PAD + start, size), :] = turned

        vorticity, divergence, height = total(0), total(1), total(2)
        put(0, vorticity * damped)
        put(1, (divergence + ratio * height) / denominator * damped)
        put(2, (height - stiff * divergence) / denominator * damped)


def synthesis(q, group, p_ref, st_ref, h_ref):
    sign = jnp.where(lax.broadcasted_iota(jnp.int32, (8, 128), 0) % 2 == 0, 1.0, -1.0)
    quads = set_lines(q) // 32
    n, s = group // 3, group % 3
    for which, (begin, end) in enumerate(((0, quads), (quads, QUADS))):

        def degrees(quad, sums):
            sums = list(sums)
            for b in range(4):
                block = quad * 4 + b
                values = [st_ref[pl.ds(pl.multiple_of(f * LINES_PAD + block * 8, 8), 8), :] for f in range(3)]
                for row in range(8):
                    first = block * PLANE + group * 64 + row * 8
                    plane = p_ref[pl.ds(pl.multiple_of(first, 8), 8), :]
                    for f in range(3):
                        sums[f * 8 + row] = sums[f * 8 + row] + plane * values[f]
            return tuple(sums)

        sums = lax.fori_loop(begin, end, degrees, (jnp.zeros((8, 128), F32),) * 24)
        for f in range(3):
            parts = list(sums[f * 8 : f * 8 + 8])
            line = which * 9 + f * 3
            h_ref[pl.ds(n * 8 * MSG_C + line + s, 8, stride=MSG_C), :] = fold_rows(parts)
            parts = [part * sign for part in parts]
            h_ref[pl.ds((16 + n * 8) * MSG_C + line + 2 - s, 8, stride=MSG_C), :] = fold_rows(parts)


def inverse_operand(group, south, cp_ref, y_ref):
    for column in range(2):
        first = (group * 8 + column * 4) * SLOT_C
        items = swap_groups([cp_ref[pl.ds(first + g // 2 * SLOT_C + g % 2 * 9, 16), :] for g in range(GROUPS)])
        for a in range(GROUPS):
            row = mirrored(south, a)
            high, low = split(items[a])
            y_ref[block_rows(row, 16), block_rows(group * 2 + column, 128)] = high
            y_ref[block_rows(row + GROUPS, 16), block_rows(group * 2 + column, 128)] = low


def inverse_blocks(q, y_ref, high_ref, low_ref, block_ref, w_ref, send):
    lane = lanes((16, 128))

    def body(step, _):
        block = (step + q % 4 * 2) % 8
        columns = block_rows(block, 256)
        block_ref[...] = product(y_ref, high_ref, low_ref, slice(None), columns)
        for index in range(4):
            half, par = divmod(index, 2)
            owner = block * 4 + index
            columns = [None] * 3
            for a in range(GROUPS):
                first, offset = divmod(BLK * a, 128)
                piece = block_ref[a * 16 : (a + 1) * 16, half * 128 : (half + 1) * 128]
                shift = (offset - 64 * par) % 128
                piece = pltpu.roll(piece, shift, 1) if shift else piece
                if columns[first] is None:
                    columns[first] = piece
                else:
                    columns[first] = jnp.where(lane >= offset, piece, columns[first])
                if offset + BLK > 128:
                    columns[first + 1] = piece
            for c in range(3):
                w_ref[pl.ds(owner * MSG_G + c, 9, stride=3), :] = columns[c][0:9]
            send(owner)
        return 0

    lax.fori_loop(0, 8, body, 0)


def slot_of(source):
    return jnp.where(source < 16, source, 47 - source)


def kernel(
    t_any,
    state_any,
    start_any,
    stiff_any,
    damp_any,
    fh_any,
    fl_any,
    ih_any,
    il_any,
    ns_ref,
    o_ref,
    t_ref,
    low_state_ref,
    high_state_ref,
    low_new_ref,
    high_new_ref,
    start_ref,
    stiff_ref,
    damp_ref,
    fh_ref,
    fl_ref,
    ih_ref,
    il_ref,
    sb_ref,
    r_ref,
    x_ref,
    fsum_ref,
    block_ref,
    m_ref,
    g_ref,
    eo_ref,
    slope_ref,
    lag_ref,
    trig_ref,
    p_ref,
    a_ref,
    st_ref,
    h_ref,
    cp_ref,
    y_ref,
    w_ref,
    load_sem,
    send_sem,
    recv_sem,
    ready_sem,
):
    q = lax.axis_index("lon")
    p = lax.axis_index("lat")
    here = place_of(q)
    south = p >= LAT // 2
    owned, half = q // 2, q % 2
    my_source = slot_of(p * 2 + half)
    back_mode = (q // 4 + 16 - p // 2 - p % 2 * 4) % 8 * 2 + q % 4 // 2
    back_half = q % 2
    back_slot = slot_of(p * 2 + back_half)

    ns_ref[...] = jnp.zeros_like(ns_ref)
    barrier = pltpu.get_barrier_semaphore()

    def greet_lon(n, _):
        pl.semaphore_signal(barrier, inc=1, device_id=((q + n) % LON, p), device_id_type=MESH)
        return 0

    def greet_lat(n, _):
        pl.semaphore_signal(barrier, inc=1, device_id=(q, (p + n) % LAT), device_id_type=MESH)
        return 0

    lax.fori_loop(1, LON, greet_lon, 0)
    lax.fori_loop(1, LAT, greet_lat, 0)

    loads = [
        pltpu.make_async_copy(source, target, load_sem.at[index])
        for index, (source, target) in enumerate(
            (
                (t_any, t_ref),
                (start_any, start_ref),
                (fh_any, fh_ref),
                (fl_any, fl_ref),
                (stiff_any, stiff_ref),
                (damp_any, damp_ref),
                (ih_any, ih_ref),
                (il_any, il_ref),
            )
        )
    ]
    for load in loads:
        load.start()

    def copy(source, target, stage, group, peer):
        return pltpu.make_async_remote_copy(
            src_ref=source,
            dst_ref=target,
            send_sem=send_sem.at[stage],
            recv_sem=recv_sem.at[4 if stage in (4, 5) else 5 if stage > 5 else stage, group],
            device_id=peer,
            device_id_type=MESH,
        )

    def copy_or_keep(source, target, stage, group, peer):
        lon, lat = peer
        own = jnp.logical_and(lon == q, lat == p)

        @pl.when(jnp.logical_not(own))
        def _():
            copy(source, target, stage, group, peer).start()

        @pl.when(own)
        def _():
            pltpu.make_async_copy(source, target, recv_sem.at[stage, group]).start()

    def wait(ref, first, rows, sem):
        part = ref.at[pl.ds(first, rows)]
        pltpu.make_async_copy(part, part, sem).wait()

    def send_grid(n, _):
        place = (here // 8 + n // 8) % 4 * 8 + (here + n) % 8
        lon = lon_of(place)
        copy(sb_ref.at[pl.ds(lon * MSG_G, MSG_G)], r_ref.at[pl.ds(here * SLOT_G, MSG_G)], 0, here // 8, (lon, p)).start()
        return 0

    def send_waves(place):
        copy_or_keep(
            m_ref.at[pl.ds(place * MSG_C, MSG_C)],
            g_ref.at[pl.ds(my_source * MSG_C, MSG_C)],
            1,
            0,
            (lon_of(place), owned),
        )

    def send_rows(n, part):
        index = (here // 8 * 4 + n) % 16
        slot = index // 8 * 16 + part * 8 + index % 8
        source = slot_of(slot)
        lat = source // 2
        lon = (p // 2 + lat // 2 + lat % 2 * 4) % 8 * 4 + p % 2 * 2 + source % 2
        copy_or_keep(
            h_ref.at[pl.ds(slot * MSG_C, MSG_C)],
            cp_ref.at[pl.ds(here * SLOT_C, MSG_C)],
            2,
            here // 8,
            (lon, lat),
        )
        return part

    def send_back(place):
        for f in range(3):
            copy_or_keep(
                w_ref.at[pl.ds(place * MSG_G + f * 9, 9)],
                o_ref.at[pl.ds((f * MODES + back_mode) * 18 + back_half * 9, 9)],
                3,
                0,
                (lon_of(place), p),
            )

    def state_copies(index):
        rows = pl.ds(index * HALF, HALF)
        low = (
            (2 * q + index, p),
            lambda: copy(state_any.at[:, rows, :], low_state_ref, 4 + index, 0, (2 * q + index, p)),
            lambda: pltpu.make_async_copy(state_any.at[:, rows, :], low_state_ref, recv_sem.at[4, 0]),
        )
        worker = 63 - 2 * q - index
        high = (
            (worker, p),
            lambda: copy(state_any.at[:, rows, 0:256], high_state_ref, 4 + index, 1, (worker, p)),
            lambda: pltpu.make_async_copy(state_any.at[:, rows, 0:256], high_state_ref, recv_sem.at[4, 1]),
        )
        return low, high

    def new_copies():
        low_rows = pl.ds(q % 2 * HALF, HALF)
        high_rows = pl.ds((63 - q) % 2 * HALF, HALF)
        owner = (63 - q) // 2
        low = (
            q // 2,
            lambda: copy(low_new_ref, ns_ref.at[:, low_rows, :], 6, 0, (q // 2, p)),
            lambda: pltpu.make_async_copy(low_new_ref, ns_ref.at[:, low_rows, :], recv_sem.at[5, 0]),
        )
        high = (
            owner,
            lambda: copy(high_new_ref, ns_ref.at[:, high_rows, 0:256], 7, 0, (owner, p)),
            lambda: pltpu.make_async_copy(high_new_ref, ns_ref.at[:, high_rows, 0:256], recv_sem.at[5, 0]),
        )
        return low, high

    def each_state_copy(act):
        for index in range(2):
            low, high = state_copies(index)
            for (peer, remote, local), mine in ((low, q < 16), (high, q >= 16)):

                @pl.when(jnp.logical_and(mine, peer[0] != q))
                def _():
                    act(remote, False)

                @pl.when(jnp.logical_and(mine, peer[0] == q))
                def _():
                    act(local, True)

    def each_new_copy(act):
        for peer, remote, local in new_copies():

            @pl.when(peer != q)
            def _():
                act(remote, False)

            @pl.when(peer == q)
            def _():
                act(local, True)

    def begin(item, own):
        item().start()

    def sent(item, own):
        if not own:
            item().wait_send()

    loads[0].wait()
    gather_rows(t_ref, sb_ref)
    pl.semaphore_wait(barrier, LON - 1 + LAT - 1)
    lax.fori_loop(1, LON, send_grid, 0)
    pltpu.make_async_copy(
        sb_ref.at[pl.ds(q * MSG_G, MSG_G)], r_ref.at[pl.ds(here * SLOT_G, MSG_G)], recv_sem.at[0, here // 8]
    ).start()

    def tell(n, _):
        pl.semaphore_signal(ready_sem, inc=1, device_id=(q, (p + n) % LAT), device_id_type=MESH)
        return 0

    lax.fori_loop(1, LAT, tell, 0)

    loads[1].wait()
    legendre_tables(q, start_ref, slope_ref, lag_ref, trig_ref, p_ref)
    each_state_copy(begin)
    fsum_ref[...] = jnp.zeros_like(fsum_ref)
    loads[2].wait()
    loads[3].wait()

    def grid_group(step):
        group = (here // 8 + 4 - step) % 4
        wait(r_ref, group * 8 * SLOT_G, 8 * MSG_G, recv_sem.at[0, group])
        forward_operand(group, r_ref, x_ref)
        return group

    def forward_step(step, _):
        add_products(grid_group(step), x_ref, fh_ref, fl_ref, fsum_ref)
        return 0

    lax.fori_loop(0, 3, forward_step, 0)
    group = grid_group(3)
    pl.semaphore_wait(ready_sem, LAT - 1)
    forward_blocks(q, south, group, x_ref, fh_ref, fl_ref, fsum_ref, block_ref, m_ref, send_waves)
    for load in loads[4:]:
        load.wait()
    wait(sb_ref, 0, (LON - 1) * MSG_G, send_sem.at[0])
    wait(g_ref, 0, 32 * MSG_C, recv_sem.at[1, 0])
    analysis(q, g_ref, trig_ref, eo_ref, p_ref, a_ref)
    each_state_copy(sent)
    pltpu.make_async_copy(low_state_ref, low_state_ref, recv_sem.at[4, 0]).wait()
    pltpu.make_async_copy(high_state_ref, high_state_ref, recv_sem.at[4, 1]).wait()
    update(
        q,
        stiff_ref[p],
        damp_ref[p],
        (low_state_ref, high_state_ref),
        a_ref,
        (low_new_ref, high_new_ref),
        st_ref,
    )
    each_new_copy(begin)

    def synthesize(part, _):
        lax.fori_loop(0, 3, lambda s, _: (synthesis(q, part * 3 + s, p_ref, st_ref, h_ref), 0)[1], 0)
        lax.fori_loop(0, 16, send_rows, part)
        return 0

    lax.fori_loop(0, 2, synthesize, 0)

    def wait_sent(ref, own, stage):
        @pl.when(own)
        def _():
            wait(ref, 0, 31 * MSG_C, send_sem.at[stage])

        @pl.when(jnp.logical_not(own))
        def _():
            wait(ref, 0, 32 * MSG_C, send_sem.at[stage])

    wait_sent(m_ref, owned == p, 1)

    def waves_group(step, _):
        group = (back_slot // 8 + 4 - step) % 4
        wait(cp_ref, group * 8 * SLOT_C, 8 * MSG_C, recv_sem.at[2, group])
        inverse_operand(group, south, cp_ref, y_ref)
        return 0

    lax.fori_loop(0, 4, waves_group, 0)
    inverse_blocks(q, y_ref, ih_ref, il_ref, block_ref, w_ref, send_back)
    wait_sent(h_ref, back_mode == p, 2)
    each_new_copy(sent)

    @pl.when(q < 16)
    def _():
        pltpu.make_async_copy(ns_ref, ns_ref, recv_sem.at[5, 0]).wait()

    @pl.when(q >= 16)
    def _():
        part = ns_ref.at[:, :, 0:256]
        pltpu.make_async_copy(part, part, recv_sem.at[5, 0]).wait()

    wait(o_ref, 0, LON * MSG_G, recv_sem.at[3, 0])
    wait(w_ref, 0, (LON - 1) * MSG_G, send_sem.at[3])


def body(tendency, state, stiffness, damping):
    rows = LON * MSG_G
    vmem = pl.BlockSpec(memory_space=pltpu.VMEM)
    anywhere = pl.BlockSpec(memory_space=pl.ANY)
    shapes = (jax.ShapeDtypeStruct((FR, MDEV, WAVES), F32), jax.ShapeDtypeStruct((rows, 128), F32))
    new_state, new_fields = pl.pallas_call(
        kernel,
        out_shape=shapes,
        in_specs=[anywhere] * 9,
        out_specs=(vmem, vmem),
        scratch_shapes=[
            pltpu.VMEM((rows, 128), F32),
            pltpu.VMEM((FR, HALF, WAVES), F32),
            pltpu.VMEM((FR, HALF, 256), F32),
            pltpu.VMEM((FR, HALF, WAVES), F32),
            pltpu.VMEM((FR, HALF, 256), F32),
            pltpu.VMEM((64, 128), F32),
            pltpu.SMEM((MODES,), F32),
            pltpu.SMEM((MODES,), F32),
            pltpu.VMEM((64 * LON, 2 * WAVES), BF16),
            pltpu.VMEM((64 * LON, 2 * WAVES), BF16),
            pltpu.VMEM((2 * WAVES, 64 * LON), BF16),
            pltpu.VMEM((2 * WAVES, 64 * LON), BF16),
            pltpu.VMEM((rows, 128), F32),
            pltpu.VMEM((LON * SLOT_G, 128), F32),
            pltpu.VMEM((256, 512), BF16),
            pltpu.VMEM((128, 2 * WAVES), F32),
            pltpu.VMEM((128, 256), F32),
            pltpu.VMEM((32 * MSG_C, 128), F32),
            pltpu.VMEM((32 * MSG_C, 128), F32),
            pltpu.VMEM((FR * PLANE, 128), F32),
            pltpu.VMEM((LINES, 128), F32),
            pltpu.VMEM((LINES, 128), F32),
            pltpu.VMEM((ROWS, 128), F32),
            pltpu.VMEM((LINES // 8 * PLANE, 128), F32),
            pltpu.VMEM((3 * LINES_PAD, 128), F32),
            pltpu.VMEM((3 * LINES_PAD, 128), F32),
            pltpu.VMEM((32 * MSG_C, 128), F32),
            pltpu.VMEM((32 * SLOT_C, 128), F32),
            pltpu.VMEM((256, 2 * WAVES), BF16),
            pltpu.VMEM((rows, 128), F32),
            pltpu.SemaphoreType.DMA((8,)),
            pltpu.SemaphoreType.DMA((8,)),
            pltpu.SemaphoreType.DMA((6, 4)),
            pltpu.SemaphoreType.REGULAR,
        ],
        compiler_params=pltpu.CompilerParams(
            collective_id=0, has_side_effects=True, vmem_limit_bytes=63 * 2**20
        ),
        name="spectral_step",
    )(
        tendency.reshape(rows, 128),
        state.reshape(FR, MDEV, WAVES),
        jnp.asarray(start_constants()),
        stiffness,
        damping,
        *[jnp.asarray(table) for table in fourier_constants()],
    )
    return new_state.reshape(state.shape), new_fields.reshape(tendency.shape)


def solution(mesh):
    return jax.shard_map(
        body,
        mesh=mesh,
        in_specs=(P(None, None, "lat", "lon", None), P("lat", None, None, "lon", None), P(), P()),
        out_specs=(P("lat", None, None, "lon", None), P(None, None, "lat", "lon", None)),
        check_vma=False,
    )
```

```python
import functools
import math

import jax
import jax.numpy as jnp
import ml_dtypes
import numpy as np
from jax import lax
from jax.experimental import pallas as pl
from jax.experimental.pallas import tpu as pltpu
from jax.sharding import PartitionSpec as P

NLAT = 768
NLON = 1536
WAVES = 512
MODES = 16
LON = 32
LAT = 16
BLK = 48
MDEV = 16
GROUPS = 8
MSG_G = 27
SLOT_G = 48
SLOT_C = 32
MSG_C = 18
FR = 6
HALF = 8
QUADS = 17
LINES = QUADS * 32
LINES_PAD = 768
PLANE = 384
ROWS = 48
MESH = pl.DeviceIdType.MESH
F32 = jnp.float32
BF16 = jnp.bfloat16


def split_constant(table):
    high = table.astype(np.float32).astype(ml_dtypes.bfloat16)
    low = (table - high.astype(np.float64)).astype(np.float32).astype(ml_dtypes.bfloat16)
    return high, low


def lon_of(place):
    return (place % 8) * 4 + place // 8


def place_of(lon):
    return (lon % 4) * 8 + lon // 4


@functools.lru_cache(maxsize=None)
def fourier_constants():
    slot = np.arange(LON * 64)
    block, inner = lon_of(slot // 64), slot % 64
    lon = block * BLK + inner
    valid = (inner < BLK)[:, None]
    wave = np.arange(WAVES)
    angle = 2.0 * np.pi / NLON * ((lon[:, None] * wave[None, :]) % NLON)
    owners = lon_of(np.arange(LON))
    sets = np.stack([owners, 63 - owners], axis=1)
    cosine = np.where(valid, np.cos(angle), 0.0).reshape(-1, 64, HALF)[:, sets]
    sine = np.where(valid, np.sin(angle), 0.0).reshape(-1, 64, HALF)[:, sets]
    basis = np.stack([cosine, -sine], axis=3).reshape(LON * 64, 2 * WAVES)
    factor = np.where(wave == 0, 1.0, 2.0).reshape(64, HALF)[sets] / WAVES
    factor = np.broadcast_to(factor[:, :, None, :], (LON, 2, 2, HALF)).reshape(2 * WAVES, 1)
    return split_constant(basis / NLON) + split_constant(factor * basis.T)


@functools.lru_cache(maxsize=None)
def start_constants():
    start = [
        (0.5 * math.log(m + 0.5) + 0.5 * math.lgamma(m + 0.5) - 0.5 * math.lgamma(m + 1.0) - 0.25 * math.log(math.pi))
        / math.log(2.0)
        for m in range(WAVES)
    ]
    return np.tile(np.array(start, np.float32).reshape(64, HALF), (1, 2 * GROUPS))


def lanes(shape):
    return lax.broadcasted_iota(jnp.int32, shape, len(shape) - 1)


def swap_groups(items):
    group = lanes(items[0].shape) // 16
    items = list(items)
    for step in (4, 2, 1):
        keep = (group & step) == 0
        for low in range(GROUPS):
            if low & step:
                continue
            high = low + step
            x, y = items[low], items[high]
            items[low] = jnp.where(keep, x, pltpu.roll(y, 16 * step, 1))
            items[high] = jnp.where(keep, pltpu.roll(x, 128 - 16 * step, 1), y)
    return items


def fold_rows(parts):
    row = lax.broadcasted_iota(jnp.int32, (8, 128), 0)
    upper = row < 4
    four = []
    for index in range(4):
        x, y = parts[index], parts[index + 4]
        four.append(jnp.where(upper, x, y) + pltpu.roll(jnp.where(upper, y, x), 4, 0))
    for step in (2, 1):
        keep = (row & step) == 0
        four = [
            jnp.where(
                keep,
                four[index] + pltpu.roll(four[index], 8 - step, 0),
                four[index + step] + pltpu.roll(four[index + step], step, 0),
            )
            for index in range(step)
        ]
    return four[0]


def split(x):
    high = x.astype(BF16)
    return high, (x - high.astype(F32)).astype(BF16)


def mirrored(south, a):
    return jnp.where(south, GROUPS - 1 - a, a)


def block_rows(index, size):
    return pl.ds(pl.multiple_of(index * size, size), size)


def gather_rows(t_ref, sb_ref):
    def body(d, _):
        c, h = d // 2, d % 2
        for f in range(3):
            sb_ref[pl.ds(d * MSG_G + f * 9, 9), :] = t_ref[pl.ds((f * MODES + c) * 18 + h * 9, 9), :]
        return 0

    lax.fori_loop(0, LON, body, 0)


def set_lines(q):
    return (64 - q + 3) // 4 * 32


def legendre_tables(q, start_ref, slope_ref, lag_ref, trig_ref, p_ref):
    member = lanes((1, 128)) % HALF
    waves = ((member + HALF * q).astype(F32), (member + HALF * (63 - q)).astype(F32))
    split_line = set_lines(q)

    def coefficients(block, _):
        line = lax.broadcasted_iota(jnp.int32, (32, 128), 0) + block * 32
        second = line >= split_line
        offsets = jnp.where(second, line - split_line, line).astype(F32)
        wave = jnp.where(second, waves[1], waves[0])
        degree = wave + offsets
        spacing = jnp.maximum(offsets * (2.0 * wave + offsets), 1.0)
        slope = jnp.sqrt(jnp.maximum(4.0 * degree * degree - 1.0, 0.0) / spacing)
        numerator = (2.0 * degree + 1.0) * (offsets - 1.0) * (degree - 1.0 + wave)
        lag = jnp.sqrt(jnp.maximum(numerator, 0.0) / (jnp.maximum(2.0 * degree - 3.0, 1.0) * spacing))
        first = offsets < 0.5
        slope_ref[block_rows(block, 32), :] = jnp.where(first, 0.0, slope)
        lag_ref[block_rows(block, 32), :] = jnp.where(first, 1.0, lag)
        return 0

    lax.fori_loop(0, QUADS, coefficients, 0)
    row = lax.broadcasted_iota(jnp.int32, (ROWS, 128), 0)
    colat = ((row // 24) * 8 + row % 8) * 24 + (row // 8 % 3) * 8 + lanes((ROWS, 128)) // MDEV
    theta = math.pi * (colat.astype(F32) + 0.5) / NLAT
    mu = jnp.cos(theta)
    sine = jnp.sin(theta)
    trig_ref[...] = sine * (WAVES * math.pi / NLAT)
    log_sine = jnp.log(sine) * (1.0 / math.log(2.0))
    coarse = jnp.floor(log_sine * 1024.0) * (1.0 / 1024.0)
    blocks = split_line // 8

    for which, (begin, end) in enumerate(((0, blocks), (blocks, LINES // 8))):
        wave = waves[which]
        whole = wave * coarse
        exponent = jnp.floor(whole)
        start = start_ref[pl.ds(63 - q if which else q, 1), :]
        lower = -jnp.exp2((whole - exponent) + wave * (log_sine - coarse) + start)

        def body(block, carry, begin=begin, wave=wave):
            upper, lower, exponent = carry
            growth = jnp.exp2(jnp.maximum(exponent, -140.0))
            for offset in range(8):
                line = block * 8 + offset
                moved = (slope_ref[pl.ds(line, 1), :] * mu) * upper - lag_ref[pl.ds(line, 1), :] * lower
                upper, lower = moved, upper
                k = line - begin * 8
                inside = wave + k.astype(F32) <= WAVES - 1.0
                p_ref[pl.ds(block * PLANE + offset, ROWS, stride=8), :] = jnp.where(inside, upper * growth, 0.0)
            big = jnp.maximum(jnp.abs(upper), jnp.abs(lower)) > 2.0**32
            scale = jnp.where(big, 2.0**-32, 1.0)
            return upper * scale, lower * scale, exponent + jnp.where(big, 32.0, 0.0)

        lax.fori_loop(begin, end, body, (jnp.zeros_like(lower), lower, exponent))


def forward_operand(group, r_ref, x_ref):
    lane = lanes((16, 128))

    def body(pair, _):
        first_row = (group * 8 + 2 * pair) * SLOT_G
        columns = [[r_ref[pl.ds(first_row + par * SLOT_G + c, 16, stride=3), :] for c in range(3)] for par in range(2)]
        for a in range(GROUPS):
            first, offset = divmod(BLK * a, 128)
            pieces = []
            for par in range(2):
                source = columns[par][first]
                if offset + BLK > 128:
                    source = jnp.where(lane >= offset, source, columns[par][first + 1])
                shift = (64 * par - offset) % 128
                pieces.append(pltpu.roll(source, shift, 1) if shift else source)
            high, low = split(jnp.where(lane < 64, pieces[0], pieces[1]))
            x_ref[a * 16 : (a + 1) * 16, block_rows(pair, 128)] = high
            x_ref[128 + a * 16 : 128 + (a + 1) * 16, block_rows(pair, 128)] = low
        return 0

    lax.fori_loop(0, 4, body, 0)


def product(x_ref, high_ref, low_ref, rows, columns):
    both = jnp.dot(x_ref[...], high_ref[rows, columns], preferred_element_type=F32)
    rest = jnp.dot(x_ref[0:128, :], low_ref[rows, columns], preferred_element_type=F32)
    return both[0:128] + both[128:256] + rest


def add_products(group, x_ref, high_ref, low_ref, sum_ref):
    rows = block_rows(group, x_ref.shape[1])

    def body(block, _):
        columns = block_rows(block, 256)
        sum_ref[:, columns] += product(x_ref, high_ref, low_ref, rows, columns)
        return 0

    lax.fori_loop(0, sum_ref.shape[1] // 256, body, 0)


def forward_blocks(q, south, group, x_ref, high_ref, low_ref, sum_ref, block_ref, m_ref, send):
    rows = block_rows(group, x_ref.shape[1])

    def body(step, _):
        block = (q + turn(step)) % 4
        columns = block_rows(block, 256)
        block_ref[...] = sum_ref[:, columns] + product(x_ref, high_ref, low_ref, rows, columns)
        for order in range(2):
            half = jnp.where(q // 4 < 4, 1 - order, order)
            items = swap_groups(
                [block_ref[block_rows(mirrored(south, a), 16), block_rows(half, 128)] for a in range(GROUPS)]
            )
            for group in range(GROUPS):
                owner = block * 8 + half * 4 + group // 2
                m_ref[pl.ds(owner * MSG_C + (group % 2) * 9, 9), :] = items[group][0:9]
            for index in range(4):
                send(block * 8 + half * 4 + index)
        return 0

    lax.fori_loop(0, 4, body, 0)


def analysis(q, g_ref, trig_ref, eo_ref, p_ref, a_ref):
    for n in range(2):
        for s in range(3):
            weight = trig_ref[n * 24 + s * 8 : n * 24 + s * 8 + 8, :]
            for which in range(2):
                for f in range(3):
                    line = which * 9 + f * 3
                    north = g_ref[pl.ds(n * 8 * MSG_C + line + s, 8, stride=MSG_C), :]
                    south = g_ref[pl.ds((16 + n * 8) * MSG_C + line + 2 - s, 8, stride=MSG_C), :]
                    first = (which * 3 + f) * PLANE + (n * 24 + s * 8) * 8
                    even, odd = (north + south) * weight, (north - south) * weight
                    for k in range(8):
                        eo_ref[pl.ds(first + k, 8, stride=8), :] = odd if k % 2 else even

    quads = set_lines(q) // 32

    def body(quad, _):
        base = jnp.where(quad >= quads, 3 * PLANE, 0)

        def rows(group, sums):
            sums = list(sums)
            for row in range(16):
                first = (group * 16 + row) * 8
                fields = [eo_ref[pl.ds(pl.multiple_of(base + f * PLANE + first, 8), 8), :] for f in range(3)]
                for b in range(4):
                    plane = p_ref[pl.ds(pl.multiple_of((quad * 4 + b) * PLANE + first, 8), 8), :]
                    for f in range(3):
                        sums[b * 3 + f] = sums[b * 3 + f] + plane * fields[f]
            return tuple(sums)

        sums = lax.fori_loop(0, ROWS // 16, rows, (jnp.zeros((8, 128), F32),) * 12)
        for b in range(4):
            for f in range(3):
                a_ref[pl.ds(pl.multiple_of(f * LINES_PAD + (quad * 4 + b) * 8, 8), 8), :] = sums[b * 3 + f]
        return 0

    lax.fori_loop(0, QUADS, body, 0)


def update(q, stiff, damp, state_refs, a_ref, ns_refs, st_ref):
    for which in range(2):
        state_ref, ns_ref = state_refs[which], ns_refs[which]
        size = ns_ref.shape[2]
        start = pl.multiple_of(set_lines(q) if which else 0 * q, 32)
        member = lax.broadcasted_iota(jnp.int32, (MDEV, size), 0) % HALF
        wave = (member + HALF * (63 - q if which else q)).astype(F32)
        degree = wave + lanes((MDEV, size)).astype(F32)
        ratio = degree * (degree + 1.0) / (WAVES * (WAVES - 1.0))
        inside = degree <= WAVES - 1.0
        denominator = 1.0 + stiff * ratio
        damped = jnp.where(inside, 1.0 / (1.0 + damp * ratio * ratio), 0.0)

        def total(f):
            turned = jnp.transpose(a_ref[pl.ds(f * LINES_PAD + start, size), :])
            pieces = [turned[16 * n : 16 * n + 16] for n in range(GROUPS)]
            summed = ((pieces[0] + pieces[1]) + (pieces[2] + pieces[3])) + (
                (pieces[4] + pieces[5]) + (pieces[6] + pieces[7])
            )
            old = jnp.concatenate([state_ref[f * 2], state_ref[f * 2 + 1]], axis=0)
            return jnp.where(inside, old + summed, 0.0)

        def put(f, value):
            ns_ref[f * 2] = value[0:8]
            ns_ref[f * 2 + 1] = value[8:16]
            turned = jnp.transpose(jnp.concatenate([value] * GROUPS, axis=0))
            st_ref[pl.ds(f * LINES_PAD + start, size), :] = turned

        vorticity, divergence, height = total(0), total(1), total(2)
        put(0, vorticity * damped)
        put(1, (divergence + ratio * height) / denominator * damped)
        put(2, (height - stiff * divergence) / denominator * damped)


def synthesis(q, group, p_ref, st_ref, h_ref):
    sign = jnp.where(lax.broadcasted_iota(jnp.int32, (8, 128), 0) % 2 == 0, 1.0, -1.0)
    quads = set_lines(q) // 32
    n, s = group // 3, group % 3
    for which, (begin, end) in enumerate(((0, quads), (quads, QUADS))):

        def degrees(quad, sums):
            sums = list(sums)
            for b in range(4):
                block = quad * 4 + b
                values = [st_ref[pl.ds(pl.multiple_of(f * LINES_PAD + block * 8, 8), 8), :] for f in range(3)]
                for row in range(8):
                    first = block * PLANE + group * 64 + row * 8
                    plane = p_ref[pl.ds(pl.multiple_of(first, 8), 8), :]
                    for f in range(3):
                        sums[f * 8 + row] = sums[f * 8 + row] + plane * values[f]
            return tuple(sums)

        sums = lax.fori_loop(begin, end, degrees, (jnp.zeros((8, 128), F32),) * 24)
        for f in range(3):
            parts = list(sums[f * 8 : f * 8 + 8])
            line = which * 9 + f * 3
            h_ref[pl.ds(n * 8 * MSG_C + line + s, 8, stride=MSG_C), :] = fold_rows(parts)
            parts = [part * sign for part in parts]
            h_ref[pl.ds((16 + n * 8) * MSG_C + line + 2 - s, 8, stride=MSG_C), :] = fold_rows(parts)


def inverse_operand(group, south, cp_ref, y_ref):
    for column in range(2):
        first = (group * 8 + column * 4) * SLOT_C
        items = swap_groups([cp_ref[pl.ds(first + g // 2 * SLOT_C + g % 2 * 9, 16), :] for g in range(GROUPS)])
        for a in range(GROUPS):
            row = mirrored(south, a)
            high, low = split(items[a])
            y_ref[block_rows(row, 16), block_rows(group * 2 + column, 128)] = high
            y_ref[block_rows(row + GROUPS, 16), block_rows(group * 2 + column, 128)] = low


def inverse_blocks(q, y_ref, high_ref, low_ref, block_ref, w_ref, send):
    lane = lanes((16, 128))

    def body(step, _):
        block = (q + turn(step // 2)) % 4 * 2 + jnp.where(q // 4 < 4, 1 - step % 2, step % 2)
        columns = block_rows(block, 256)
        block_ref[...] = product(y_ref, high_ref, low_ref, slice(None), columns)
        for index in range(4):
            half, par = divmod(index, 2)
            owner = block * 4 + index
            columns = [None] * 3
            for a in range(GROUPS):
                first, offset = divmod(BLK * a, 128)
                piece = block_ref[a * 16 : (a + 1) * 16, half * 128 : (half + 1) * 128]
                shift = (offset - 64 * par) % 128
                piece = pltpu.roll(piece, shift, 1) if shift else piece
                if columns[first] is None:
                    columns[first] = piece
                else:
                    columns[first] = jnp.where(lane >= offset, piece, columns[first])
                if offset + BLK > 128:
                    columns[first + 1] = piece
            for c in range(3):
                w_ref[pl.ds(owner * MSG_G + c, 9, stride=3), :] = columns[c][0:9]
            send(owner)
        return 0

    lax.fori_loop(0, 8, body, 0)


def far_first(y, n):
    return (y + jnp.where(n % 2 == 0, 4 - n // 2, 4 + (n + 1) // 2)) % 8


def turn(step):
    return jnp.where(step == 0, 2, jnp.where(step == 1, 1, jnp.where(step == 2, 3, 0)))


def slot_of(source):
    return jnp.where(source < 16, source, 47 - source)


def kernel(
    t_any,
    state_any,
    start_any,
    stiff_any,
    damp_any,
    fh_any,
    fl_any,
    ih_any,
    il_any,
    ns_ref,
    o_ref,
    t_ref,
    low_state_ref,
    high_state_ref,
    low_new_ref,
    high_new_ref,
    zero_ref,
    start_ref,
    stiff_ref,
    damp_ref,
    fh_ref,
    fl_ref,
    ih_ref,
    il_ref,
    sb_ref,
    r_ref,
    x_ref,
    fsum_ref,
    block_ref,
    m_ref,
    g_ref,
    eo_ref,
    slope_ref,
    lag_ref,
    trig_ref,
    p_ref,
    a_ref,
    st_ref,
    h_ref,
    cp_ref,
    y_ref,
    w_ref,
    load_sem,
    send_sem,
    recv_sem,
    ready_sem,
):
    q = lax.axis_index("lon")
    p = lax.axis_index("lat")
    here = place_of(q)
    south = p >= LAT // 2
    owned, half = q // 2, q % 2
    my_source = slot_of(p * 2 + half)
    back_mode = (q // 4 + 16 - p // 2 - p % 2 * 4) % 8 * 2 + q % 4 // 2
    back_half = q % 2
    back_slot = slot_of(p * 2 + back_half)

    zero_copy = pltpu.make_async_copy(zero_ref, ns_ref.at[:, :, 256:512], load_sem.at[8])

    @pl.when(q >= 16)
    def _():
        zero_ref[...] = jnp.zeros_like(zero_ref)
        zero_copy.start()

    barrier = pltpu.get_barrier_semaphore()

    def greet_lon(n, _):
        pl.semaphore_signal(barrier, inc=1, device_id=((q + n) % LON, p), device_id_type=MESH)
        return 0

    def greet_lat(n, _):
        pl.semaphore_signal(barrier, inc=1, device_id=(q, (p + n) % LAT), device_id_type=MESH)
        return 0

    lax.fori_loop(1, LON, greet_lon, 0)
    lax.fori_loop(1, LAT, greet_lat, 0)

    loads = [
        pltpu.make_async_copy(source, target, load_sem.at[index])
        for index, (source, target) in enumerate(
            (
                (t_any, t_ref),
                (start_any, start_ref),
                (fh_any, fh_ref),
                (fl_any, fl_ref),
                (stiff_any, stiff_ref),
                (damp_any, damp_ref),
                (ih_any, ih_ref),
                (il_any, il_ref),
            )
        )
    ]
    for load in loads:
        load.start()

    def copy(source, target, stage, group, peer):
        return pltpu.make_async_remote_copy(
            src_ref=source,
            dst_ref=target,
            send_sem=send_sem.at[stage],
            recv_sem=recv_sem.at[4 if stage in (4, 5) else 5 if stage > 5 else stage, group],
            device_id=peer,
            device_id_type=MESH,
        )

    def copy_or_keep(source, target, stage, group, peer):
        lon, lat = peer
        own = jnp.logical_and(lon == q, lat == p)

        @pl.when(jnp.logical_not(own))
        def _():
            copy(source, target, stage, group, peer).start()

        @pl.when(own)
        def _():
            pltpu.make_async_copy(source, target, recv_sem.at[stage, group]).start()

    def wait(ref, first, rows, sem):
        part = ref.at[pl.ds(first, rows)]
        pltpu.make_async_copy(part, part, sem).wait()

    def send_grid(n, _):
        place = (here // 8 + turn(n // 8)) % 4 * 8 + far_first(here % 8, n % 8)
        lon = lon_of(place)
        copy(sb_ref.at[pl.ds(lon * MSG_G, MSG_G)], r_ref.at[pl.ds(here * SLOT_G, MSG_G)], 0, here // 8, (lon, p)).start()
        return 0

    def send_waves(place):
        copy_or_keep(
            m_ref.at[pl.ds(place * MSG_C, MSG_C)],
            g_ref.at[pl.ds(my_source * MSG_C, MSG_C)],
            1,
            0,
            (lon_of(place), owned),
        )

    def send_rows(n, part):
        index = (here // 8 * 4 + n) % 16
        slot = index // 8 * 16 + part * 8 + index % 8
        source = slot_of(slot)
        lat = source // 2
        lon = (p // 2 + lat // 2 + lat % 2 * 4) % 8 * 4 + p % 2 * 2 + source % 2
        copy_or_keep(
            h_ref.at[pl.ds(slot * MSG_C, MSG_C)],
            cp_ref.at[pl.ds(here * SLOT_C, MSG_C)],
            2,
            here // 8,
            (lon, lat),
        )
        return part

    def send_back(place):
        for f in range(3):
            copy_or_keep(
                w_ref.at[pl.ds(place * MSG_G + f * 9, 9)],
                o_ref.at[pl.ds((f * MODES + back_mode) * 18 + back_half * 9, 9)],
                3,
                0,
                (lon_of(place), p),
            )

    def state_copies(index):
        rows = pl.ds(index * HALF, HALF)
        low = (
            (2 * q + index, p),
            lambda: copy(state_any.at[:, rows, :], low_state_ref, 4 + index, 0, (2 * q + index, p)),
            lambda: pltpu.make_async_copy(state_any.at[:, rows, :], low_state_ref, recv_sem.at[4, 0]),
        )
        worker = 63 - 2 * q - index
        high = (
            (worker, p),
            lambda: copy(state_any.at[:, rows, 0:256], high_state_ref, 4 + index, 1, (worker, p)),
            lambda: pltpu.make_async_copy(state_any.at[:, rows, 0:256], high_state_ref, recv_sem.at[4, 1]),
        )
        return low, high

    def new_copies():
        low_rows = pl.ds(q % 2 * HALF, HALF)
        high_rows = pl.ds((63 - q) % 2 * HALF, HALF)
        owner = (63 - q) // 2
        low = (
            q // 2,
            lambda: copy(low_new_ref, ns_ref.at[:, low_rows, :], 6, 0, (q // 2, p)),
            lambda: pltpu.make_async_copy(low_new_ref, ns_ref.at[:, low_rows, :], recv_sem.at[5, 0]),
        )
        high = (
            owner,
            lambda: copy(high_new_ref, ns_ref.at[:, high_rows, 0:256], 7, 0, (owner, p)),
            lambda: pltpu.make_async_copy(high_new_ref, ns_ref.at[:, high_rows, 0:256], recv_sem.at[5, 0]),
        )
        return low, high

    def each_state_copy(act):
        for index in range(2):
            low, high = state_copies(index)
            for (peer, remote, local), mine in ((low, q < 16), (high, q >= 16)):

                @pl.when(jnp.logical_and(mine, peer[0] != q))
                def _():
                    act(remote, False)

                @pl.when(jnp.logical_and(mine, peer[0] == q))
                def _():
                    act(local, True)

    def each_new_copy(act):
        for peer, remote, local in new_copies():

            @pl.when(peer != q)
            def _():
                act(remote, False)

            @pl.when(peer == q)
            def _():
                act(local, True)

    def begin(item, own):
        item().start()

    def sent(item, own):
        if not own:
            item().wait_send()

    loads[0].wait()
    gather_rows(t_ref, sb_ref)
    pl.semaphore_wait(barrier, LON - 1 + LAT - 1)
    lax.fori_loop(0, LON - 1, send_grid, 0)
    pltpu.make_async_copy(
        sb_ref.at[pl.ds(q * MSG_G, MSG_G)], r_ref.at[pl.ds(here * SLOT_G, MSG_G)], recv_sem.at[0, here // 8]
    ).start()

    def tell(n, _):
        pl.semaphore_signal(ready_sem, inc=1, device_id=(q, (p + n) % LAT), device_id_type=MESH)
        return 0

    lax.fori_loop(1, LAT, tell, 0)

    loads[1].wait()
    legendre_tables(q, start_ref, slope_ref, lag_ref, trig_ref, p_ref)
    each_state_copy(begin)
    fsum_ref[...] = jnp.zeros_like(fsum_ref)
    loads[2].wait()
    loads[3].wait()

    def grid_group(step):
        group = (here // 8 + 4 - turn(step)) % 4
        wait(r_ref, group * 8 * SLOT_G, 8 * MSG_G, recv_sem.at[0, group])
        forward_operand(group, r_ref, x_ref)
        return group

    def forward_step(step, _):
        add_products(grid_group(step), x_ref, fh_ref, fl_ref, fsum_ref)
        return 0

    lax.fori_loop(0, 3, forward_step, 0)
    group = grid_group(3)
    pl.semaphore_wait(ready_sem, LAT - 1)
    forward_blocks(q, south, group, x_ref, fh_ref, fl_ref, fsum_ref, block_ref, m_ref, send_waves)
    for load in loads[4:]:
        load.wait()
    wait(sb_ref, 0, (LON - 1) * MSG_G, send_sem.at[0])
    wait(g_ref, 0, 32 * MSG_C, recv_sem.at[1, 0])
    analysis(q, g_ref, trig_ref, eo_ref, p_ref, a_ref)
    each_state_copy(sent)
    pltpu.make_async_copy(low_state_ref, low_state_ref, recv_sem.at[4, 0]).wait()
    pltpu.make_async_copy(high_state_ref, high_state_ref, recv_sem.at[4, 1]).wait()
    update(
        q,
        stiff_ref[p],
        damp_ref[p],
        (low_state_ref, high_state_ref),
        a_ref,
        (low_new_ref, high_new_ref),
        st_ref,
    )
    each_new_copy(begin)

    def synthesize(part, _):
        lax.fori_loop(0, 3, lambda s, _: (synthesis(q, part * 3 + s, p_ref, st_ref, h_ref), 0)[1], 0)
        lax.fori_loop(0, 16, send_rows, part)
        return 0

    lax.fori_loop(0, 2, synthesize, 0)

    def wait_sent(ref, own, stage):
        @pl.when(own)
        def _():
            wait(ref, 0, 31 * MSG_C, send_sem.at[stage])

        @pl.when(jnp.logical_not(own))
        def _():
            wait(ref, 0, 32 * MSG_C, send_sem.at[stage])

    wait_sent(m_ref, owned == p, 1)

    def waves_group(step, _):
        group = (back_slot // 8 + 4 - step) % 4
        wait(cp_ref, group * 8 * SLOT_C, 8 * MSG_C, recv_sem.at[2, group])
        inverse_operand(group, south, cp_ref, y_ref)
        return 0

    lax.fori_loop(0, 4, waves_group, 0)
    inverse_blocks(q, y_ref, ih_ref, il_ref, block_ref, w_ref, send_back)
    wait_sent(h_ref, back_mode == p, 2)
    each_new_copy(sent)

    @pl.when(q < 16)
    def _():
        pltpu.make_async_copy(ns_ref, ns_ref, recv_sem.at[5, 0]).wait()

    @pl.when(q >= 16)
    def _():
        zero_copy.wait()
        part = ns_ref.at[:, :, 0:256]
        pltpu.make_async_copy(part, part, recv_sem.at[5, 0]).wait()

    wait(o_ref, 0, LON * MSG_G, recv_sem.at[3, 0])
    wait(w_ref, 0, (LON - 1) * MSG_G, send_sem.at[3])


def result_kernel(ns_ref, o_ref, new_state_any, new_fields_any, sem):
    copies = [
        pltpu.make_async_copy(source, target, sem.at[index])
        for index, (source, target) in enumerate(((ns_ref, new_state_any), (o_ref, new_fields_any)))
    ]
    for item in copies:
        item.start()
    for item in copies:
        item.wait()


def body(tendency, state, stiffness, damping):
    rows = LON * MSG_G
    vmem = pl.BlockSpec(memory_space=pltpu.VMEM)
    anywhere = pl.BlockSpec(memory_space=pl.ANY)
    shapes = (jax.ShapeDtypeStruct((FR, MDEV, WAVES), F32), jax.ShapeDtypeStruct((rows, 128), F32))
    new_state, new_fields = pl.pallas_call(
        kernel,
        out_shape=shapes,
        in_specs=[anywhere] * 9,
        out_specs=(vmem, vmem),
        scratch_shapes=[
            pltpu.VMEM((rows, 128), F32),
            pltpu.VMEM((FR, HALF, WAVES), F32),
            pltpu.VMEM((FR, HALF, 256), F32),
            pltpu.VMEM((FR, HALF, WAVES), F32),
            pltpu.VMEM((FR, HALF, 256), F32),
            pltpu.VMEM((FR, MDEV, 256), F32),
            pltpu.VMEM((64, 128), F32),
            pltpu.SMEM((MODES,), F32),
            pltpu.SMEM((MODES,), F32),
            pltpu.VMEM((64 * LON, 2 * WAVES), BF16),
            pltpu.VMEM((64 * LON, 2 * WAVES), BF16),
            pltpu.VMEM((2 * WAVES, 64 * LON), BF16),
            pltpu.VMEM((2 * WAVES, 64 * LON), BF16),
            pltpu.VMEM((rows, 128), F32),
            pltpu.VMEM((LON * SLOT_G, 128), F32),
            pltpu.VMEM((256, 512), BF16),
            pltpu.VMEM((128, 2 * WAVES), F32),
            pltpu.VMEM((128, 256), F32),
            pltpu.VMEM((32 * MSG_C, 128), F32),
            pltpu.VMEM((32 * MSG_C, 128), F32),
            pltpu.VMEM((FR * PLANE, 128), F32),
            pltpu.VMEM((LINES, 128), F32),
            pltpu.VMEM((LINES, 128), F32),
            pltpu.VMEM((ROWS, 128), F32),
            pltpu.VMEM((LINES // 8 * PLANE, 128), F32),
            pltpu.VMEM((3 * LINES_PAD, 128), F32),
            pltpu.VMEM((3 * LINES_PAD, 128), F32),
            pltpu.VMEM((32 * MSG_C, 128), F32),
            pltpu.VMEM((32 * SLOT_C, 128), F32),
            pltpu.VMEM((256, 2 * WAVES), BF16),
            pltpu.VMEM((rows, 128), F32),
            pltpu.SemaphoreType.DMA((9,)),
            pltpu.SemaphoreType.DMA((8,)),
            pltpu.SemaphoreType.DMA((6, 4)),
            pltpu.SemaphoreType.REGULAR,
        ],
        compiler_params=pltpu.CompilerParams(
            collective_id=0, has_side_effects=True, vmem_limit_bytes=60 * 2**20
        ),
        name="spectral_step",
    )(
        tendency.reshape(rows, 128),
        state.reshape(FR, MDEV, WAVES),
        jnp.asarray(start_constants()),
        stiffness,
        damping,
        *[jnp.asarray(table) for table in fourier_constants()],
    )
    new_state, new_fields = pl.pallas_call(
        result_kernel,
        out_shape=shapes,
        in_specs=[vmem, vmem],
        out_specs=(anywhere, anywhere),
        scratch_shapes=[pltpu.SemaphoreType.DMA((2,))],
        name="results",
    )(new_state, new_fields)
    return new_state.reshape(state.shape), new_fields.reshape(tendency.shape)


def solution(mesh):
    return jax.shard_map(
        body,
        mesh=mesh,
        in_specs=(P(None, None, "lat", "lon", None), P("lat", None, None, "lon", None), P(), P()),
        out_specs=(P("lat", None, None, "lon", None), P(None, None, "lat", "lon", None)),
        check_vma=False,
    )
```

```python
import functools
import math

import jax
import jax.numpy as jnp
import ml_dtypes
import numpy as np
from jax import lax
from jax.experimental import pallas as pl
from jax.experimental.pallas import tpu as pltpu
from jax.sharding import PartitionSpec as P

NLAT = 768
NLON = 1536
WAVES = 512
MODES = 16
LON = 32
LAT = 16
BLK = 48
MDEV = 16
GROUPS = 8
MSG_G = 27
SLOT_G = 48
SLOT_C = 32
MSG_C = 18
FR = 6
HALF = 8
QUADS = 17
LINES = QUADS * 32
LINES_PAD = 768
PLANE = 384
ROWS = 48
MESH = pl.DeviceIdType.MESH
F32 = jnp.float32
BF16 = jnp.bfloat16


def split_constant(table):
    high = table.astype(np.float32).astype(ml_dtypes.bfloat16)
    low = (table - high.astype(np.float64)).astype(np.float32).astype(ml_dtypes.bfloat16)
    return high, low


def lon_of(place):
    return (place % 8) * 4 + place // 8


def place_of(lon):
    return (lon % 4) * 8 + lon // 4


@functools.lru_cache(maxsize=None)
def fourier_constants():
    slot = np.arange(LON * 64)
    block, inner = lon_of(slot // 64), slot % 64
    lon = block * BLK + inner
    valid = (inner < BLK)[:, None]
    wave = np.arange(WAVES)
    angle = 2.0 * np.pi / NLON * ((lon[:, None] * wave[None, :]) % NLON)
    owners = lon_of(np.arange(LON))
    first = np.where(owners < LON // 2, 2 * owners, 63 - 2 * owners)
    sets = np.stack([first, 63 - first], axis=1)
    cosine = np.where(valid, np.cos(angle), 0.0).reshape(-1, 64, HALF)[:, sets]
    sine = np.where(valid, np.sin(angle), 0.0).reshape(-1, 64, HALF)[:, sets]
    basis = np.stack([cosine, -sine], axis=3).reshape(LON * 64, 2 * WAVES)
    factor = np.where(wave == 0, 1.0, 2.0).reshape(64, HALF)[sets] / WAVES
    factor = np.broadcast_to(factor[:, :, None, :], (LON, 2, 2, HALF)).reshape(2 * WAVES, 1)
    return split_constant(basis / NLON) + split_constant(factor * basis.T)


@functools.lru_cache(maxsize=None)
def start_constants():
    start = [
        (0.5 * math.log(m + 0.5) + 0.5 * math.lgamma(m + 0.5) - 0.5 * math.lgamma(m + 1.0) - 0.25 * math.log(math.pi))
        / math.log(2.0)
        for m in range(WAVES)
    ]
    return np.tile(np.array(start, np.float32).reshape(64, HALF), (1, 2 * GROUPS))


def lanes(shape):
    return lax.broadcasted_iota(jnp.int32, shape, len(shape) - 1)


def swap_groups(items):
    group = lanes(items[0].shape) // 16
    items = list(items)
    for step in (4, 2, 1):
        keep = (group & step) == 0
        for low in range(GROUPS):
            if low & step:
                continue
            high = low + step
            x, y = items[low], items[high]
            items[low] = jnp.where(keep, x, pltpu.roll(y, 16 * step, 1))
            items[high] = jnp.where(keep, pltpu.roll(x, 128 - 16 * step, 1), y)
    return items


def fold_rows(parts):
    row = lax.broadcasted_iota(jnp.int32, (8, 128), 0)
    upper = row < 4
    four = []
    for index in range(4):
        x, y = parts[index], parts[index + 4]
        four.append(jnp.where(upper, x, y) + pltpu.roll(jnp.where(upper, y, x), 4, 0))
    keep = (row & 2) == 0
    a, b = [
        jnp.where(
            keep,
            four[index] + pltpu.roll(four[index], 6, 0),
            four[index + 2] + pltpu.roll(four[index + 2], 2, 0),
        )
        for index in range(2)
    ]
    keep = (row & 1) == 0
    after, before = pltpu.roll(a, 7, 0), pltpu.roll(b, 1, 0)
    return jnp.where(keep, a + after, before + b), jnp.where(keep, a - after, before - b)


def split(x):
    high = x.astype(BF16)
    return high, (x - high.astype(F32)).astype(BF16)


def mirrored(south, a):
    return jnp.where(south, GROUPS - 1 - a, a)


def block_rows(index, size):
    return pl.ds(pl.multiple_of(index * size, size), size)


def gather_rows(t_ref, sb_ref):
    def body(d, _):
        c, h = d // 2, d % 2
        for f in range(3):
            sb_ref[pl.ds(d * MSG_G + f * 9, 9), :] = t_ref[pl.ds((f * MODES + c) * 18 + h * 9, 9), :]
        return 0

    lax.fori_loop(0, LON, body, 0)


def set_lines(g):
    return (64 - g + 3) // 4 * 32


def legendre_tables(g, start_ref, slope_ref, lag_ref, trig_ref, p_ref):
    member = lanes((1, 128)) % HALF
    waves = ((member + HALF * g).astype(F32), (member + HALF * (63 - g)).astype(F32))
    split_line = set_lines(g)

    def coefficients(block, _):
        line = lax.broadcasted_iota(jnp.int32, (32, 128), 0) + block * 32
        second = line >= split_line
        offsets = jnp.where(second, line - split_line, line).astype(F32)
        wave = jnp.where(second, waves[1], waves[0])
        degree = wave + offsets
        spacing = jnp.maximum(offsets * (2.0 * wave + offsets), 1.0)
        slope = jnp.sqrt(jnp.maximum(4.0 * degree * degree - 1.0, 0.0) / spacing)
        numerator = (2.0 * degree + 1.0) * (offsets - 1.0) * (degree - 1.0 + wave)
        lag = jnp.sqrt(jnp.maximum(numerator, 0.0) / (jnp.maximum(2.0 * degree - 3.0, 1.0) * spacing))
        first = offsets < 0.5
        slope_ref[block_rows(block, 32), :] = jnp.where(first, 0.0, slope)
        lag_ref[block_rows(block, 32), :] = jnp.where(first, 1.0, lag)
        return 0

    lax.fori_loop(0, QUADS, coefficients, 0)
    row = lax.broadcasted_iota(jnp.int32, (ROWS, 128), 0)
    colat = ((row // 24) * 8 + row % 8) * 24 + (row // 8 % 3) * 8 + lanes((ROWS, 128)) // MDEV
    theta = math.pi * (colat.astype(F32) + 0.5) / NLAT
    mu = jnp.cos(theta)
    sine = jnp.sin(theta)
    trig_ref[...] = sine * (WAVES * math.pi / NLAT)
    log_sine = jnp.log(sine) * (1.0 / math.log(2.0))
    coarse = jnp.floor(log_sine * 1024.0) * (1.0 / 1024.0)
    blocks = split_line // 8

    for which, (begin, end) in enumerate(((0, blocks), (blocks, LINES // 8))):
        wave = waves[which]
        whole = wave * coarse
        exponent = jnp.floor(whole)
        start = start_ref[pl.ds(63 - g if which else g, 1), :]
        lower = -jnp.exp2((whole - exponent) + wave * (log_sine - coarse) + start)

        def body(block, carry, begin=begin, wave=wave):
            upper, lower, exponent = carry
            growth = jnp.exp2(jnp.maximum(exponent, -140.0))
            for offset in range(8):
                line = block * 8 + offset
                moved = (slope_ref[pl.ds(line, 1), :] * mu) * upper - lag_ref[pl.ds(line, 1), :] * lower
                upper, lower = moved, upper
                k = line - begin * 8
                inside = wave + k.astype(F32) <= WAVES - 1.0
                p_ref[pl.ds(block * PLANE + offset, ROWS, stride=8), :] = jnp.where(inside, upper * growth, 0.0)
            big = jnp.maximum(jnp.abs(upper), jnp.abs(lower)) > 2.0**32
            scale = jnp.where(big, 2.0**-32, 1.0)
            return upper * scale, lower * scale, exponent + jnp.where(big, 32.0, 0.0)

        lax.fori_loop(begin, end, body, (jnp.zeros_like(lower), lower, exponent))


def forward_operand(group, r_ref, x_ref):
    lane = lanes((16, 128))

    def body(pair, _):
        first_row = (group * 8 + 2 * pair) * SLOT_G
        columns = [[r_ref[pl.ds(first_row + par * SLOT_G + c, 16, stride=3), :] for c in range(3)] for par in range(2)]
        for a in range(GROUPS):
            first, offset = divmod(BLK * a, 128)
            pieces = []
            for par in range(2):
                source = columns[par][first]
                if offset + BLK > 128:
                    source = jnp.where(lane >= offset, source, columns[par][first + 1])
                shift = (64 * par - offset) % 128
                pieces.append(pltpu.roll(source, shift, 1) if shift else source)
            high, low = split(jnp.where(lane < 64, pieces[0], pieces[1]))
            x_ref[a * 16 : (a + 1) * 16, block_rows(pair, 128)] = high
            x_ref[128 + a * 16 : 128 + (a + 1) * 16, block_rows(pair, 128)] = low
        return 0

    lax.fori_loop(0, 4, body, 0)


def product(x_ref, high_ref, low_ref, rows, columns):
    both = jnp.dot(x_ref[...], high_ref[rows, columns], preferred_element_type=F32)
    rest = jnp.dot(x_ref[0:128, :], low_ref[rows, columns], preferred_element_type=F32)
    return both[0:128] + both[128:256] + rest


def add_products(group, x_ref, high_ref, low_ref, sum_ref):
    rows = block_rows(group, x_ref.shape[1])

    def body(block, _):
        columns = block_rows(block, 256)
        sum_ref[:, columns] += product(x_ref, high_ref, low_ref, rows, columns)
        return 0

    lax.fori_loop(0, sum_ref.shape[1] // 256, body, 0)


def forward_blocks(q, south, group, x_ref, high_ref, low_ref, sum_ref, block_ref, m_ref, send):
    rows = block_rows(group, x_ref.shape[1])

    def body(step, _):
        block = (q + turn(step)) % 4
        columns = block_rows(block, 256)
        block_ref[...] = sum_ref[:, columns] + product(x_ref, high_ref, low_ref, rows, columns)
        for order in range(2):
            half = jnp.where(q // 4 < 4, 1 - order, order)
            items = swap_groups(
                [block_ref[block_rows(mirrored(south, a), 16), block_rows(half, 128)] for a in range(GROUPS)]
            )
            for group in range(GROUPS):
                owner = block * 8 + half * 4 + group // 2
                m_ref[pl.ds(owner * MSG_C + (group % 2) * 9, 9), :] = items[group][0:9]
            for index in range(4):
                send(block * 8 + half * 4 + index)
        return 0

    lax.fori_loop(0, 4, body, 0)


def analysis(g, g_ref, trig_ref, eo_ref, p_ref, a_ref):
    for n in range(2):
        for s in range(3):
            weight = trig_ref[n * 24 + s * 8 : n * 24 + s * 8 + 8, :]
            for which in range(2):
                for f in range(3):
                    line = which * 9 + f * 3
                    north = g_ref[pl.ds(n * 8 * MSG_C + line + s, 8, stride=MSG_C), :]
                    south = g_ref[pl.ds((16 + n * 8) * MSG_C + line + 2 - s, 8, stride=MSG_C), :]
                    first = (which * 3 + f) * PLANE + (n * 24 + s * 8) * 8
                    even, odd = (north + south) * weight, (north - south) * weight
                    for k in range(8):
                        eo_ref[pl.ds(first + k, 8, stride=8), :] = odd if k % 2 else even

    quads = set_lines(g) // 32

    def body(quad, _):
        base = jnp.where(quad >= quads, 3 * PLANE, 0)

        def rows(group, sums):
            sums = list(sums)
            for row in range(16):
                first = (group * 16 + row) * 8
                fields = [eo_ref[pl.ds(pl.multiple_of(base + f * PLANE + first, 8), 8), :] for f in range(3)]
                for b in range(4):
                    plane = p_ref[pl.ds(pl.multiple_of((quad * 4 + b) * PLANE + first, 8), 8), :]
                    for f in range(3):
                        sums[b * 3 + f] = sums[b * 3 + f] + plane * fields[f]
            return tuple(sums)

        sums = lax.fori_loop(0, ROWS // 16, rows, (jnp.zeros((8, 128), F32),) * 12)
        for b in range(4):
            for f in range(3):
                a_ref[pl.ds(pl.multiple_of(f * LINES_PAD + (quad * 4 + b) * 8, 8), 8), :] = sums[b * 3 + f]
        return 0

    lax.fori_loop(0, QUADS, body, 0)


def update(g, stiff, damp, state_refs, a_ref, ns_refs, st_ref):
    for which in range(2):
        state_ref, ns_ref = state_refs[which], ns_refs[which]
        size = ns_ref.shape[2]
        start = pl.multiple_of(set_lines(g) if which else 0 * g, 32)
        member = lax.broadcasted_iota(jnp.int32, (MDEV, size), 0) % HALF
        wave = (member + HALF * (63 - g if which else g)).astype(F32)
        degree = wave + lanes((MDEV, size)).astype(F32)
        ratio = degree * (degree + 1.0) / (WAVES * (WAVES - 1.0))
        inside = degree <= WAVES - 1.0
        denominator = 1.0 + stiff * ratio
        damped = jnp.where(inside, 1.0 / (1.0 + damp * ratio * ratio), 0.0)

        def total(f):
            turned = jnp.transpose(a_ref[pl.ds(f * LINES_PAD + start, size), :])
            pieces = [turned[16 * n : 16 * n + 16] for n in range(GROUPS)]
            summed = ((pieces[0] + pieces[1]) + (pieces[2] + pieces[3])) + (
                (pieces[4] + pieces[5]) + (pieces[6] + pieces[7])
            )
            old = jnp.concatenate([state_ref[f * 2], state_ref[f * 2 + 1]], axis=0)
            return jnp.where(inside, old + summed, 0.0)

        def put(f, value):
            ns_ref[f * 2] = value[0:8]
            ns_ref[f * 2 + 1] = value[8:16]
            turned = jnp.transpose(jnp.concatenate([value] * GROUPS, axis=0))
            st_ref[pl.ds(f * LINES_PAD + start, size), :] = turned

        vorticity, divergence, height = total(0), total(1), total(2)
        put(0, vorticity * damped)
        put(1, (divergence + ratio * height) / denominator * damped)
        put(2, (height - stiff * divergence) / denominator * damped)


def synthesis(g, group, p_ref, st_ref, h_ref):
    quads = set_lines(g) // 32
    n, s = group // 3, group % 3

    def degrees(quad, sums):
        sums = list(sums)
        for b in range(4):
            block = quad * 4 + b
            values = [st_ref[pl.ds(pl.multiple_of(f * LINES_PAD + block * 8, 8), 8), :] for f in range(3)]
            for row in range(8):
                first = block * PLANE + group * 64 + row * 8
                plane = p_ref[pl.ds(pl.multiple_of(first, 8), 8), :]
                for f in range(3):
                    sums[f * 8 + row] = sums[f * 8 + row] + plane * values[f]
        return tuple(sums)

    zeros = (jnp.zeros((8, 128), F32),) * 24
    sets = [lax.fori_loop(0, quads, degrees, zeros), lax.fori_loop(quads, QUADS, degrees, zeros)]
    for which in range(2):
        for f in range(3):
            north, south = fold_rows(sets[which][f * 8 : f * 8 + 8])
            line = which * 9 + f * 3
            h_ref[pl.ds(n * 8 * MSG_C + line + s, 8, stride=MSG_C), :] = north
            h_ref[pl.ds((16 + n * 8) * MSG_C + line + 2 - s, 8, stride=MSG_C), :] = south


def inverse_operand(group, south, cp_ref, y_ref):
    for column in range(2):
        first = (group * 8 + column * 4) * SLOT_C
        items = swap_groups([cp_ref[pl.ds(first + g // 2 * SLOT_C + g % 2 * 9, 16), :] for g in range(GROUPS)])
        for a in range(GROUPS):
            row = mirrored(south, a)
            high, low = split(items[a])
            y_ref[block_rows(row, 16), block_rows(group * 2 + column, 128)] = high
            y_ref[block_rows(row + GROUPS, 16), block_rows(group * 2 + column, 128)] = low


def inverse_blocks(q, y_ref, high_ref, low_ref, block_ref, w_ref, send):
    lane = lanes((16, 128))

    def body(step, _):
        block = (q + turn(step // 2)) % 4 * 2 + jnp.where(q // 4 < 4, 1 - step % 2, step % 2)
        columns = block_rows(block, 256)
        block_ref[...] = product(y_ref, high_ref, low_ref, slice(None), columns)
        for index in range(4):
            half, par = divmod(index, 2)
            owner = block * 4 + index
            columns = [None] * 3
            for a in range(GROUPS):
                first, offset = divmod(BLK * a, 128)
                piece = block_ref[a * 16 : (a + 1) * 16, half * 128 : (half + 1) * 128]
                shift = (offset - 64 * par) % 128
                piece = pltpu.roll(piece, shift, 1) if shift else piece
                if columns[first] is None:
                    columns[first] = piece
                else:
                    columns[first] = jnp.where(lane >= offset, piece, columns[first])
                if offset + BLK > 128:
                    columns[first + 1] = piece
            for c in range(3):
                w_ref[pl.ds(owner * MSG_G + c, 9, stride=3), :] = columns[c][0:9]
            send(owner)
        return 0

    lax.fori_loop(0, 8, body, 0)


def far_first(y, n):
    return (y + jnp.where(n % 2 == 0, 4 - n // 2, 4 + (n + 1) // 2)) % 8


def turn(step):
    return jnp.where(step == 0, 2, jnp.where(step == 1, 1, jnp.where(step == 2, 3, 0)))


def slot_of(source):
    return jnp.where(source < 16, source, 47 - source)


def kernel(
    t_any,
    state_any,
    start_any,
    stiff_any,
    damp_any,
    fh_any,
    fl_any,
    ih_any,
    il_any,
    ns_ref,
    o_ref,
    t_ref,
    low_state_ref,
    high_state_ref,
    low_new_ref,
    high_new_ref,
    zero_ref,
    start_ref,
    stiff_ref,
    damp_ref,
    fh_ref,
    fl_ref,
    ih_ref,
    il_ref,
    sb_ref,
    r_ref,
    x_ref,
    fsum_ref,
    block_ref,
    m_ref,
    g_ref,
    eo_ref,
    slope_ref,
    lag_ref,
    trig_ref,
    p_ref,
    a_ref,
    st_ref,
    h_ref,
    cp_ref,
    y_ref,
    w_ref,
    load_sem,
    send_sem,
    recv_sem,
    ready_sem,
):
    q = lax.axis_index("lon")
    p = lax.axis_index("lat")
    here = place_of(q)
    south = p >= LAT // 2
    low_set = jnp.where(q < LON // 2, 2 * q, 63 - 2 * q)
    owned, half = q // 2, q % 2
    my_source = slot_of(p * 2 + half)
    back_mode = (q // 4 + 16 - p // 2 - p % 2 * 4) % 8 * 2 + q % 4 // 2
    back_half = q % 2
    back_slot = slot_of(p * 2 + back_half)

    zero_copy = pltpu.make_async_copy(zero_ref, ns_ref.at[:, :, 256:512], load_sem.at[8])

    @pl.when(q >= LON // 2)
    def _():
        zero_ref[...] = jnp.zeros_like(zero_ref)
        zero_copy.start()

    barrier = pltpu.get_barrier_semaphore()

    def greet_lon(n, _):
        pl.semaphore_signal(barrier, inc=1, device_id=((q + n) % LON, p), device_id_type=MESH)
        return 0

    def greet_lat(n, _):
        pl.semaphore_signal(barrier, inc=1, device_id=(q, (p + n) % LAT), device_id_type=MESH)
        return 0

    lax.fori_loop(1, LON, greet_lon, 0)
    lax.fori_loop(1, LAT, greet_lat, 0)

    loads = [
        pltpu.make_async_copy(source, target, load_sem.at[index])
        for index, (source, target) in enumerate(
            (
                (t_any, t_ref),
                (start_any, start_ref),
                (fh_any, fh_ref),
                (fl_any, fl_ref),
                (stiff_any, stiff_ref),
                (damp_any, damp_ref),
                (ih_any, ih_ref),
                (il_any, il_ref),
            )
        )
    ]
    for load in loads:
        load.start()

    def copy(source, target, stage, group, peer):
        return pltpu.make_async_remote_copy(
            src_ref=source,
            dst_ref=target,
            send_sem=send_sem.at[stage],
            recv_sem=recv_sem.at[stage, group],
            device_id=peer,
            device_id_type=MESH,
        )

    def copy_or_keep(source, target, stage, group, peer):
        lon, lat = peer
        own = jnp.logical_and(lon == q, lat == p)

        @pl.when(jnp.logical_not(own))
        def _():
            copy(source, target, stage, group, peer).start()

        @pl.when(own)
        def _():
            pltpu.make_async_copy(source, target, recv_sem.at[stage, group]).start()

    def wait(ref, first, rows, sem):
        part = ref.at[pl.ds(first, rows)]
        pltpu.make_async_copy(part, part, sem).wait()

    def send_grid(n, _):
        place = (here // 8 + turn(n // 8)) % 4 * 8 + far_first(here % 8, n % 8)
        lon = lon_of(place)
        copy(sb_ref.at[pl.ds(lon * MSG_G, MSG_G)], r_ref.at[pl.ds(here * SLOT_G, MSG_G)], 0, here // 8, (lon, p)).start()
        return 0

    def send_waves(place):
        copy_or_keep(
            m_ref.at[pl.ds(place * MSG_C, MSG_C)],
            g_ref.at[pl.ds(my_source * MSG_C, MSG_C)],
            1,
            0,
            (lon_of(place), owned),
        )

    def send_rows(n, part):
        index = (here // 8 * 4 + n) % 16
        slot = index // 8 * 16 + part * 8 + index % 8
        source = slot_of(slot)
        lat = source // 2
        lon = (p // 2 + lat // 2 + lat % 2 * 4) % 8 * 4 + p % 2 * 2 + source % 2
        copy_or_keep(
            h_ref.at[pl.ds(slot * MSG_C, MSG_C)],
            cp_ref.at[pl.ds(here * SLOT_C, MSG_C)],
            2,
            here // 8,
            (lon, lat),
        )
        return part

    def send_back(place):
        for f in range(3):
            copy_or_keep(
                w_ref.at[pl.ds(place * MSG_G + f * 9, 9)],
                o_ref.at[pl.ds((f * MODES + back_mode) * 18 + back_half * 9, 9)],
                3,
                0,
                (lon_of(place), p),
            )

    partner = (LON - 1 - q, p)
    keeps_low = q < LON // 2
    mine, other = pl.ds(0, HALF), pl.ds(HALF, HALF)

    def state_copies(low):
        if low:
            keep = pltpu.make_async_copy(state_any.at[:, mine, :], low_state_ref, recv_sem.at[4, 0])
            return keep, copy(state_any.at[:, other, :], low_state_ref, 4, 0, partner)
        keep = pltpu.make_async_copy(state_any.at[:, mine, 0:256], high_state_ref, recv_sem.at[4, 1])
        return keep, copy(state_any.at[:, other, 0:256], high_state_ref, 4, 1, partner)

    def new_copies(low):
        if low:
            keep = pltpu.make_async_copy(low_new_ref, ns_ref.at[:, mine, :], recv_sem.at[5, 1])
            return keep, copy(high_new_ref, ns_ref.at[:, other, 0:256], 5, 0, partner)
        keep = pltpu.make_async_copy(high_new_ref, ns_ref.at[:, mine, 0:256], recv_sem.at[5, 1])
        return keep, copy(low_new_ref, ns_ref.at[:, other, :], 5, 0, partner)

    def either(act):
        @pl.when(keeps_low)
        def _():
            act(True)

        @pl.when(jnp.logical_not(keeps_low))
        def _():
            act(False)

    def send_state(low):
        keep, go = state_copies(low)
        keep.start()
        go.start()

    def send_new(low):
        keep, go = new_copies(low)
        keep.start()
        go.start()

    def sent_state(low):
        state_copies(low)[1].wait_send()

    def finish_new(low):
        keep, go = new_copies(low)
        keep.wait()
        go.wait_send()
        if not low:
            zero_copy.wait()
        part = ns_ref.at[:, other, :] if low else ns_ref.at[:, other, 0:256]
        pltpu.make_async_copy(part, part, recv_sem.at[5, 0]).wait()

    loads[0].wait()
    gather_rows(t_ref, sb_ref)
    pl.semaphore_wait(barrier, LON - 1 + LAT - 1)
    lax.fori_loop(0, LON - 1, send_grid, 0)
    pltpu.make_async_copy(
        sb_ref.at[pl.ds(q * MSG_G, MSG_G)], r_ref.at[pl.ds(here * SLOT_G, MSG_G)], recv_sem.at[0, here // 8]
    ).start()

    def tell(n, _):
        pl.semaphore_signal(ready_sem, inc=1, device_id=(q, (p + n) % LAT), device_id_type=MESH)
        return 0

    lax.fori_loop(1, LAT, tell, 0)

    loads[1].wait()
    legendre_tables(low_set, start_ref, slope_ref, lag_ref, trig_ref, p_ref)
    either(send_state)
    fsum_ref[...] = jnp.zeros_like(fsum_ref)
    loads[2].wait()
    loads[3].wait()

    def grid_group(step):
        group = (here // 8 + 4 - turn(step)) % 4
        wait(r_ref, group * 8 * SLOT_G, 8 * MSG_G, recv_sem.at[0, group])
        forward_operand(group, r_ref, x_ref)
        return group

    def forward_step(step, _):
        add_products(grid_group(step), x_ref, fh_ref, fl_ref, fsum_ref)
        return 0

    lax.fori_loop(0, 3, forward_step, 0)
    group = grid_group(3)
    pl.semaphore_wait(ready_sem, LAT - 1)
    forward_blocks(q, south, group, x_ref, fh_ref, fl_ref, fsum_ref, block_ref, m_ref, send_waves)
    for load in loads[4:]:
        load.wait()
    wait(sb_ref, 0, (LON - 1) * MSG_G, send_sem.at[0])
    wait(g_ref, 0, 32 * MSG_C, recv_sem.at[1, 0])
    analysis(low_set, g_ref, trig_ref, eo_ref, p_ref, a_ref)
    either(sent_state)
    pltpu.make_async_copy(low_state_ref, low_state_ref, recv_sem.at[4, 0]).wait()
    pltpu.make_async_copy(high_state_ref, high_state_ref, recv_sem.at[4, 1]).wait()
    update(
        low_set,
        stiff_ref[p],
        damp_ref[p],
        (low_state_ref, high_state_ref),
        a_ref,
        (low_new_ref, high_new_ref),
        st_ref,
    )
    either(send_new)

    def synthesize(part, _):
        lax.fori_loop(0, 3, lambda s, _: (synthesis(low_set, part * 3 + s, p_ref, st_ref, h_ref), 0)[1], 0)
        lax.fori_loop(0, 16, send_rows, part)
        return 0

    lax.fori_loop(0, 2, synthesize, 0)

    def wait_sent(ref, own, stage):
        @pl.when(own)
        def _():
            wait(ref, 0, 31 * MSG_C, send_sem.at[stage])

        @pl.when(jnp.logical_not(own))
        def _():
            wait(ref, 0, 32 * MSG_C, send_sem.at[stage])

    wait_sent(m_ref, owned == p, 1)

    def waves_group(step, _):
        group = (back_slot // 8 + 4 - step) % 4
        wait(cp_ref, group * 8 * SLOT_C, 8 * MSG_C, recv_sem.at[2, group])
        inverse_operand(group, south, cp_ref, y_ref)
        return 0

    lax.fori_loop(0, 4, waves_group, 0)
    inverse_blocks(q, y_ref, ih_ref, il_ref, block_ref, w_ref, send_back)
    wait_sent(h_ref, back_mode == p, 2)
    either(finish_new)
    wait(o_ref, 0, LON * MSG_G, recv_sem.at[3, 0])
    wait(w_ref, 0, (LON - 1) * MSG_G, send_sem.at[3])


def result_kernel(ns_ref, o_ref, new_state_any, new_fields_any, sem):
    copies = [
        pltpu.make_async_copy(source, target, sem.at[index])
        for index, (source, target) in enumerate(((ns_ref, new_state_any), (o_ref, new_fields_any)))
    ]
    for item in copies:
        item.start()
    for item in copies:
        item.wait()


def body(tendency, state, stiffness, damping):
    rows = LON * MSG_G
    vmem = pl.BlockSpec(memory_space=pltpu.VMEM)
    anywhere = pl.BlockSpec(memory_space=pl.ANY)
    shapes = (jax.ShapeDtypeStruct((FR, MDEV, WAVES), F32), jax.ShapeDtypeStruct((rows, 128), F32))
    new_state, new_fields = pl.pallas_call(
        kernel,
        out_shape=shapes,
        in_specs=[anywhere] * 9,
        out_specs=(vmem, vmem),
        scratch_shapes=[
            pltpu.VMEM((rows, 128), F32),
            pltpu.VMEM((FR, HALF, WAVES), F32),
            pltpu.VMEM((FR, HALF, 256), F32),
            pltpu.VMEM((FR, HALF, WAVES), F32),
            pltpu.VMEM((FR, HALF, 256), F32),
            pltpu.VMEM((FR, MDEV, 256), F32),
            pltpu.VMEM((64, 128), F32),
            pltpu.SMEM((MODES,), F32),
            pltpu.SMEM((MODES,), F32),
            pltpu.VMEM((64 * LON, 2 * WAVES), BF16),
            pltpu.VMEM((64 * LON, 2 * WAVES), BF16),
            pltpu.VMEM((2 * WAVES, 64 * LON), BF16),
            pltpu.VMEM((2 * WAVES, 64 * LON), BF16),
            pltpu.VMEM((rows, 128), F32),
            pltpu.VMEM((LON * SLOT_G, 128), F32),
            pltpu.VMEM((256, 512), BF16),
            pltpu.VMEM((128, 2 * WAVES), F32),
            pltpu.VMEM((128, 256), F32),
            pltpu.VMEM((32 * MSG_C, 128), F32),
            pltpu.VMEM((32 * MSG_C, 128), F32),
            pltpu.VMEM((FR * PLANE, 128), F32),
            pltpu.VMEM((LINES, 128), F32),
            pltpu.VMEM((LINES, 128), F32),
            pltpu.VMEM((ROWS, 128), F32),
            pltpu.VMEM((LINES // 8 * PLANE, 128), F32),
            pltpu.VMEM((3 * LINES_PAD, 128), F32),
            pltpu.VMEM((3 * LINES_PAD, 128), F32),
            pltpu.VMEM((32 * MSG_C, 128), F32),
            pltpu.VMEM((32 * SLOT_C, 128), F32),
            pltpu.VMEM((256, 2 * WAVES), BF16),
            pltpu.VMEM((rows, 128), F32),
            pltpu.SemaphoreType.DMA((9,)),
            pltpu.SemaphoreType.DMA((6,)),
            pltpu.SemaphoreType.DMA((6, 4)),
            pltpu.SemaphoreType.REGULAR,
        ],
        compiler_params=pltpu.CompilerParams(
            collective_id=0, has_side_effects=True, vmem_limit_bytes=60 * 2**20
        ),
        name="spectral_step",
    )(
        tendency.reshape(rows, 128),
        state.reshape(FR, MDEV, WAVES),
        jnp.asarray(start_constants()),
        stiffness,
        damping,
        *[jnp.asarray(table) for table in fourier_constants()],
    )
    new_state, new_fields = pl.pallas_call(
        result_kernel,
        out_shape=shapes,
        in_specs=[vmem, vmem],
        out_specs=(anywhere, anywhere),
        scratch_shapes=[pltpu.SemaphoreType.DMA((2,))],
        name="results",
    )(new_state, new_fields)
    return new_state.reshape(state.shape), new_fields.reshape(tendency.shape)


def solution(mesh):
    return jax.shard_map(
        body,
        mesh=mesh,
        in_specs=(P(None, None, "lat", "lon", None), P("lat", None, None, "lon", None), P(), P()),
        out_specs=(P("lat", None, None, "lon", None), P(None, None, "lat", "lon", None)),
        check_vma=False,
    )
```

```python
import functools
import math

import jax
import jax.numpy as jnp
import ml_dtypes
import numpy as np
from jax import lax
from jax.experimental import pallas as pl
from jax.experimental.pallas import tpu as pltpu
from jax.sharding import PartitionSpec as P

NLAT = 768
NLON = 1536
WAVES = 512
MODES = 16
LON = 32
LAT = 16
BLK = 48
MDEV = 16
GROUPS = 8
MSG_G = 27
SLOT_G = 48
SLOT_C = 32
MSG_C = 18
FR = 6
HALF = 8
QUADS = 17
LINES = QUADS * 32
LINES_PAD = 768
PLANE = 384
ROWS = 48
MESH = pl.DeviceIdType.MESH
F32 = jnp.float32
BF16 = jnp.bfloat16


def split_constant(table):
    high = table.astype(np.float32).astype(ml_dtypes.bfloat16)
    low = (table - high.astype(np.float64)).astype(np.float32).astype(ml_dtypes.bfloat16)
    return high, low


def lon_of(place):
    return (place % 8) * 4 + place // 8


def place_of(lon):
    return (lon % 4) * 8 + lon // 4


@functools.lru_cache(maxsize=None)
def fourier_constants():
    slot = np.arange(LON * 64)
    block, inner = lon_of(slot // 64), slot % 64
    lon = block * BLK + inner
    valid = (inner < BLK)[:, None]
    wave = np.arange(WAVES)
    angle = 2.0 * np.pi / NLON * ((lon[:, None] * wave[None, :]) % NLON)
    owners = lon_of(np.arange(LON))
    first = np.where(owners < LON // 2, 2 * owners, 63 - 2 * owners)
    sets = np.stack([first, 63 - first], axis=1)
    cosine = np.where(valid, np.cos(angle), 0.0).reshape(-1, 64, HALF)[:, sets]
    sine = np.where(valid, np.sin(angle), 0.0).reshape(-1, 64, HALF)[:, sets]
    basis = np.stack([cosine, -sine], axis=3).reshape(LON * 64, 2 * WAVES)
    factor = np.where(wave == 0, 1.0, 2.0).reshape(64, HALF)[sets] / WAVES
    factor = np.broadcast_to(factor[:, :, None, :], (LON, 2, 2, HALF)).reshape(2 * WAVES, 1)
    return split_constant(basis / NLON) + split_constant(factor * basis.T)


@functools.lru_cache(maxsize=None)
def start_constants():
    start = [
        (0.5 * math.log(m + 0.5) + 0.5 * math.lgamma(m + 0.5) - 0.5 * math.lgamma(m + 1.0) - 0.25 * math.log(math.pi))
        / math.log(2.0)
        for m in range(WAVES)
    ]
    return np.tile(np.array(start, np.float32).reshape(64, HALF), (1, 2 * GROUPS))


def lanes(shape):
    return lax.broadcasted_iota(jnp.int32, shape, len(shape) - 1)


def swap_groups(items):
    group = lanes(items[0].shape) // 16
    items = list(items)
    for step in (4, 2, 1):
        keep = (group & step) == 0
        for low in range(GROUPS):
            if low & step:
                continue
            high = low + step
            x, y = items[low], items[high]
            items[low] = jnp.where(keep, x, pltpu.roll(y, 16 * step, 1))
            items[high] = jnp.where(keep, pltpu.roll(x, 128 - 16 * step, 1), y)
    return items


def fold_rows(parts):
    row = lax.broadcasted_iota(jnp.int32, (8, 128), 0)
    upper = row < 4
    four = []
    for index in range(4):
        x, y = parts[index], parts[index + 4]
        four.append(jnp.where(upper, x, y) + pltpu.roll(jnp.where(upper, y, x), 4, 0))
    keep = (row & 2) == 0
    a, b = [
        jnp.where(
            keep,
            four[index] + pltpu.roll(four[index], 6, 0),
            four[index + 2] + pltpu.roll(four[index + 2], 2, 0),
        )
        for index in range(2)
    ]
    keep = (row & 1) == 0
    after, before = pltpu.roll(a, 7, 0), pltpu.roll(b, 1, 0)
    return jnp.where(keep, a + after, before + b), jnp.where(keep, a - after, before - b)


def split(x):
    high = x.astype(BF16)
    return high, (x - high.astype(F32)).astype(BF16)


def mirrored(south, a):
    return jnp.where(south, GROUPS - 1 - a, a)


def block_rows(index, size):
    return pl.ds(pl.multiple_of(index * size, size), size)


def gather_rows(t_ref, sb_ref):
    def body(d, _):
        c, h = d // 2, d % 2
        for f in range(3):
            sb_ref[pl.ds(d * MSG_G + f * 9, 9), :] = t_ref[pl.ds((f * MODES + c) * 18 + h * 9, 9), :]
        return 0

    lax.fori_loop(0, LON, body, 0)


def set_lines(g):
    return (64 - g + 3) // 4 * 32


def legendre_tables(g, start_ref, slope_ref, lag_ref, trig_ref, p_ref):
    member = lanes((1, 128)) % HALF
    waves = ((member + HALF * g).astype(F32), (member + HALF * (63 - g)).astype(F32))
    split_line = set_lines(g)

    def coefficients(block, _):
        line = lax.broadcasted_iota(jnp.int32, (32, 128), 0) + block * 32
        second = line >= split_line
        offsets = jnp.where(second, line - split_line, line).astype(F32)
        wave = jnp.where(second, waves[1], waves[0])
        degree = wave + offsets
        spacing = jnp.maximum(offsets * (2.0 * wave + offsets), 1.0)
        slope = jnp.sqrt(jnp.maximum(4.0 * degree * degree - 1.0, 0.0) / spacing)
        numerator = (2.0 * degree + 1.0) * (offsets - 1.0) * (degree - 1.0 + wave)
        lag = jnp.sqrt(jnp.maximum(numerator, 0.0) / (jnp.maximum(2.0 * degree - 3.0, 1.0) * spacing))
        first = offsets < 0.5
        slope_ref[block_rows(block, 32), :] = jnp.where(first, 0.0, slope)
        lag_ref[block_rows(block, 32), :] = jnp.where(first, 1.0, lag)
        return 0

    lax.fori_loop(0, QUADS, coefficients, 0)
    row = lax.broadcasted_iota(jnp.int32, (ROWS, 128), 0)
    colat = ((row // 24) * 8 + row % 8) * 24 + (row // 8 % 3) * 8 + lanes((ROWS, 128)) // MDEV
    theta = math.pi * (colat.astype(F32) + 0.5) / NLAT
    mu = jnp.cos(theta)
    sine = jnp.sin(theta)
    trig_ref[...] = sine * (WAVES * math.pi / NLAT)
    log_sine = jnp.log(sine) * (1.0 / math.log(2.0))
    coarse = jnp.floor(log_sine * 1024.0) * (1.0 / 1024.0)
    blocks = split_line // 8

    for which, (begin, end) in enumerate(((0, blocks), (blocks, LINES // 8))):
        wave = waves[which]
        whole = wave * coarse
        exponent = jnp.floor(whole)
        start = start_ref[pl.ds(63 - g if which else g, 1), :]
        lower = -jnp.exp2((whole - exponent) + wave * (log_sine - coarse) + start)

        def body(block, carry, begin=begin, wave=wave):
            upper, lower, exponent = carry
            growth = jnp.exp2(jnp.maximum(exponent, -140.0))
            for offset in range(8):
                line = block * 8 + offset
                moved = (slope_ref[pl.ds(line, 1), :] * mu) * upper - lag_ref[pl.ds(line, 1), :] * lower
                upper, lower = moved, upper
                k = line - begin * 8
                inside = wave + k.astype(F32) <= WAVES - 1.0
                p_ref[pl.ds(block * PLANE + offset, ROWS, stride=8), :] = jnp.where(inside, upper * growth, 0.0)
            big = jnp.maximum(jnp.abs(upper), jnp.abs(lower)) > 2.0**32
            scale = jnp.where(big, 2.0**-32, 1.0)
            return upper * scale, lower * scale, exponent + jnp.where(big, 32.0, 0.0)

        lax.fori_loop(begin, end, body, (jnp.zeros_like(lower), lower, exponent))


def forward_operand(group, r_ref, x_ref):
    lane = lanes((16, 128))

    def body(pair, _):
        first_row = (group * 8 + 2 * pair) * SLOT_G
        columns = [[r_ref[pl.ds(first_row + par * SLOT_G + c, 16, stride=3), :] for c in range(3)] for par in range(2)]
        for a in range(GROUPS):
            first, offset = divmod(BLK * a, 128)
            pieces = []
            for par in range(2):
                source = columns[par][first]
                if offset + BLK > 128:
                    source = jnp.where(lane >= offset, source, columns[par][first + 1])
                shift = (64 * par - offset) % 128
                pieces.append(pltpu.roll(source, shift, 1) if shift else source)
            high, low = split(jnp.where(lane < 64, pieces[0], pieces[1]))
            x_ref[a * 16 : (a + 1) * 16, block_rows(pair, 128)] = high
            x_ref[128 + a * 16 : 128 + (a + 1) * 16, block_rows(pair, 128)] = low
        return 0

    lax.fori_loop(0, 4, body, 0)


def product(x_ref, high_ref, low_ref, rows, columns):
    both = jnp.dot(x_ref[...], high_ref[rows, columns], preferred_element_type=F32)
    rest = jnp.dot(x_ref[0:128, :], low_ref[rows, columns], preferred_element_type=F32)
    return both[0:128] + both[128:256] + rest


def add_products(group, x_ref, high_ref, low_ref, sum_ref):
    rows = block_rows(group, x_ref.shape[1])

    def body(block, _):
        columns = block_rows(block, 256)
        sum_ref[:, columns] += product(x_ref, high_ref, low_ref, rows, columns)
        return 0

    lax.fori_loop(0, sum_ref.shape[1] // 256, body, 0)


def forward_blocks(q, south, group, x_ref, high_ref, low_ref, sum_ref, block_ref, m_ref, send):
    rows = block_rows(group, x_ref.shape[1])

    def body(step, _):
        block = (q + turn(step)) % 4
        columns = block_rows(block, 256)
        block_ref[...] = sum_ref[:, columns] + product(x_ref, high_ref, low_ref, rows, columns)
        for order in range(2):
            half = jnp.where(q // 4 < 4, 1 - order, order)
            items = swap_groups(
                [block_ref[block_rows(mirrored(south, a), 16), block_rows(half, 128)] for a in range(GROUPS)]
            )
            for group in range(GROUPS):
                owner = block * 8 + half * 4 + group // 2
                m_ref[pl.ds(owner * MSG_C + (group % 2) * 9, 9), :] = items[group][0:9]
            for index in range(4):
                send(block * 8 + half * 4 + index)
        return 0

    lax.fori_loop(0, 4, body, 0)


def analysis(g, g_ref, trig_ref, eo_ref, p_ref, a_ref):
    for n in range(2):
        for s in range(3):
            weight = trig_ref[n * 24 + s * 8 : n * 24 + s * 8 + 8, :]
            for which in range(2):
                for f in range(3):
                    line = which * 9 + f * 3
                    north = g_ref[pl.ds(n * 8 * MSG_C + line + s, 8, stride=MSG_C), :]
                    south = g_ref[pl.ds((16 + n * 8) * MSG_C + line + 2 - s, 8, stride=MSG_C), :]
                    first = (which * 3 + f) * PLANE + (n * 24 + s * 8) * 8
                    even, odd = (north + south) * weight, (north - south) * weight
                    for k in range(8):
                        eo_ref[pl.ds(first + k, 8, stride=8), :] = odd if k % 2 else even

    quads = set_lines(g) // 32

    def body(quad, _):
        base = jnp.where(quad >= quads, 3 * PLANE, 0)

        def rows(group, sums):
            sums = list(sums)
            for row in range(16):
                first = (group * 16 + row) * 8
                fields = [eo_ref[pl.ds(pl.multiple_of(base + f * PLANE + first, 8), 8), :] for f in range(3)]
                for b in range(4):
                    plane = p_ref[pl.ds(pl.multiple_of((quad * 4 + b) * PLANE + first, 8), 8), :]
                    for f in range(3):
                        sums[b * 3 + f] = sums[b * 3 + f] + plane * fields[f]
            return tuple(sums)

        sums = lax.fori_loop(0, ROWS // 16, rows, (jnp.zeros((8, 128), F32),) * 12)
        for b in range(4):
            for f in range(3):
                a_ref[pl.ds(pl.multiple_of(f * LINES_PAD + (quad * 4 + b) * 8, 8), 8), :] = sums[b * 3 + f]
        return 0

    lax.fori_loop(0, QUADS, body, 0)


def update(g, stiff, damp, state_refs, a_ref, ns_refs, st_ref):
    for which in range(2):
        state_ref, ns_ref = state_refs[which], ns_refs[which]
        size = ns_ref.shape[2]
        start = pl.multiple_of(set_lines(g) if which else 0 * g, 32)
        member = lax.broadcasted_iota(jnp.int32, (MDEV, size), 0) % HALF
        wave = (member + HALF * (63 - g if which else g)).astype(F32)
        degree = wave + lanes((MDEV, size)).astype(F32)
        ratio = degree * (degree + 1.0) / (WAVES * (WAVES - 1.0))
        inside = degree <= WAVES - 1.0
        denominator = 1.0 + stiff * ratio
        damped = jnp.where(inside, 1.0 / (1.0 + damp * ratio * ratio), 0.0)

        def total(f):
            turned = jnp.transpose(a_ref[pl.ds(f * LINES_PAD + start, size), :])
            pieces = [turned[16 * n : 16 * n + 16] for n in range(GROUPS)]
            summed = ((pieces[0] + pieces[1]) + (pieces[2] + pieces[3])) + (
                (pieces[4] + pieces[5]) + (pieces[6] + pieces[7])
            )
            old = jnp.concatenate([state_ref[f * 2], state_ref[f * 2 + 1]], axis=0)
            return jnp.where(inside, old + summed, 0.0)

        def put(f, value):
            ns_ref[f * 2] = value[0:8]
            ns_ref[f * 2 + 1] = value[8:16]
            turned = jnp.transpose(jnp.concatenate([value] * GROUPS, axis=0))
            st_ref[pl.ds(f * LINES_PAD + start, size), :] = turned

        vorticity, divergence, height = total(0), total(1), total(2)
        put(0, vorticity * damped)
        put(1, (divergence + ratio * height) / denominator * damped)
        put(2, (height - stiff * divergence) / denominator * damped)


def synthesis(g, group, p_ref, st_ref, h_ref):
    quads = set_lines(g) // 32
    n, s = group // 3, group % 3

    def degrees(quad, sums):
        sums = list(sums)
        for b in range(4):
            block = quad * 4 + b
            values = [st_ref[pl.ds(pl.multiple_of(f * LINES_PAD + block * 8, 8), 8), :] for f in range(3)]
            for row in range(8):
                first = block * PLANE + group * 64 + row * 8
                plane = p_ref[pl.ds(pl.multiple_of(first, 8), 8), :]
                for f in range(3):
                    sums[f * 8 + row] = sums[f * 8 + row] + plane * values[f]
        return tuple(sums)

    zeros = (jnp.zeros((8, 128), F32),) * 24
    sets = [lax.fori_loop(0, quads, degrees, zeros), lax.fori_loop(quads, QUADS, degrees, zeros)]
    for which in range(2):
        for f in range(3):
            north, south = fold_rows(sets[which][f * 8 : f * 8 + 8])
            line = which * 9 + f * 3
            h_ref[pl.ds(n * 8 * MSG_C + line + s, 8, stride=MSG_C), :] = north
            h_ref[pl.ds((16 + n * 8) * MSG_C + line + 2 - s, 8, stride=MSG_C), :] = south


def inverse_operand(group, south, cp_ref, y_ref):
    for column in range(2):
        first = (group * 8 + column * 4) * SLOT_C
        items = swap_groups([cp_ref[pl.ds(first + g // 2 * SLOT_C + g % 2 * 9, 16), :] for g in range(GROUPS)])
        for a in range(GROUPS):
            row = mirrored(south, a)
            high, low = split(items[a])
            y_ref[block_rows(row, 16), block_rows(group * 2 + column, 128)] = high
            y_ref[block_rows(row + GROUPS, 16), block_rows(group * 2 + column, 128)] = low


def inverse_blocks(q, y_ref, high_ref, low_ref, block_ref, w_ref, send):
    lane = lanes((16, 128))

    def body(step, _):
        block = (q + turn(step // 2)) % 4 * 2 + jnp.where(q // 4 < 4, 1 - step % 2, step % 2)
        columns = block_rows(block, 256)
        block_ref[...] = product(y_ref, high_ref, low_ref, slice(None), columns)
        for index in range(4):
            half, par = divmod(index, 2)
            owner = block * 4 + index
            columns = [None] * 3
            for a in range(GROUPS):
                first, offset = divmod(BLK * a, 128)
                piece = block_ref[a * 16 : (a + 1) * 16, half * 128 : (half + 1) * 128]
                shift = (offset - 64 * par) % 128
                piece = pltpu.roll(piece, shift, 1) if shift else piece
                if columns[first] is None:
                    columns[first] = piece
                else:
                    columns[first] = jnp.where(lane >= offset, piece, columns[first])
                if offset + BLK > 128:
                    columns[first + 1] = piece
            for c in range(3):
                w_ref[pl.ds(owner * MSG_G + c, 9, stride=3), :] = columns[c][0:9]
            send(owner)
        return 0

    lax.fori_loop(0, 8, body, 0)


def far_first(y, n):
    return (y + jnp.where(n % 2 == 0, 4 - n // 2, 4 + (n + 1) // 2)) % 8


def turn(step):
    return jnp.where(step == 0, 2, jnp.where(step == 1, 1, jnp.where(step == 2, 3, 0)))


def slot_of(source):
    return jnp.where(source < 16, source, 47 - source)


def kernel(
    t_any,
    state_any,
    start_any,
    stiff_any,
    damp_any,
    fh_any,
    fl_any,
    ih_any,
    il_any,
    ns_ref,
    o_ref,
    t_ref,
    low_state_ref,
    high_state_ref,
    low_new_ref,
    high_new_ref,
    zero_ref,
    start_ref,
    stiff_ref,
    damp_ref,
    fh_ref,
    fl_ref,
    ih_ref,
    il_ref,
    sb_ref,
    r_ref,
    x_ref,
    fsum_ref,
    block_ref,
    m_ref,
    g_ref,
    eo_ref,
    slope_ref,
    lag_ref,
    trig_ref,
    p_ref,
    a_ref,
    st_ref,
    h_ref,
    cp_ref,
    y_ref,
    w_ref,
    load_sem,
    send_sem,
    recv_sem,
    ready_sem,
):
    q = lax.axis_index("lon")
    p = lax.axis_index("lat")
    here = place_of(q)
    south = p >= LAT // 2
    low_set = jnp.where(q < LON // 2, 2 * q, 63 - 2 * q)
    owned, half = q // 2, q % 2
    my_source = slot_of(p * 2 + half)
    back_mode = (q // 4 + 16 - p // 2 - p % 2 * 4) % 8 * 2 + q % 4 // 2
    back_half = q % 2
    back_slot = slot_of(p * 2 + back_half)

    zero_copy = pltpu.make_async_copy(zero_ref, ns_ref.at[:, :, 256:512], load_sem.at[8])

    @pl.when(q >= LON // 2)
    def _():
        zero_ref[...] = jnp.zeros_like(zero_ref)
        zero_copy.start()

    barrier = pltpu.get_barrier_semaphore()

    def greet_lon(n, _):
        pl.semaphore_signal(barrier, inc=1, device_id=((q + n) % LON, p), device_id_type=MESH)
        return 0

    def greet_lat(n, _):
        pl.semaphore_signal(barrier, inc=1, device_id=(q, (p + n) % LAT), device_id_type=MESH)
        return 0

    lax.fori_loop(1, LON, greet_lon, 0)
    lax.fori_loop(1, LAT, greet_lat, 0)

    loads = [
        pltpu.make_async_copy(source, target, load_sem.at[index])
        for index, (source, target) in enumerate(
            (
                (t_any, t_ref),
                (start_any, start_ref),
                (fh_any, fh_ref),
                (fl_any, fl_ref),
                (stiff_any, stiff_ref),
                (damp_any, damp_ref),
                (ih_any, ih_ref),
                (il_any, il_ref),
            )
        )
    ]
    for load in loads:
        load.start()

    def copy(source, target, stage, group, peer):
        return pltpu.make_async_remote_copy(
            src_ref=source,
            dst_ref=target,
            send_sem=send_sem.at[stage],
            recv_sem=recv_sem.at[stage, group],
            device_id=peer,
            device_id_type=MESH,
        )

    def copy_or_keep(source, target, stage, group, peer):
        lon, lat = peer
        own = jnp.logical_and(lon == q, lat == p)

        @pl.when(jnp.logical_not(own))
        def _():
            copy(source, target, stage, group, peer).start()

        @pl.when(own)
        def _():
            pltpu.make_async_copy(source, target, recv_sem.at[stage, group]).start()

    def wait(ref, first, rows, sem):
        part = ref.at[pl.ds(first, rows)]
        pltpu.make_async_copy(part, part, sem).wait()

    def send_grid(n, _):
        place = (here // 8 + turn(n // 8)) % 4 * 8 + far_first(here % 8, n % 8)
        lon = lon_of(place)
        copy(sb_ref.at[pl.ds(lon * MSG_G, MSG_G)], r_ref.at[pl.ds(here * SLOT_G, MSG_G)], 0, here // 8, (lon, p)).start()
        return 0

    def send_waves(place):
        copy_or_keep(
            m_ref.at[pl.ds(place * MSG_C, MSG_C)],
            g_ref.at[pl.ds(my_source * MSG_C, MSG_C)],
            1,
            0,
            (lon_of(place), owned),
        )

    def send_rows(n, part):
        index = (here // 8 * 4 + n) % 16
        slot = index // 8 * 16 + part * 8 + index % 8
        source = slot_of(slot)
        lat = source // 2
        lon = (p // 2 + lat // 2 + lat % 2 * 4) % 8 * 4 + p % 2 * 2 + source % 2
        copy_or_keep(
            h_ref.at[pl.ds(slot * MSG_C, MSG_C)],
            cp_ref.at[pl.ds(here * SLOT_C, MSG_C)],
            2,
            here // 8,
            (lon, lat),
        )
        return part

    def send_back(place):
        for f in range(3):
            copy_or_keep(
                w_ref.at[pl.ds(place * MSG_G + f * 9, 9)],
                o_ref.at[pl.ds((f * MODES + back_mode) * 18 + back_half * 9, 9)],
                3,
                0,
                (lon_of(place), p),
            )

    partner = (LON - 1 - q, p)
    keeps_low = q < LON // 2
    mine, other = pl.ds(0, HALF), pl.ds(HALF, HALF)

    def state_copies(low):
        if low:
            keep = pltpu.make_async_copy(state_any.at[:, mine, :], low_state_ref, recv_sem.at[4, 0])
            return keep, copy(state_any.at[:, other, :], low_state_ref, 4, 0, partner)
        keep = pltpu.make_async_copy(state_any.at[:, mine, 0:256], high_state_ref, recv_sem.at[4, 1])
        return keep, copy(state_any.at[:, other, 0:256], high_state_ref, 4, 1, partner)

    def new_copies(low):
        if low:
            keep = pltpu.make_async_copy(low_new_ref, ns_ref.at[:, mine, :], recv_sem.at[5, 1])
            return keep, copy(high_new_ref, ns_ref.at[:, other, 0:256], 5, 0, partner)
        keep = pltpu.make_async_copy(high_new_ref, ns_ref.at[:, mine, 0:256], recv_sem.at[5, 1])
        return keep, copy(low_new_ref, ns_ref.at[:, other, :], 5, 0, partner)

    def either(act):
        @pl.when(keeps_low)
        def _():
            act(True)

        @pl.when(jnp.logical_not(keeps_low))
        def _():
            act(False)

    def send_state(low):
        keep, go = state_copies(low)
        keep.start()
        go.start()

    def send_new(low):
        keep, go = new_copies(low)
        keep.start()
        go.start()

    def sent_state(low):
        state_copies(low)[1].wait_send()

    def finish_new(low):
        keep, go = new_copies(low)
        keep.wait()
        go.wait_send()
        if not low:
            zero_copy.wait()
        part = ns_ref.at[:, other, :] if low else ns_ref.at[:, other, 0:256]
        pltpu.make_async_copy(part, part, recv_sem.at[5, 0]).wait()

    loads[0].wait()
    gather_rows(t_ref, sb_ref)
    pl.semaphore_wait(barrier, LON - 1 + LAT - 1)
    lax.fori_loop(0, LON - 1, send_grid, 0)
    pltpu.make_async_copy(
        sb_ref.at[pl.ds(q * MSG_G, MSG_G)], r_ref.at[pl.ds(here * SLOT_G, MSG_G)], recv_sem.at[0, here // 8]
    ).start()

    def tell(n, _):
        pl.semaphore_signal(ready_sem, inc=1, device_id=(q, (p + n) % LAT), device_id_type=MESH)
        return 0

    lax.fori_loop(1, LAT, tell, 0)

    loads[1].wait()
    legendre_tables(low_set, start_ref, slope_ref, lag_ref, trig_ref, p_ref)
    fsum_ref[...] = jnp.zeros_like(fsum_ref)
    loads[2].wait()
    loads[3].wait()

    def grid_group(step):
        group = (here // 8 + 4 - turn(step)) % 4
        wait(r_ref, group * 8 * SLOT_G, 8 * MSG_G, recv_sem.at[0, group])
        forward_operand(group, r_ref, x_ref)
        return group

    def forward_step(step, _):
        add_products(grid_group(step), x_ref, fh_ref, fl_ref, fsum_ref)
        return 0

    lax.fori_loop(0, 3, forward_step, 0)
    group = grid_group(3)
    pl.semaphore_wait(ready_sem, LAT - 1)
    forward_blocks(q, south, group, x_ref, fh_ref, fl_ref, fsum_ref, block_ref, m_ref, send_waves)
    either(send_state)
    for load in loads[4:]:
        load.wait()
    wait(sb_ref, 0, (LON - 1) * MSG_G, send_sem.at[0])
    wait(g_ref, 0, 32 * MSG_C, recv_sem.at[1, 0])
    analysis(low_set, g_ref, trig_ref, eo_ref, p_ref, a_ref)
    either(sent_state)
    pltpu.make_async_copy(low_state_ref, low_state_ref, recv_sem.at[4, 0]).wait()
    pltpu.make_async_copy(high_state_ref, high_state_ref, recv_sem.at[4, 1]).wait()
    update(
        low_set,
        stiff_ref[p],
        damp_ref[p],
        (low_state_ref, high_state_ref),
        a_ref,
        (low_new_ref, high_new_ref),
        st_ref,
    )

    def synthesize(part, _):
        lax.fori_loop(0, 3, lambda s, _: (synthesis(low_set, part * 3 + s, p_ref, st_ref, h_ref), 0)[1], 0)
        lax.fori_loop(0, 16, send_rows, part)
        return 0

    lax.fori_loop(0, 2, synthesize, 0)
    either(send_new)

    def wait_sent(ref, own, stage):
        @pl.when(own)
        def _():
            wait(ref, 0, 31 * MSG_C, send_sem.at[stage])

        @pl.when(jnp.logical_not(own))
        def _():
            wait(ref, 0, 32 * MSG_C, send_sem.at[stage])

    wait_sent(m_ref, owned == p, 1)

    def waves_group(step, _):
        group = (back_slot // 8 + 4 - step) % 4
        wait(cp_ref, group * 8 * SLOT_C, 8 * MSG_C, recv_sem.at[2, group])
        inverse_operand(group, south, cp_ref, y_ref)
        return 0

    lax.fori_loop(0, 4, waves_group, 0)
    inverse_blocks(q, y_ref, ih_ref, il_ref, block_ref, w_ref, send_back)
    wait_sent(h_ref, back_mode == p, 2)
    either(finish_new)
    wait(o_ref, 0, LON * MSG_G, recv_sem.at[3, 0])
    wait(w_ref, 0, (LON - 1) * MSG_G, send_sem.at[3])


def result_kernel(ns_ref, o_ref, new_state_any, new_fields_any, sem):
    copies = [
        pltpu.make_async_copy(source, target, sem.at[index])
        for index, (source, target) in enumerate(((ns_ref, new_state_any), (o_ref, new_fields_any)))
    ]
    for item in copies:
        item.start()
    for item in copies:
        item.wait()


def body(tendency, state, stiffness, damping):
    rows = LON * MSG_G
    vmem = pl.BlockSpec(memory_space=pltpu.VMEM)
    anywhere = pl.BlockSpec(memory_space=pl.ANY)
    shapes = (jax.ShapeDtypeStruct((FR, MDEV, WAVES), F32), jax.ShapeDtypeStruct((rows, 128), F32))
    new_state, new_fields = pl.pallas_call(
        kernel,
        out_shape=shapes,
        in_specs=[anywhere] * 9,
        out_specs=(vmem, vmem),
        scratch_shapes=[
            pltpu.VMEM((rows, 128), F32),
            pltpu.VMEM((FR, HALF, WAVES), F32),
            pltpu.VMEM((FR, HALF, 256), F32),
            pltpu.VMEM((FR, HALF, WAVES), F32),
            pltpu.VMEM((FR, HALF, 256), F32),
            pltpu.VMEM((FR, MDEV, 256), F32),
            pltpu.VMEM((64, 128), F32),
            pltpu.SMEM((MODES,), F32),
            pltpu.SMEM((MODES,), F32),
            pltpu.VMEM((64 * LON, 2 * WAVES), BF16),
            pltpu.VMEM((64 * LON, 2 * WAVES), BF16),
            pltpu.VMEM((2 * WAVES, 64 * LON), BF16),
            pltpu.VMEM((2 * WAVES, 64 * LON), BF16),
            pltpu.VMEM((rows, 128), F32),
            pltpu.VMEM((LON * SLOT_G, 128), F32),
            pltpu.VMEM((256, 512), BF16),
            pltpu.VMEM((128, 2 * WAVES), F32),
            pltpu.VMEM((128, 256), F32),
            pltpu.VMEM((32 * MSG_C, 128), F32),
            pltpu.VMEM((32 * MSG_C, 128), F32),
            pltpu.VMEM((FR * PLANE, 128), F32),
            pltpu.VMEM((LINES, 128), F32),
            pltpu.VMEM((LINES, 128), F32),
            pltpu.VMEM((ROWS, 128), F32),
            pltpu.VMEM((LINES // 8 * PLANE, 128), F32),
            pltpu.VMEM((3 * LINES_PAD, 128), F32),
            pltpu.VMEM((3 * LINES_PAD, 128), F32),
            pltpu.VMEM((32 * MSG_C, 128), F32),
            pltpu.VMEM((32 * SLOT_C, 128), F32),
            pltpu.VMEM((256, 2 * WAVES), BF16),
            pltpu.VMEM((rows, 128), F32),
            pltpu.SemaphoreType.DMA((9,)),
            pltpu.SemaphoreType.DMA((6,)),
            pltpu.SemaphoreType.DMA((6, 4)),
            pltpu.SemaphoreType.REGULAR,
        ],
        compiler_params=pltpu.CompilerParams(
            collective_id=0, has_side_effects=True, vmem_limit_bytes=60 * 2**20
        ),
        name="spectral_step",
    )(
        tendency.reshape(rows, 128),
        state.reshape(FR, MDEV, WAVES),
        jnp.asarray(start_constants()),
        stiffness,
        damping,
        *[jnp.asarray(table) for table in fourier_constants()],
    )
    new_state, new_fields = pl.pallas_call(
        result_kernel,
        out_shape=shapes,
        in_specs=[vmem, vmem],
        out_specs=(anywhere, anywhere),
        scratch_shapes=[pltpu.SemaphoreType.DMA((2,))],
        name="results",
    )(new_state, new_fields)
    return new_state.reshape(state.shape), new_fields.reshape(tendency.shape)


def solution(mesh):
    return jax.shard_map(
        body,
        mesh=mesh,
        in_specs=(P(None, None, "lat", "lon", None), P("lat", None, None, "lon", None), P(), P()),
        out_specs=(P("lat", None, None, "lon", None), P(None, None, "lat", "lon", None)),
        check_vma=False,
    )
```

```python
import functools
import math

import jax
import jax.numpy as jnp
import ml_dtypes
import numpy as np
from jax import lax
from jax.experimental import pallas as pl
from jax.experimental.pallas import tpu as pltpu
from jax.sharding import PartitionSpec as P

NLAT = 768
NLON = 1536
WAVES = 512
MODES = 16
LON = 32
LAT = 16
BLK = 48
MDEV = 16
GROUPS = 8
MSG_G = 27
SLOT_G = 48
SLOT_C = 32
MSG_C = 18
FR = 6
HALF = 8
QUADS = 17
LINES = QUADS * 32
LINES_PAD = 768
PLANE = 384
ROWS = 48
MESH = pl.DeviceIdType.MESH
F32 = jnp.float32
BF16 = jnp.bfloat16


def split_constant(table):
    high = table.astype(np.float32).astype(ml_dtypes.bfloat16)
    low = (table - high.astype(np.float64)).astype(np.float32).astype(ml_dtypes.bfloat16)
    return high, low


def lon_of(place):
    return (place % 8) * 4 + place // 8


def place_of(lon):
    return (lon % 4) * 8 + lon // 4


@functools.lru_cache(maxsize=None)
def fourier_constants():
    slot = np.arange(LON * 64)
    block, inner = lon_of(slot // 64), slot % 64
    lon = block * BLK + inner
    valid = (inner < BLK)[:, None]
    wave = np.arange(WAVES)
    angle = 2.0 * np.pi / NLON * ((lon[:, None] * wave[None, :]) % NLON)
    owners = lon_of(np.arange(LON))
    first = np.where(owners < LON // 2, 2 * owners, 63 - 2 * owners)
    sets = np.stack([first, 63 - first], axis=1)
    cosine = np.where(valid, np.cos(angle), 0.0).reshape(-1, 64, HALF)[:, sets]
    sine = np.where(valid, np.sin(angle), 0.0).reshape(-1, 64, HALF)[:, sets]
    basis = np.stack([cosine, -sine], axis=3).reshape(LON * 64, 2 * WAVES)
    factor = np.where(wave == 0, 1.0, 2.0).reshape(64, HALF)[sets] / WAVES
    factor = np.broadcast_to(factor[:, :, None, :], (LON, 2, 2, HALF)).reshape(2 * WAVES, 1)
    return split_constant(basis / NLON) + split_constant(factor * basis.T)


@functools.lru_cache(maxsize=None)
def start_constants():
    start = [
        (0.5 * math.log(m + 0.5) + 0.5 * math.lgamma(m + 0.5) - 0.5 * math.lgamma(m + 1.0) - 0.25 * math.log(math.pi))
        / math.log(2.0)
        for m in range(WAVES)
    ]
    return np.tile(np.array(start, np.float32).reshape(64, HALF), (1, 2 * GROUPS))


def lanes(shape):
    return lax.broadcasted_iota(jnp.int32, shape, len(shape) - 1)


def swap_groups(items):
    group = lanes(items[0].shape) // 16
    items = list(items)
    for step in (4, 2, 1):
        keep = (group & step) == 0
        for low in range(GROUPS):
            if low & step:
                continue
            high = low + step
            x, y = items[low], items[high]
            items[low] = jnp.where(keep, x, pltpu.roll(y, 16 * step, 1))
            items[high] = jnp.where(keep, pltpu.roll(x, 128 - 16 * step, 1), y)
    return items


def fold_rows(parts):
    row = lax.broadcasted_iota(jnp.int32, (8, 128), 0)
    upper = row < 4
    four = []
    for index in range(4):
        x, y = parts[index], parts[index + 4]
        four.append(jnp.where(upper, x, y) + pltpu.roll(jnp.where(upper, y, x), 4, 0))
    keep = (row & 2) == 0
    a, b = [
        jnp.where(
            keep,
            four[index] + pltpu.roll(four[index], 6, 0),
            four[index + 2] + pltpu.roll(four[index + 2], 2, 0),
        )
        for index in range(2)
    ]
    keep = (row & 1) == 0
    after, before = pltpu.roll(a, 7, 0), pltpu.roll(b, 1, 0)
    return jnp.where(keep, a + after, before + b), jnp.where(keep, a - after, before - b)


def split(x):
    high = x.astype(BF16)
    return high, (x - high.astype(F32)).astype(BF16)


def mirrored(south, a):
    return jnp.where(south, GROUPS - 1 - a, a)


def block_rows(index, size):
    return pl.ds(pl.multiple_of(index * size, size), size)


def gather_rows(t_ref, sb_ref):
    def body(d, _):
        c, h = d // 2, d % 2
        for f in range(3):
            sb_ref[pl.ds(d * MSG_G + f * 9, 9), :] = t_ref[pl.ds((f * MODES + c) * 18 + h * 9, 9), :]
        return 0

    lax.fori_loop(0, LON, body, 0)


def set_lines(g):
    return (64 - g + 3) // 4 * 32


def legendre_tables(g, start_ref, slope_ref, lag_ref, trig_ref, p_ref):
    member = lanes((1, 128)) % HALF
    waves = ((member + HALF * g).astype(F32), (member + HALF * (63 - g)).astype(F32))
    split_line = set_lines(g)

    def coefficients(block, _):
        line = lax.broadcasted_iota(jnp.int32, (32, 128), 0) + block * 32
        second = line >= split_line
        offsets = jnp.where(second, line - split_line, line).astype(F32)
        wave = jnp.where(second, waves[1], waves[0])
        degree = wave + offsets
        spacing = jnp.maximum(offsets * (2.0 * wave + offsets), 1.0)
        slope = jnp.sqrt(jnp.maximum(4.0 * degree * degree - 1.0, 0.0) / spacing)
        numerator = (2.0 * degree + 1.0) * (offsets - 1.0) * (degree - 1.0 + wave)
        lag = jnp.sqrt(jnp.maximum(numerator, 0.0) / (jnp.maximum(2.0 * degree - 3.0, 1.0) * spacing))
        first = offsets < 0.5
        slope_ref[block_rows(block, 32), :] = jnp.where(first, 0.0, slope)
        lag_ref[block_rows(block, 32), :] = jnp.where(first, 1.0, lag)
        return 0

    lax.fori_loop(0, QUADS, coefficients, 0)
    row = lax.broadcasted_iota(jnp.int32, (ROWS, 128), 0)
    colat = ((row // 24) * 8 + row % 8) * 24 + (row // 8 % 3) * 8 + lanes((ROWS, 128)) // MDEV
    theta = math.pi * (colat.astype(F32) + 0.5) / NLAT
    mu = jnp.cos(theta)
    sine = jnp.sin(theta)
    trig_ref[...] = sine * (WAVES * math.pi / NLAT)
    log_sine = jnp.log(sine) * (1.0 / math.log(2.0))
    coarse = jnp.floor(log_sine * 1024.0) * (1.0 / 1024.0)
    blocks = split_line // 8

    for which, (begin, end) in enumerate(((0, blocks), (blocks, LINES // 8))):
        wave = waves[which]
        whole = wave * coarse
        exponent = jnp.floor(whole)
        start = start_ref[pl.ds(63 - g if which else g, 1), :]
        lower = -jnp.exp2((whole - exponent) + wave * (log_sine - coarse) + start)

        def body(block, carry, begin=begin, wave=wave):
            upper, lower, exponent = carry
            growth = jnp.exp2(jnp.maximum(exponent, -140.0))
            for offset in range(8):
                line = block * 8 + offset
                moved = (slope_ref[pl.ds(line, 1), :] * mu) * upper - lag_ref[pl.ds(line, 1), :] * lower
                upper, lower = moved, upper
                k = line - begin * 8
                inside = wave + k.astype(F32) <= WAVES - 1.0
                p_ref[pl.ds(block * PLANE + offset, ROWS, stride=8), :] = jnp.where(inside, upper * growth, 0.0)
            big = jnp.maximum(jnp.abs(upper), jnp.abs(lower)) > 2.0**32
            scale = jnp.where(big, 2.0**-32, 1.0)
            return upper * scale, lower * scale, exponent + jnp.where(big, 32.0, 0.0)

        lax.fori_loop(begin, end, body, (jnp.zeros_like(lower), lower, exponent))


def forward_operand(group, r_ref, x_ref):
    lane = lanes((16, 128))

    def body(pair, _):
        first_row = (group * 8 + 2 * pair) * SLOT_G
        columns = [[r_ref[pl.ds(first_row + par * SLOT_G + c, 16, stride=3), :] for c in range(3)] for par in range(2)]
        for a in range(GROUPS):
            first, offset = divmod(BLK * a, 128)
            pieces = []
            for par in range(2):
                source = columns[par][first]
                if offset + BLK > 128:
                    source = jnp.where(lane >= offset, source, columns[par][first + 1])
                shift = (64 * par - offset) % 128
                pieces.append(pltpu.roll(source, shift, 1) if shift else source)
            high, low = split(jnp.where(lane < 64, pieces[0], pieces[1]))
            x_ref[a * 16 : (a + 1) * 16, block_rows(pair, 128)] = high
            x_ref[128 + a * 16 : 128 + (a + 1) * 16, block_rows(pair, 128)] = low
        return 0

    lax.fori_loop(0, 4, body, 0)


def product(x_ref, high_ref, low_ref, rows, columns):
    both = jnp.dot(x_ref[...], high_ref[rows, columns], preferred_element_type=F32)
    rest = jnp.dot(x_ref[0:128, :], low_ref[rows, columns], preferred_element_type=F32)
    return both[0:128] + both[128:256] + rest


def add_products(group, x_ref, high_ref, low_ref, sum_ref):
    rows = block_rows(group, x_ref.shape[1])

    def body(block, _):
        columns = block_rows(block, 256)
        sum_ref[:, columns] += product(x_ref, high_ref, low_ref, rows, columns)
        return 0

    lax.fori_loop(0, sum_ref.shape[1] // 256, body, 0)


def forward_blocks(q, south, group, x_ref, high_ref, low_ref, sum_ref, block_ref, m_ref, send):
    rows = block_rows(group, x_ref.shape[1])

    def body(step, _):
        block = (q + turn(step)) % 4
        columns = block_rows(block, 256)
        block_ref[...] = sum_ref[:, columns] + product(x_ref, high_ref, low_ref, rows, columns)
        for order in range(2):
            half = jnp.where(q // 4 < 4, 1 - order, order)
            items = swap_groups(
                [block_ref[block_rows(mirrored(south, a), 16), block_rows(half, 128)] for a in range(GROUPS)]
            )
            for group in range(GROUPS):
                owner = block * 8 + half * 4 + group // 2
                m_ref[pl.ds(owner * MSG_C + (group % 2) * 9, 9), :] = items[group][0:9]
            for index in range(4):
                send(block * 8 + half * 4 + index)
        return 0

    lax.fori_loop(0, 4, body, 0)


def analysis(g, g_ref, trig_ref, eo_ref, p_ref, a_ref):
    for n in range(2):
        for s in range(3):
            weight = trig_ref[n * 24 + s * 8 : n * 24 + s * 8 + 8, :]
            for which in range(2):
                for f in range(3):
                    line = which * 9 + f * 3
                    north = g_ref[pl.ds(n * 8 * MSG_C + line + s, 8, stride=MSG_C), :]
                    south = g_ref[pl.ds((16 + n * 8) * MSG_C + line + 2 - s, 8, stride=MSG_C), :]
                    first = (which * 3 + f) * PLANE + (n * 24 + s * 8) * 8
                    even, odd = (north + south) * weight, (north - south) * weight
                    for k in range(8):
                        eo_ref[pl.ds(first + k, 8, stride=8), :] = odd if k % 2 else even

    quads = set_lines(g) // 32

    def body(quad, _):
        base = jnp.where(quad >= quads, 3 * PLANE, 0)

        def rows(group, sums):
            sums = list(sums)
            for row in range(16):
                first = (group * 16 + row) * 8
                fields = [eo_ref[pl.ds(pl.multiple_of(base + f * PLANE + first, 8), 8), :] for f in range(3)]
                for b in range(4):
                    plane = p_ref[pl.ds(pl.multiple_of((quad * 4 + b) * PLANE + first, 8), 8), :]
                    for f in range(3):
                        sums[b * 3 + f] = sums[b * 3 + f] + plane * fields[f]
            return tuple(sums)

        sums = lax.fori_loop(0, ROWS // 16, rows, (jnp.zeros((8, 128), F32),) * 12)
        for b in range(4):
            for f in range(3):
                a_ref[pl.ds(pl.multiple_of(f * LINES_PAD + (quad * 4 + b) * 8, 8), 8), :] = sums[b * 3 + f]
        return 0

    lax.fori_loop(0, QUADS, body, 0)


def update(g, stiff, damp, state_refs, a_ref, ns_refs, st_ref):
    for which in range(2):
        state_ref, ns_ref = state_refs[which], ns_refs[which]
        size = ns_ref.shape[2]
        start = pl.multiple_of(set_lines(g) if which else 0 * g, 32)
        member = lax.broadcasted_iota(jnp.int32, (MDEV, size), 0) % HALF
        wave = (member + HALF * (63 - g if which else g)).astype(F32)
        degree = wave + lanes((MDEV, size)).astype(F32)
        ratio = degree * (degree + 1.0) / (WAVES * (WAVES - 1.0))
        inside = degree <= WAVES - 1.0
        denominator = 1.0 + stiff * ratio
        damped = jnp.where(inside, 1.0 / (1.0 + damp * ratio * ratio), 0.0)

        def total(f):
            turned = jnp.transpose(a_ref[pl.ds(f * LINES_PAD + start, size), :])
            pieces = [turned[16 * n : 16 * n + 16] for n in range(GROUPS)]
            summed = ((pieces[0] + pieces[1]) + (pieces[2] + pieces[3])) + (
                (pieces[4] + pieces[5]) + (pieces[6] + pieces[7])
            )
            old = jnp.concatenate([state_ref[f * 2], state_ref[f * 2 + 1]], axis=0)
            return jnp.where(inside, old + summed, 0.0)

        def put(f, value):
            ns_ref[f * 2] = value[0:8]
            ns_ref[f * 2 + 1] = value[8:16]
            turned = jnp.transpose(jnp.concatenate([value] * GROUPS, axis=0))
            st_ref[pl.ds(f * LINES_PAD + start, size), :] = turned

        vorticity, divergence, height = total(0), total(1), total(2)
        put(0, vorticity * damped)
        put(1, (divergence + ratio * height) / denominator * damped)
        put(2, (height - stiff * divergence) / denominator * damped)


def synthesis(g, group, p_ref, st_ref, h_ref):
    quads = set_lines(g) // 32
    n, s = group // 3, group % 3

    def degrees(quad, sums):
        sums = list(sums)
        for b in range(4):
            block = quad * 4 + b
            values = [st_ref[pl.ds(pl.multiple_of(f * LINES_PAD + block * 8, 8), 8), :] for f in range(3)]
            for row in range(8):
                first = block * PLANE + group * 64 + row * 8
                plane = p_ref[pl.ds(pl.multiple_of(first, 8), 8), :]
                for f in range(3):
                    sums[f * 8 + row] = sums[f * 8 + row] + plane * values[f]
        return tuple(sums)

    zeros = (jnp.zeros((8, 128), F32),) * 24
    sets = [lax.fori_loop(0, quads, degrees, zeros), lax.fori_loop(quads, QUADS, degrees, zeros)]
    for which in range(2):
        for f in range(3):
            north, south = fold_rows(sets[which][f * 8 : f * 8 + 8])
            line = which * 9 + f * 3
            h_ref[pl.ds(n * 8 * MSG_C + line + s, 8, stride=MSG_C), :] = north
            h_ref[pl.ds((16 + n * 8) * MSG_C + line + 2 - s, 8, stride=MSG_C), :] = south


def inverse_operand(group, south, cp_ref, y_ref):
    for column in range(2):
        first = (group * 8 + column * 4) * SLOT_C
        items = swap_groups([cp_ref[pl.ds(first + g // 2 * SLOT_C + g % 2 * 9, 16), :] for g in range(GROUPS)])
        for a in range(GROUPS):
            row = mirrored(south, a)
            high, low = split(items[a])
            y_ref[block_rows(row, 16), block_rows(group * 2 + column, 128)] = high
            y_ref[block_rows(row + GROUPS, 16), block_rows(group * 2 + column, 128)] = low


def inverse_blocks(q, y_ref, high_ref, low_ref, block_ref, w_ref, send):
    lane = lanes((16, 128))

    def body(step, _):
        block = (q + turn(step // 2)) % 4 * 2 + jnp.where(q // 4 < 4, 1 - step % 2, step % 2)
        columns = block_rows(block, 256)
        block_ref[...] = product(y_ref, high_ref, low_ref, slice(None), columns)
        for index in range(4):
            half, par = divmod(index, 2)
            owner = block * 4 + index
            columns = [None] * 3
            for a in range(GROUPS):
                first, offset = divmod(BLK * a, 128)
                piece = block_ref[a * 16 : (a + 1) * 16, half * 128 : (half + 1) * 128]
                shift = (offset - 64 * par) % 128
                piece = pltpu.roll(piece, shift, 1) if shift else piece
                if columns[first] is None:
                    columns[first] = piece
                else:
                    columns[first] = jnp.where(lane >= offset, piece, columns[first])
                if offset + BLK > 128:
                    columns[first + 1] = piece
            for c in range(3):
                w_ref[pl.ds(owner * MSG_G + c, 9, stride=3), :] = columns[c][0:9]
            send(owner)
        return 0

    lax.fori_loop(0, 8, body, 0)


def far_first(y, n):
    return (y + jnp.where(n % 2 == 0, 4 - n // 2, 4 + (n + 1) // 2)) % 8


def turn(step):
    return jnp.where(step == 0, 2, jnp.where(step == 1, 1, jnp.where(step == 2, 3, 0)))


def slot_of(source):
    return jnp.where(source < 16, source, 47 - source)


def kernel(
    t_any,
    state_any,
    start_any,
    stiff_any,
    damp_any,
    fh_any,
    fl_any,
    ih_any,
    il_any,
    ns_ref,
    o_ref,
    t_ref,
    low_state_ref,
    high_state_ref,
    low_new_ref,
    high_new_ref,
    zero_ref,
    start_ref,
    stiff_ref,
    damp_ref,
    fh_ref,
    fl_ref,
    ih_ref,
    il_ref,
    sb_ref,
    r_ref,
    x_ref,
    fsum_ref,
    block_ref,
    m_ref,
    g_ref,
    eo_ref,
    slope_ref,
    lag_ref,
    trig_ref,
    p_ref,
    a_ref,
    st_ref,
    h_ref,
    cp_ref,
    y_ref,
    w_ref,
    load_sem,
    send_sem,
    recv_sem,
    ready_sem,
):
    q = lax.axis_index("lon")
    p = lax.axis_index("lat")
    here = place_of(q)
    south = p >= LAT // 2
    low_set = jnp.where(q < LON // 2, 2 * q, 63 - 2 * q)
    owned, half = q // 2, q % 2
    my_source = slot_of(p * 2 + half)
    back_mode = (q // 4 + 16 - p // 2 - p % 2 * 4) % 8 * 2 + q % 4 // 2
    back_half = q % 2
    back_slot = slot_of(p * 2 + back_half)

    zero_copy = pltpu.make_async_copy(zero_ref, ns_ref.at[:, :, 256:512], load_sem.at[8])

    @pl.when(q >= LON // 2)
    def _():
        zero_ref[...] = jnp.zeros_like(zero_ref)
        zero_copy.start()

    barrier = pltpu.get_barrier_semaphore()

    def greet_lon(n, _):
        pl.semaphore_signal(barrier, inc=1, device_id=((q + n) % LON, p), device_id_type=MESH)
        return 0

    def greet_lat(n, _):
        pl.semaphore_signal(barrier, inc=1, device_id=(q, (p + n) % LAT), device_id_type=MESH)
        return 0

    lax.fori_loop(1, LON, greet_lon, 0)
    lax.fori_loop(1, LAT, greet_lat, 0)

    loads = [
        pltpu.make_async_copy(source, target, load_sem.at[index])
        for index, (source, target) in enumerate(
            (
                (t_any, t_ref),
                (start_any, start_ref),
                (fh_any, fh_ref),
                (fl_any, fl_ref),
                (stiff_any, stiff_ref),
                (damp_any, damp_ref),
                (ih_any, ih_ref),
                (il_any, il_ref),
            )
        )
    ]
    for load in loads:
        load.start()

    def copy(source, target, stage, group, peer):
        return pltpu.make_async_remote_copy(
            src_ref=source,
            dst_ref=target,
            send_sem=send_sem.at[stage],
            recv_sem=recv_sem.at[stage, group],
            device_id=peer,
            device_id_type=MESH,
        )

    def copy_or_keep(source, target, stage, group, peer):
        lon, lat = peer
        own = jnp.logical_and(lon == q, lat == p)

        @pl.when(jnp.logical_not(own))
        def _():
            copy(source, target, stage, group, peer).start()

        @pl.when(own)
        def _():
            pltpu.make_async_copy(source, target, recv_sem.at[stage, group]).start()

    def wait(ref, first, rows, sem):
        part = ref.at[pl.ds(first, rows)]
        pltpu.make_async_copy(part, part, sem).wait()

    def send_grid(n, _):
        place = (here // 8 + turn(n // 8)) % 4 * 8 + far_first(here % 8, n % 8)
        lon = lon_of(place)
        copy(sb_ref.at[pl.ds(lon * MSG_G, MSG_G)], r_ref.at[pl.ds(here * SLOT_G, MSG_G)], 0, here // 8, (lon, p)).start()
        return 0

    def send_waves(place):
        copy_or_keep(
            m_ref.at[pl.ds(place * MSG_C, MSG_C)],
            g_ref.at[pl.ds(my_source * MSG_C, MSG_C)],
            1,
            0,
            (lon_of(place), owned),
        )

    def send_rows(n, part):
        index = (here // 8 * 4 + n) % 16
        slot = index // 8 * 16 + part * 8 + index % 8
        source = slot_of(slot)
        lat = source // 2
        lon = (p // 2 + lat // 2 + lat % 2 * 4) % 8 * 4 + p % 2 * 2 + source % 2
        copy_or_keep(
            h_ref.at[pl.ds(slot * MSG_C, MSG_C)],
            cp_ref.at[pl.ds(here * SLOT_C, MSG_C)],
            2,
            here // 8,
            (lon, lat),
        )
        return part

    def send_back(place):
        for f in range(3):
            copy_or_keep(
                w_ref.at[pl.ds(place * MSG_G + f * 9, 9)],
                o_ref.at[pl.ds((f * MODES + back_mode) * 18 + back_half * 9, 9)],
                3,
                0,
                (lon_of(place), p),
            )

    partner = (LON - 1 - q, p)
    keeps_low = q < LON // 2
    mine, other = pl.ds(0, HALF), pl.ds(HALF, HALF)

    def state_copies(low):
        if low:
            keep = pltpu.make_async_copy(state_any.at[:, mine, :], low_state_ref, recv_sem.at[4, 0])
            return keep, copy(state_any.at[:, other, :], low_state_ref, 4, 0, partner)
        keep = pltpu.make_async_copy(state_any.at[:, mine, 0:256], high_state_ref, recv_sem.at[4, 1])
        return keep, copy(state_any.at[:, other, 0:256], high_state_ref, 4, 1, partner)

    def new_copies(low):
        if low:
            keep = pltpu.make_async_copy(low_new_ref, ns_ref.at[:, mine, :], recv_sem.at[5, 1])
            return keep, copy(high_new_ref, ns_ref.at[:, other, 0:256], 5, 0, partner)
        keep = pltpu.make_async_copy(high_new_ref, ns_ref.at[:, mine, 0:256], recv_sem.at[5, 1])
        return keep, copy(low_new_ref, ns_ref.at[:, other, :], 5, 0, partner)

    def either(act):
        @pl.when(keeps_low)
        def _():
            act(True)

        @pl.when(jnp.logical_not(keeps_low))
        def _():
            act(False)

    def send_state(low):
        keep, go = state_copies(low)
        keep.start()
        go.start()

    def send_new(low):
        keep, go = new_copies(low)
        keep.start()
        go.start()

    def sent_state(low):
        state_copies(low)[1].wait_send()

    def finish_new(low):
        keep, go = new_copies(low)
        keep.wait()
        go.wait_send()
        if not low:
            zero_copy.wait()
        part = ns_ref.at[:, other, :] if low else ns_ref.at[:, other, 0:256]
        pltpu.make_async_copy(part, part, recv_sem.at[5, 0]).wait()

    loads[0].wait()
    gather_rows(t_ref, sb_ref)
    pl.semaphore_wait(barrier, LON - 1 + LAT - 1)
    lax.fori_loop(0, LON - 1, send_grid, 0)
    pltpu.make_async_copy(
        sb_ref.at[pl.ds(q * MSG_G, MSG_G)], r_ref.at[pl.ds(here * SLOT_G, MSG_G)], recv_sem.at[0, here // 8]
    ).start()

    def tell(n, _):
        pl.semaphore_signal(ready_sem, inc=1, device_id=(q, (p + n) % LAT), device_id_type=MESH)
        return 0

    lax.fori_loop(1, LAT, tell, 0)

    loads[1].wait()
    legendre_tables(low_set, start_ref, slope_ref, lag_ref, trig_ref, p_ref)
    fsum_ref[...] = jnp.zeros_like(fsum_ref)
    loads[2].wait()
    loads[3].wait()

    def grid_group(step):
        group = (here // 8 + 4 - turn(step)) % 4
        wait(r_ref, group * 8 * SLOT_G, 8 * MSG_G, recv_sem.at[0, group])
        forward_operand(group, r_ref, x_ref)
        return group

    def forward_step(step, _):
        add_products(grid_group(step), x_ref, fh_ref, fl_ref, fsum_ref)
        return 0

    lax.fori_loop(0, 3, forward_step, 0)
    group = grid_group(3)
    pl.semaphore_wait(ready_sem, LAT - 1)
    forward_blocks(q, south, group, x_ref, fh_ref, fl_ref, fsum_ref, block_ref, m_ref, send_waves)
    either(send_state)
    for load in loads[4:]:
        load.wait()
    wait(sb_ref, 0, (LON - 1) * MSG_G, send_sem.at[0])
    wait(g_ref, 0, 32 * MSG_C, recv_sem.at[1, 0])
    analysis(low_set, g_ref, trig_ref, eo_ref, p_ref, a_ref)
    either(sent_state)
    pltpu.make_async_copy(low_state_ref, low_state_ref, recv_sem.at[4, 0]).wait()
    pltpu.make_async_copy(high_state_ref, high_state_ref, recv_sem.at[4, 1]).wait()
    update(
        low_set,
        stiff_ref[p],
        damp_ref[p],
        (low_state_ref, high_state_ref),
        a_ref,
        (low_new_ref, high_new_ref),
        st_ref,
    )

    def synthesize(part, _):
        lax.fori_loop(0, 3, lambda s, _: (synthesis(low_set, part * 3 + s, p_ref, st_ref, h_ref), 0)[1], 0)
        lax.fori_loop(0, 16, send_rows, part)
        return 0

    lax.fori_loop(0, 2, synthesize, 0)
    either(send_new)

    def wait_sent(ref, own, stage):
        @pl.when(own)
        def _():
            wait(ref, 0, 31 * MSG_C, send_sem.at[stage])

        @pl.when(jnp.logical_not(own))
        def _():
            wait(ref, 0, 32 * MSG_C, send_sem.at[stage])

    wait_sent(m_ref, owned == p, 1)

    def waves_group(step, _):
        group = (back_slot // 8 + 4 - step) % 4
        wait(cp_ref, group * 8 * SLOT_C, 8 * MSG_C, recv_sem.at[2, group])
        inverse_operand(group, south, cp_ref, y_ref)
        return 0

    lax.fori_loop(0, 4, waves_group, 0)
    inverse_blocks(q, y_ref, ih_ref, il_ref, block_ref, w_ref, send_back)
    wait_sent(h_ref, back_mode == p, 2)
    either(finish_new)
    wait(o_ref, 0, LON * MSG_G, recv_sem.at[3, 0])
    wait(w_ref, 0, (LON - 1) * MSG_G, send_sem.at[3])


def result_kernel(ns_any, o_any, new_state_any, new_fields_any, ns_ref, o_ref, in_sem, out_sem):
    moves = []
    for n in range(3):
        part, rows = pl.ds(n * 2, 2), pl.ds(n * 288, 288)
        moves.append((ns_any.at[part], ns_ref.at[part], new_state_any.at[part]))
        moves.append((o_any.at[rows], o_ref.at[rows], new_fields_any.at[rows]))
    loads = [pltpu.make_async_copy(a, b, in_sem.at[n]) for n, (a, b, _) in enumerate(moves)]
    stores = [pltpu.make_async_copy(b, c, out_sem.at[n]) for n, (_, b, c) in enumerate(moves)]
    for load in loads:
        load.start()
    for load, store in zip(loads, stores):
        load.wait()
        store.start()
    for store in stores:
        store.wait()


def body(tendency, state, stiffness, damping):
    rows = LON * MSG_G
    vmem = pl.BlockSpec(memory_space=pltpu.VMEM)
    anywhere = pl.BlockSpec(memory_space=pl.ANY)
    shapes = (jax.ShapeDtypeStruct((FR, MDEV, WAVES), F32), jax.ShapeDtypeStruct((rows, 128), F32))
    new_state, new_fields = pl.pallas_call(
        kernel,
        out_shape=shapes,
        in_specs=[anywhere] * 9,
        out_specs=(vmem, vmem),
        scratch_shapes=[
            pltpu.VMEM((rows, 128), F32),
            pltpu.VMEM((FR, HALF, WAVES), F32),
            pltpu.VMEM((FR, HALF, 256), F32),
            pltpu.VMEM((FR, HALF, WAVES), F32),
            pltpu.VMEM((FR, HALF, 256), F32),
            pltpu.VMEM((FR, MDEV, 256), F32),
            pltpu.VMEM((64, 128), F32),
            pltpu.SMEM((MODES,), F32),
            pltpu.SMEM((MODES,), F32),
            pltpu.VMEM((64 * LON, 2 * WAVES), BF16),
            pltpu.VMEM((64 * LON, 2 * WAVES), BF16),
            pltpu.VMEM((2 * WAVES, 64 * LON), BF16),
            pltpu.VMEM((2 * WAVES, 64 * LON), BF16),
            pltpu.VMEM((rows, 128), F32),
            pltpu.VMEM((LON * SLOT_G, 128), F32),
            pltpu.VMEM((256, 512), BF16),
            pltpu.VMEM((128, 2 * WAVES), F32),
            pltpu.VMEM((128, 256), F32),
            pltpu.VMEM((32 * MSG_C, 128), F32),
            pltpu.VMEM((32 * MSG_C, 128), F32),
            pltpu.VMEM((FR * PLANE, 128), F32),
            pltpu.VMEM((LINES, 128), F32),
            pltpu.VMEM((LINES, 128), F32),
            pltpu.VMEM((ROWS, 128), F32),
            pltpu.VMEM((LINES // 8 * PLANE, 128), F32),
            pltpu.VMEM((3 * LINES_PAD, 128), F32),
            pltpu.VMEM((3 * LINES_PAD, 128), F32),
            pltpu.VMEM((32 * MSG_C, 128), F32),
            pltpu.VMEM((32 * SLOT_C, 128), F32),
            pltpu.VMEM((256, 2 * WAVES), BF16),
            pltpu.VMEM((rows, 128), F32),
            pltpu.SemaphoreType.DMA((9,)),
            pltpu.SemaphoreType.DMA((6,)),
            pltpu.SemaphoreType.DMA((6, 4)),
            pltpu.SemaphoreType.REGULAR,
        ],
        compiler_params=pltpu.CompilerParams(
            collective_id=0, has_side_effects=True, vmem_limit_bytes=60 * 2**20
        ),
        name="spectral_step",
    )(
        tendency.reshape(rows, 128),
        state.reshape(FR, MDEV, WAVES),
        jnp.asarray(start_constants()),
        stiffness,
        damping,
        *[jnp.asarray(table) for table in fourier_constants()],
    )
    new_state, new_fields = pl.pallas_call(
        result_kernel,
        out_shape=shapes,
        in_specs=[anywhere, anywhere],
        out_specs=(anywhere, anywhere),
        scratch_shapes=[
            pltpu.VMEM((FR, MDEV, WAVES), F32),
            pltpu.VMEM((rows, 128), F32),
            pltpu.SemaphoreType.DMA((6,)),
            pltpu.SemaphoreType.DMA((6,)),
        ],
        compiler_params=pltpu.CompilerParams(vmem_limit_bytes=60 * 2**20),
        name="results",
    )(new_state, new_fields)
    return new_state.reshape(state.shape), new_fields.reshape(tendency.shape)


def solution(mesh):
    return jax.shard_map(
        body,
        mesh=mesh,
        in_specs=(P(None, None, "lat", "lon", None), P("lat", None, None, "lon", None), P(), P()),
        out_specs=(P("lat", None, None, "lon", None), P(None, None, "lat", "lon", None)),
        check_vma=False,
    )
```
